32 devices in a mesh: dp: 4 (over y, core), seq: 8 (over z, x).
Axes of the slice: x: 2, y: 2, z: 4, core: 2. Of those that a mesh axis runs over, the one named last changes fastest.
Arguments:
- activations: float32 [4, 1024, 1024], P('dp', 'seq'), may hold values from -6 to 6
- cotangent: bfloat16 [4, 1024, 1024], P('dp', 'seq'), may hold values from -6 to 6
- block_sizes: int32 [4], P('dp'), may hold values from 256 to 512, as said below
- context_back: int32 [128], replicated, may hold values from 1 to 512, as said below
- first_gain: bfloat16 [1024], P('seq'), may hold values from 0.5 to 1.5
- first_bias: bfloat16 [1024], P('seq'), may hold values from -3 to 3
- w_query: bfloat16 [1024, 1024], P('seq'), may hold values from -0.1875 to 0.1875
- w_key: bfloat16 [1024, 1024], P('seq'), may hold values from -0.1875 to 0.1875
- w_value: bfloat16 [1024, 1024], P('seq'), may hold values from -0.1875 to 0.1875
- w_out: bfloat16 [1024, 1024], P('seq'), may hold values from -1 to 1
- second_gain: bfloat16 [1024], P('seq'), may hold values from 0.5 to 1.5
- second_bias: bfloat16 [1024], P('seq'), may hold values from -3 to 3
- w_up: bfloat16 [1024, 4096], P('seq'), may hold values from -0.1875 to 0.1875
- w_down: bfloat16 [4096, 1024], P('seq'), may hold values from -0.09375 to 0.09375
- decay_rate: float32 [1024, 16], P('seq'), may hold values from 0.5 to 2
- input_map: float32 [1024, 16], P('seq'), may hold values from 0.5 to 1.5
- output_map: float32 [1024, 16], P('seq'), may hold values from -12 to 12
- step_size: float32 [1024], P('seq'), may hold values from 0.0009765625 to 0.1
- skip_gain: float32 [1024], P('seq'), may hold values from 0.5 to 1.5
Outputs:
- result: float32 [4, 1024, 1024], P('dp', 'seq')
- grad_inputs: float32 [4, 1024, 1024], P('dp', 'seq')
- grad_first_gain: float32 [1024], P('seq')
- grad_first_bias: float32 [1024], P('seq')
- grad_w_query: float32 [1024, 1024], P('seq')
- grad_w_key: float32 [1024, 1024], P('seq')
- grad_w_value: float32 [1024, 1024], P('seq')
- grad_w_out: float32 [1024, 1024], P('seq')
- grad_second_gain: float32 [1024], P('seq')
- grad_second_bias: float32 [1024], P('seq')
- grad_w_up: float32 [1024, 4096], P('seq')
- grad_w_down: float32 [4096, 1024], P('seq')
- grad_decay_rate: float32 [1024, 16], P('seq')
- grad_input_map: float32 [1024, 16], P('seq')
- grad_output_map: float32 [1024, 16], P('seq')
- grad_step_size: float32 [1024], P('seq')
- grad_skip_gain: float32 [1024], P('seq')
The draws below stay inside these ranges and needn't reach their ends.
Inputs may be any that keep to these rules, and one draw needn't show every extreme that they name: `block_sizes`: each entry is 256 or 512, and both occur in every draw. `context_back`: strictly increasing; entry j lies between j * 4 + 1 and (j + 1) * 4.
All inputs are finite; a program needn't handle non-finite values.
Results may differ from the reference program's by a relative error of at most 0.019.
Values may be sent and summed in bfloat16 or wider, within the bound.
No kernel may reach another device: no remote copies, remote signals or barrier semaphores. Data moves between devices by JAX's collectives and lax.ppermute only.
A program may use at most 192 MiB of HBM per device.

```python
import math
from functools import partial
import jax
import jax.numpy as jnp
from jax import lax

D = 1024
HEADS = 8
HEAD_DIM = 128
STATE = 16
FF = 4096
CTX = 128
BLK_A = 256
BLK_B = 512
STRIDE = 4
SEQLEN = 1024
SEQS = 4


def draw_block_sizes(key, part):
    key = jax.random.fold_in(key, 11)
    first_key, second_key = jax.random.split(key)
    chosen = jax.random.randint(first_key, (SEQS,), 0, 2)
    pick_one = jax.random.randint(second_key, (), 0, 2)
    chosen = chosen.at[0].set(pick_one).at[1].set(1 - pick_one)
    return jnp.where(chosen == 1, BLK_B, BLK_A).astype(jnp.int32)


def draw_context_back(key, part):
    key = jax.random.fold_in(key, 23)
    extra = jax.random.randint(key, (CTX,), 0, STRIDE)
    extra = extra.at[0].set(0).at[CTX - 1].set(STRIDE - 1)
    return (jnp.arange(CTX, dtype=jnp.int32) * STRIDE + 1 + extra).astype(jnp.int32)


def steps_of(key, extent, cuts, smallest, top_value):
    level, own = 1.0, jax.random.fold_in(key, 6)
    for position, shards_of in cuts:
        steps = jnp.exp(jax.random.uniform(jax.random.fold_in(own, position), (shards_of,), jnp.float32, smallest / len(cuts), top_value / len(cuts)))
        level = level * jnp.repeat(steps, extent[position] // shards_of).reshape([-1 if axis == position else 1 for axis in range(len(extent))])
    return level


def scatter_about(stream_key, extent, deviation, limit, shards=(), kind=jnp.bfloat16):
    level = steps_of(stream_key, extent, shards, -0.22, 0.18) if shards else 1.0
    values = jax.random.normal(stream_key, extent, jnp.float32) * deviation * level
    return jnp.minimum(jnp.maximum(values, -limit), limit).astype(kind)


def setup_inputs(seed: int = 0) -> dict:
    key_of = jax.random.split(jax.random.key(seed), 20)
    return {
        "activations": scatter_about(key_of[0], (SEQS, SEQLEN, D), 1.0, 6.0, ((0, 4), (1, 8)), jnp.float32),
        "cotangent": scatter_about(key_of[1], (SEQS, SEQLEN, D), 1.0, 6.0, ((0, 4), (1, 8))),
        "block_sizes": draw_block_sizes(jax.random.fold_in(key_of[19], 71), 0),
        "context_back": draw_context_back(jax.random.fold_in(key_of[19], 71), 0),
        "first_gain": jnp.clip(1.0 + 0.1 * jax.random.normal(key_of[4], (D,), jnp.float32), 0.5, 1.5).astype(jnp.bfloat16),
        "first_bias": scatter_about(key_of[5], (D,), 0.5, 3.0, ((0, 8),)),
        "w_query": scatter_about(key_of[6], (D, D), D ** -0.5, 0.1875, ((0, 8),)),
        "w_key": scatter_about(key_of[7], (D, D), D ** -0.5, 0.1875, ((0, 8),)),
        "w_value": scatter_about(key_of[8], (D, D), D ** -0.5, 0.1875, ((0, 8),)),
        "w_out": scatter_about(key_of[9], (D, D), (D // 32) ** -0.5, 1.0, ((0, 8),)),
        "second_gain": jnp.clip(1.0 + 0.1 * jax.random.normal(key_of[10], (D,), jnp.float32), 0.5, 1.5).astype(jnp.bfloat16),
        "second_bias": scatter_about(key_of[11], (D,), 0.5, 3.0, ((0, 8),)),
        "w_up": scatter_about(key_of[12], (D, FF), D ** -0.5, 0.1875, ((0, 8),)),
        "w_down": scatter_about(key_of[13], (FF, D), FF ** -0.5, 0.09375, ((0, 8),)),
        "decay_rate": jnp.clip(jnp.exp(math.log(2.0) - 1.3862944 * jax.random.uniform(key_of[14], (D, STATE), jnp.float32) ** steps_of(key_of[14], (D, STATE), ((0, 8),), -0.2, 0.2)), 0.5, 2.0),
        "input_map": jnp.clip(0.5 + 1.0 * jax.random.uniform(key_of[15], (D, STATE), jnp.float32) ** steps_of(key_of[15], (D, STATE), ((0, 8),), -0.2, 0.2), 0.5, 1.5),
        "output_map": scatter_about(key_of[16], (D, STATE), 2.0, 12.0, ((0, 8),), jnp.float32),
        "step_size": jnp.clip(jnp.exp(math.log(0.1) - 4.6288867 * jax.random.uniform(key_of[17], (D,), jnp.float32) ** steps_of(key_of[17], (D,), ((0, 8),), -0.2, 0.2)), 0.0009765625, 0.1),
        "skip_gain": jnp.clip(0.5 + 1.0 * jax.random.uniform(key_of[18], (D,), jnp.float32) ** steps_of(key_of[18], (D,), ((0, 8),), -0.2, 0.2), 0.5, 1.5),
    }


@jax.custom_vjp
def low(v):
    return lax.optimization_barrier(v.astype(jnp.bfloat16)).astype(jnp.float32)

@jax.custom_vjp
def low_back(v):
    return v

def low_keep(v):
    return (low(v), None)

def low_pass(kept, grad):
    return (grad,)

def back_keep(v):
    return (v, None)

def back_low(kept, grad):
    return (low(grad),)
low.defvjp(low_keep, low_pass)
low_back.defvjp(back_keep, back_low)

def product(left_side, right_side):
    return jnp.dot(left_side, right_side, precision=lax.Precision.HIGHEST, preferred_element_type=jnp.float32)

def both_ways(values):
    return low(low_back(values))

def smooth_gate(values):
    return jax.nn.gelu(values, approximate=True)

def normed(values, gain_vector, bias_vector):
    center = values - lax.optimization_barrier(jnp.mean(values, axis=-1, keepdims=True))
    scaled = center * lax.rsqrt(lax.optimization_barrier(jnp.mean(center * center, axis=-1, keepdims=True)) + 1e-05)
    return scaled * gain_vector + bias_vector

def ssm_kernel(decay_rate, input_map, output_map, step_size, length):
    offsets = jnp.arange(length).astype(jnp.float32)
    weight = output_map * input_map * step_size[:, None]
    decay_speed = step_size[:, None] * decay_rate
    total_sum = jnp.zeros((decay_rate.shape[0], length), jnp.float32)
    for state_index in range(decay_rate.shape[1]):
        total_sum = total_sum + weight[:, state_index:state_index + 1] * jnp.exp(-decay_speed[:, state_index:state_index + 1] * offsets[None, :])
    return total_sum

def attend_block(block_width, span_items):
    queries, keys, values, ctx_keys, ctx_values, ctx_valid, block_index = span_items
    row_ids = jnp.arange(BLK_B, dtype=jnp.int32)
    query_pos = block_index * BLK_B + row_ids
    same_block = query_pos[None, :] // block_width == query_pos[:, None] // block_width
    causal = row_ids[None, :] <= row_ids[:, None]
    ctx_group = jnp.arange(ctx_keys.shape[0], dtype=jnp.int32) // CTX
    ctx_allowed = ((row_ids // BLK_A)[:, None] == ctx_group[None, :]) & ctx_valid[None, :]
    allowed = jnp.concatenate([ctx_allowed, same_block & causal], axis=1)
    all_keys = jnp.concatenate([ctx_keys, keys], axis=0)
    all_values = jnp.concatenate([ctx_values, values], axis=0)
    scores = jnp.einsum('qhd,khd->hqk', queries, all_keys, precision=lax.Precision.HIGHEST) * HEAD_DIM ** (-0.5)
    scores = low_back(scores)
    scores = jnp.where(allowed[None], scores, -1e+30)
    row_top = lax.optimization_barrier(jnp.max(scores, axis=-1, keepdims=True))
    weights = jnp.exp(scores - row_top)
    probabilities = weights / lax.optimization_barrier(jnp.sum(weights, axis=-1, keepdims=True))
    return jnp.einsum('hqk,khd->qhd', low(probabilities), all_values, precision=lax.Precision.HIGHEST)

def layer(inputs, params, block_width, context_back):
    first_gain, first_bias, w_query, w_key, w_value, w_out, second_gain, second_bias, w_up, w_down, decay_rate, input_map, output_map, step_size, skip_gain = params
    lowered = low(normed(inputs, first_gain, first_bias))
    kernel = ssm_kernel(decay_rate, input_map, output_map, step_size, SEQLEN)
    total_len = 2 * SEQLEN
    spectra = jnp.fft.rfft(lowered.T, n=total_len, axis=-1) * jnp.fft.rfft(kernel, n=total_len, axis=-1)
    states = jnp.fft.irfft(spectra, n=total_len, axis=-1)[:, :SEQLEN] + skip_gain[:, None] * lowered.T
    starts = jnp.arange(SEQLEN // BLK_A, dtype=jnp.int32) * BLK_A
    block_start = starts // block_width * block_width
    positions = block_start[:, None] - context_back[None, :]
    ctx_valid = positions >= 0
    picked = jnp.take(states.T, jnp.maximum(positions, 0), axis=0)
    context = low(jnp.where(ctx_valid[..., None], picked, 0.0)).reshape(-1, D)
    queries = both_ways(product(lowered, w_query))
    keys = both_ways(product(lowered, w_key))
    values = both_ways(product(lowered, w_value))
    ctx_keys = low(product(context, w_key))
    ctx_values = low(product(context, w_value))
    span_count = SEQLEN // BLK_B
    per_span = BLK_B // BLK_A * CTX
    attended = lax.map(jax.checkpoint(partial(attend_block, block_width)), (queries.reshape(span_count, BLK_B, HEADS, HEAD_DIM), keys.reshape(span_count, BLK_B, HEADS, HEAD_DIM), values.reshape(span_count, BLK_B, HEADS, HEAD_DIM), ctx_keys.reshape(span_count, per_span, HEADS, HEAD_DIM), ctx_values.reshape(span_count, per_span, HEADS, HEAD_DIM), ctx_valid.reshape(span_count, per_span), jnp.arange(span_count, dtype=jnp.int32)))
    mixed_out = both_ways(attended.reshape(SEQLEN, D))
    first_sum = inputs + low_back(product(mixed_out, w_out))
    normal_two = low(normed(first_sum, second_gain, second_bias))
    pre_gate = low_back(product(normal_two, w_up))
    return first_sum + product(low(smooth_gate(pre_gate)), w_down)

def reference(activations, cotangent, block_sizes, context_back, first_gain, first_bias, w_query, w_key, w_value, w_out, second_gain, second_bias, w_up, w_down, decay_rate, input_map, output_map, step_size, skip_gain):
    params = tuple((item.astype(jnp.float32) for item in (first_gain, first_bias, w_query, w_key, w_value, w_out, second_gain, second_bias, w_up, w_down, decay_rate, input_map, output_map, step_size, skip_gain)))

    def one_sequence(totals, seq_items):
        seq_inputs, seq_cotangent, block_width = seq_items

        def forward(values, weights):
            return layer(values, weights, block_width, context_back)
        outcome, pull_back = jax.vjp(forward, seq_inputs, params)
        grad_values, grad_weights = pull_back(seq_cotangent.astype(jnp.float32))
        totals = jax.tree.map(lambda a, b: a + b, totals, grad_weights)
        return (totals, (outcome, grad_values))
    zero_grads = jax.tree.map(jnp.zeros_like, params)
    totals, (outcome, grad_values) = lax.scan(one_sequence, zero_grads, (activations, cotangent, block_sizes))
    return (outcome, grad_values, totals[0], totals[1], totals[2], totals[3], totals[4], totals[5], totals[6], totals[7], totals[8], totals[9], totals[10], totals[11], totals[12], totals[13], totals[14])
```

```python
import functools
import math

import jax
import jax.numpy as jnp
from jax import lax
from jax.experimental import pallas as pl
from jax.experimental.pallas import tpu as pltpu
from jax.sharding import Mesh
from jax.sharding import PartitionSpec as P

HEADS = 8
CTX = 128
BLK_A = 256
BLK_B = 512
LANES = 128
CHUNKS = 8
NEG = -1e30
f32 = jnp.float32
bf16 = jnp.bfloat16
PARAMS = pltpu.CompilerParams(vmem_limit_bytes=40 * 1024 * 1024)
SWAP = [(0, 1), (1, 0)]


def vmem_call(kernel, outs, scratch=(), smem=0, flops=0, moved=0):
    def call(*args):
        specs = [pl.BlockSpec(memory_space=pltpu.SMEM)] * smem + [pl.BlockSpec(memory_space=pltpu.VMEM)] * (len(args) - smem)
        return pl.pallas_call(
            kernel,
            out_shape=[jax.ShapeDtypeStruct(shape, kind) for shape, kind in outs],
            in_specs=specs,
            out_specs=[pl.BlockSpec(memory_space=pltpu.VMEM)] * len(outs),
            scratch_shapes=list(scratch),
            compiler_params=PARAMS,
            cost_estimate=pl.CostEstimate(flops=flops, bytes_accessed=moved, transcendentals=0),
        )(*args)

    return call


def spread(row):
    return jnp.broadcast_to(row, (CHUNKS, LANES))


def power(base, times):
    for _ in range(int(math.log2(times))):
        base = base * base
    return base


def scan_kernel(reverse, with_q, x_ref, a_ref, w_ref, skip_ref, y_ref, *rest):
    if with_q:
        eh_ref, eq_ref, sh, sq, ih = rest
    else:
        eh_ref, sh, ih = rest
    states, width = a_ref.shape
    steps = x_ref.shape[1] // CHUNKS

    def at(step):
        return pl.ds(steps - 1 - step if reverse else step, CHUNKS, stride=steps)

    for j in range(width // LANES):
        cols = pl.ds(j * LANES, LANES)
        rate = [spread(a_ref[n : n + 1, cols]) for n in range(states)]
        ih[0] = jnp.zeros((CHUNKS, LANES), f32)
        zero = ih[0]

        def local(step, carry):
            x = x_ref[j, at(step), :]
            if with_q:
                h, q = carry
                q = tuple(a * (u + v) for a, u, v in zip(rate, q, h))
            else:
                (h,) = carry
            h = tuple(a * v + x for a, v in zip(rate, h))
            return (h, q) if with_q else (h,)

        done = lax.fori_loop(0, steps, local, ((zero,) * states,) * (2 if with_q else 1), unroll=4)
        for n in range(states):
            sh[n] = done[0][n]
            if with_q:
                sq[n] = done[1][n]
        jump = power(a_ref[:, cols], steps)
        hold = jnp.zeros((states, LANES), f32)
        hold_q = jnp.zeros((states, LANES), f32)
        for k in range(CHUNKS):
            k = CHUNKS - 1 - k if reverse else k
            ih[:, k, :] = hold
            if with_q:
                hold_q = jump * (hold_q + float(steps) * hold) + sq[:, k, :]
            hold = jump * hold + sh[:, k, :]
        eh_ref[:, cols] = hold
        if with_q:
            eq_ref[:, cols] = hold_q
        weight = [spread(w_ref[n : n + 1, cols]) for n in range(states)]
        skip = spread(skip_ref[:, cols])

        def emit(step, h):
            x = x_ref[j, at(step), :]
            h = tuple(a * v + x for a, v in zip(rate, h))
            parts = [w * v for w, v in zip(weight, h)]
            while len(parts) > 1:
                parts = [parts[i] + parts[i + 1] for i in range(0, len(parts), 2)]
            y_ref[j, at(step), :] = parts[0] + skip * x
            return h

        lax.fori_loop(0, steps, emit, tuple(ih[n] for n in range(states)), unroll=4)


def carry_kernel(reverse, y_ref, a_ref, w_ref, h_ref, o_ref, ih):
    states, width = a_ref.shape
    steps = y_ref.shape[1] // CHUNKS

    def at(step):
        return pl.ds(steps - 1 - step if reverse else step, CHUNKS, stride=steps)

    for j in range(width // LANES):
        cols = pl.ds(j * LANES, LANES)
        rate = [spread(a_ref[n : n + 1, cols]) for n in range(states)]
        jump = power(a_ref[:, cols], steps)
        hold = w_ref[:, cols] * h_ref[:, cols]
        for k in range(CHUNKS):
            ih[:, CHUNKS - 1 - k if reverse else k, :] = hold
            hold = jump * hold

        def emit(step, h):
            h = tuple(a * v for a, v in zip(rate, h))
            parts = list(h)
            while len(parts) > 1:
                parts = [parts[i] + parts[i + 1] for i in range(0, len(parts), 2)]
            o_ref[j, at(step), :] = y_ref[j, at(step), :] + parts[0]
            return h

        lax.fori_loop(0, steps, emit, tuple(ih[n] for n in range(states)), unroll=4)


def sums_kernel(x_ref, g_ref, a_ref, h_ref, q_ref, sw_ref, sq_ref, sk_ref, sh, sv, ih, iq):
    states, width = a_ref.shape
    steps = x_ref.shape[1] // CHUNKS
    group = 8
    for j in range(width // LANES):
        cols = pl.ds(j * LANES, LANES)
        for base in range(0, states, group):
            some = pl.ds(base, group)
            rate = [spread(a_ref[n : n + 1, cols]) for n in range(base, base + group)]
            ih[0] = jnp.zeros((CHUNKS, LANES), f32)
            zero = ih[0]

            def local(step, carry):
                h, q = carry
                x = x_ref[j, pl.ds(step, CHUNKS, stride=steps), :]
                q = tuple(a * (u + v) for a, u, v in zip(rate, q, h))
                return tuple(a * v + x for a, v in zip(rate, h)), q

            h, q = lax.fori_loop(0, steps, local, ((zero,) * group,) * 2, unroll=4)
            for n in range(group):
                sh[n] = h[n]
                sv[n] = q[n]
            jump = power(a_ref[some, cols], steps)
            hold, hold_q = h_ref[some, cols], q_ref[some, cols]
            for k in range(CHUNKS):
                ih[:, k, :] = hold
                iq[:, k, :] = hold_q
                hold_q = jump * (hold_q + float(steps) * hold) + sv[:, k, :]
                hold = jump * hold + sh[:, k, :]

            def gain(step, carry):
                h, q, sw, sq = carry
                at = pl.ds(step, CHUNKS, stride=steps)
                x, g = x_ref[j, at, :], g_ref[j, at, :]
                q = tuple(a * (u + v) for a, u, v in zip(rate, q, h))
                h = tuple(a * v + x for a, v in zip(rate, h))
                sw = tuple(s + g * v for s, v in zip(sw, h))
                sq = tuple(s + g * v for s, v in zip(sq, q))
                return h, q, sw, sq

            begin = (tuple(ih[n] for n in range(group)), tuple(iq[n] for n in range(group)), (zero,) * group, (zero,) * group)
            _, _, sw, sq = lax.fori_loop(0, steps, gain, begin, unroll=2)
            for n in range(group):
                sw_ref[base + n : base + n + 1, cols] = jnp.sum(sw[n], axis=0, keepdims=True)
                sq_ref[base + n : base + n + 1, cols] = jnp.sum(sq[n], axis=0, keepdims=True)
        sk_ref[:, cols] = jnp.sum(x_ref[j] * g_ref[j], axis=0, keepdims=True)


def dot(a, b, ca, cb):
    return lax.dot_general(a, b, (((ca,), (cb,)), ((), ())), preferred_element_type=f32)


def masks(size, wide_ref, ok_ref, sub):
    context = ok_ref[sub : sub + 1, :] > 0.0
    rows = lax.broadcasted_iota(jnp.int32, (size, size), 0)
    cols = lax.broadcasted_iota(jnp.int32, (size, size), 1)
    return context, wide_ref[0] > 0, cols <= rows


def probabilities(q, ctx_k, k_ref, first, size, sub, lanes, mask, scale):
    context, wide, own = mask
    parts = [jnp.where(context, dot(q, ctx_k, 1, 1) * scale, NEG)]
    for other in range(sub):
        keys = k_ref[pl.ds(other * size, size), lanes]
        parts.append(jnp.where(wide, dot(q, keys, 1, 1) * scale, NEG))
    parts.append(jnp.where(own, dot(q, k_ref[pl.ds(sub * size, size), lanes], 1, 1) * scale, NEG))
    top = functools.reduce(jnp.maximum, [jnp.max(s, axis=1, keepdims=True) for s in parts])
    parts = [jnp.exp(s - top) for s in parts]
    total = sum(jnp.sum(s, axis=1, keepdims=True) for s in parts)
    inverse = 1.0 / total
    return [s * inverse for s in parts]


def attend_kernel(heads, scale, wide_ref, ok_ref, qkv_ref, ckv_ref, out_ref):
    rows = qkv_ref.shape[0]
    width = qkv_ref.shape[1] // 3
    dim = width // heads
    subs = ok_ref.shape[0]
    size = rows // subs
    for sub in range(subs):
        mask = masks(size, wide_ref, ok_ref, sub)
        here = pl.ds(sub * size, size)
        for h in range(heads):
            lq, lk, lv = (pl.ds(i * width + h * dim, dim) for i in range(3))
            ck = ckv_ref[pl.ds(sub * CTX, CTX), pl.ds(h * dim, dim)]
            cv = ckv_ref[pl.ds(sub * CTX, CTX), pl.ds(width + h * dim, dim)]
            probs = probabilities(qkv_ref[here, lq], ck, qkv_ref, 0, size, sub, lk, mask, scale)
            total = dot(probs[0].astype(bf16), cv, 1, 0)
            for other in range(sub + 1):
                total += dot(probs[1 + other].astype(bf16), qkv_ref[pl.ds(other * size, size), lv], 1, 0)
            out_ref[here, pl.ds(h * dim, dim)] = total.astype(bf16)


def attend_back_kernel(heads, scale, wide_ref, ok_ref, qkv_ref, ckv_ref, gm_ref, out_ref, ctx_ref, acc):
    rows = qkv_ref.shape[0]
    width = qkv_ref.shape[1] // 3
    dim = width // heads
    subs = ok_ref.shape[0]
    size = rows // subs
    acc[...] = jnp.zeros_like(acc)
    for sub in range(subs):
        mask = masks(size, wide_ref, ok_ref, sub)
        here = pl.ds(sub * size, size)
        for h in range(heads):
            lq, lk, lv = (pl.ds(i * width + h * dim, dim) for i in range(3))
            lh = pl.ds(h * dim, dim)
            cs = pl.ds(sub * CTX, CTX)
            ck = ckv_ref[cs, lh]
            cv = ckv_ref[cs, pl.ds(width + h * dim, dim)]
            q = qkv_ref[here, lq]
            gm = gm_ref[here, lh]
            probs = probabilities(q, ck, qkv_ref, 0, size, sub, lk, mask, scale)
            values = [cv] + [qkv_ref[pl.ds(o * size, size), lv] for o in range(sub + 1)]
            keys = [ck] + [qkv_ref[pl.ds(o * size, size), lk] for o in range(sub + 1)]
            grads = [dot(gm, v, 1, 1) for v in values]
            inner = sum(jnp.sum(p * g, axis=1, keepdims=True) for p, g in zip(probs, grads))
            scores = [(p * (g - inner)).astype(bf16) for p, g in zip(probs, grads)]
            grad_q = sum(dot(s, k, 1, 0) for s, k in zip(scores, keys))
            out_ref[here, lq] = (grad_q * scale).astype(bf16)
            ctx_ref[cs, lh] = dot(scores[0], q, 0, 0) * scale
            ctx_ref[cs, pl.ds(width + h * dim, dim)] = dot(probs[0].astype(bf16), gm, 0, 0)
            for o in range(sub + 1):
                there = pl.ds(o * size, size)
                acc[there, lh] += dot(scores[1 + o], q, 0, 0) * scale
                acc[there, pl.ds(width + h * dim, dim)] += dot(probs[1 + o].astype(bf16), gm, 0, 0)
    out_ref[:, pl.ds(width, 2 * width)] = acc[...].astype(bf16)


def halve(x, axis, dim):
    size = lax.axis_size(axis)
    if size == 1:
        return x
    if size != 2:
        return lax.psum_scatter(x, axis, scatter_dimension=dim, tiled=True)
    place = lax.axis_index(axis)
    half = x.shape[dim] // 2
    keep = lax.dynamic_slice_in_dim(x, place * half, half, dim)
    send = lax.dynamic_slice_in_dim(x, (1 - place) * half, half, dim)
    got = lax.ppermute(send, axis, SWAP)
    return (keep.astype(f32) + got.astype(f32)).astype(x.dtype)


def widen(x, axis, dim):
    size = lax.axis_size(axis)
    if size == 1:
        return x
    if size != 2:
        return lax.all_gather(x, axis, axis=dim, tiled=True)
    got = lax.ppermute(x, axis, SWAP)
    first = lax.axis_index(axis) == 0
    return jnp.concatenate([jnp.where(first, x, got), jnp.where(first, got, x)], axis=dim)


def gather_tp(x):
    size, place = lax.axis_size("tp"), lax.axis_index("tp")
    out = lax.dynamic_update_index_in_dim(jnp.zeros((size,) + x.shape, x.dtype), x, place, 0)
    for d in range(1, size):
        got = lax.ppermute(x, "tp", [(i, i ^ d) for i in range(size)])
        out = lax.dynamic_update_index_in_dim(out, got, place ^ d, 0)
    return out.reshape((-1,) + x.shape[1:])


def exchange_tp(x):
    size, place = lax.axis_size("tp"), lax.axis_index("tp")
    out = [lax.dynamic_index_in_dim(x, place, 0, keepdims=False)]
    for d in range(1, size):
        send = lax.dynamic_index_in_dim(x, place ^ d, 0, keepdims=False)
        out.append(lax.ppermute(send, "tp", [(i, i ^ d) for i in range(size)]))
    return out


def scatter_tp(x):
    size = lax.axis_size("tp")
    blocks = exchange_tp(x.reshape((size, -1) + x.shape[1:]))
    return sum(b.astype(f32) for b in blocks)


def shift_span(x, by):
    size = lax.axis_size("span")
    return lax.ppermute(x, "span", [(i, i + by) for i in range(size) if 0 <= i + by < size])


def norm_parts(values):
    center = values - jnp.mean(values, axis=-1, keepdims=True)
    inverse_dev = lax.rsqrt(jnp.mean(center * center, axis=-1, keepdims=True) + 1e-05)
    return center * inverse_dev, inverse_dev


def norm_back(grad_values, scaled, inverse_dev, gain_vector):
    weighted = grad_values * gain_vector
    return inverse_dev * (
        weighted
        - jnp.mean(weighted, axis=-1, keepdims=True)
        - scaled * jnp.mean(weighted * scaled, axis=-1, keepdims=True)
    )


def gelu_parts(a):
    c = math.sqrt(2.0 / math.pi)
    t = jnp.tanh(c * (a + 0.044715 * a * a * a))
    half = 0.5 * (1.0 + t)
    return a * half, half + 0.5 * a * (1.0 - t * t) * c * (1.0 + 3 * 0.044715 * a * a)


def body(
    activations,
    cotangent,
    block_sizes,
    context_back,
    first_gain,
    first_bias,
    w_query,
    w_key,
    w_value,
    w_out,
    second_gain,
    second_bias,
    w_up,
    w_down,
    decay_rate,
    input_map,
    output_map,
    step_size,
    skip_gain,
):
    spans, tp = lax.axis_size("span"), lax.axis_size("tp")
    span, place = lax.axis_index("span"), lax.axis_index("tp")
    seq_ways = spans * tp
    dp_ways = lax.axis_size("y") * lax.axis_size("core")
    dp_place = lax.axis_index("y") * lax.axis_size("core") + lax.axis_index("core")
    tokens, model = activations.shape[1:]
    rows = tp * tokens
    subs = rows // BLK_A
    ctx_rows = subs * CTX
    heads = HEADS // tp
    dim = model // HEADS
    scale = dim ** (-0.5)
    block = model // seq_ways
    ff_block = w_down.shape[0]
    channels = spans * block
    aligned = heads == spans and block == dim
    activations, cotangent, width = activations[0], cotangent[0], block_sizes[0]

    vectors = jnp.stack([first_gain, first_bias, second_gain, second_bias])
    vectors = lax.all_to_all(
        jnp.broadcast_to(vectors, (seq_ways,) + vectors.shape), ("span", "tp"), split_axis=0, concat_axis=0, tiled=True
    )
    gain_one, bias_one, gain_two, bias_two = jnp.swapaxes(vectors, 0, 1).reshape(4, model).astype(f32)
    states = decay_rate.shape[1]
    ssm = jnp.concatenate([decay_rate.T, input_map.T, output_map.T, step_size[None], skip_gain[None]])
    ssm = widen(ssm[:, None], "span", 1).reshape(-1, channels)
    speed, inward, outward = ssm[:states], ssm[states : 2 * states], ssm[2 * states : 3 * states]
    step, skip = ssm[3 * states : 3 * states + 1], ssm[3 * states + 1 :]
    decay = jnp.exp(-step * speed)
    mix = outward * inward * step

    def share(w, axis):
        size = w.shape[axis] // dp_ways
        return lax.dynamic_slice_in_dim(w, dp_place * size, size, axis)

    def from_columns(w):
        part = lax.all_to_all(share(w, 1), "tp", split_axis=0, concat_axis=0, tiled=True)
        part = widen(part[None], "span", 0)
        part = widen(widen(part, "y", 2), "core", 2) if lax.axis_size("y") == 2 else widen(part, ("y", "core"), 2)
        part = part.reshape(spans, tp, 2, dp_ways // 2, -1, w.shape[2]) if lax.axis_size("y") == 2 else part
        if lax.axis_size("y") == 2:
            part = jnp.swapaxes(part, 2, 3)
        return part.reshape(model, w.shape[2])

    def from_rows(w):
        part = widen(share(w, 0)[None], "span", 0)
        if lax.axis_size("y") == 2:
            part = widen(widen(part, "y", 1), "core", 1)
            part = jnp.swapaxes(part.reshape(spans, 2, dp_ways // 2, -1, model), 1, 2)
        else:
            part = widen(part, ("y", "core"), 1)
        return part.reshape(-1, model)

    def head_columns(w):
        return w.reshape(block, heads, tp, dim).transpose(2, 0, 1, 3).reshape(tp, block, heads * dim)

    mine = heads * dim
    qkv_w = from_columns(jnp.concatenate([head_columns(w) for w in (w_query, w_key, w_value)], axis=2))
    if aligned:
        out_w = from_rows(w_out)
    else:
        out_w = lax.all_gather(w_out, ("span", "tp"), axis=0, tiled=True).reshape(heads, tp, dim, model)
        out_w = lax.dynamic_index_in_dim(out_w, place, 1, keepdims=False).reshape(mine, model)
    up_w = from_columns(w_up.reshape(block, spans, tp, ff_block).transpose(2, 0, 1, 3).reshape(tp, block, -1))
    down_w = from_rows(w_down)

    scaled_one, inverse_one = norm_parts(activations)
    lowered = gather_tp((scaled_one * gain_one + bias_one).astype(bf16))
    cot_span = gather_tp(cotangent)

    def own_channels(x):
        return lax.dynamic_index_in_dim(x.reshape(-1, spans, tp, block), place, 2, keepdims=False).reshape(-1, channels)

    def lane_groups(x):
        return jnp.swapaxes(x.reshape(rows, -1, LANES), 0, 1)

    def joined(x):
        return jnp.swapaxes(x, 0, 1).reshape(rows, channels)

    channel_in = lane_groups(own_channels(lowered)).astype(f32)
    hold = pltpu.VMEM((states, CHUNKS, LANES), f32)
    wide_shape, state_shape = ((channels // LANES, rows, LANES), f32), ((states, channels), f32)
    scan_cost = dict(flops=rows * channels * states * 8, moved=rows * channels * 8)
    local, end_h, end_q = vmem_call(
        functools.partial(scan_kernel, False, True), [wide_shape, state_shape, state_shape], [hold] * 3, **scan_cost
    )(channel_in, decay, mix, skip)
    jump = jnp.exp(-float(rows) * step * speed)
    if spans == 2:
        begin_h, begin_q = shift_span(jnp.stack([end_h, end_q]), 1)
    else:
        begin_h, begin_q = jnp.zeros_like(end_h), jnp.zeros_like(end_q)
        all_h, all_q = lax.all_gather(jnp.stack([end_h, end_q]), "span", axis=1)
        for other in range(spans - 1):
            next_q = jump * (begin_q + float(rows) * begin_h) + all_q[other]
            next_h = jump * begin_h + all_h[other]
            begin_h, begin_q = jnp.where(other < span, next_h, begin_h), jnp.where(other < span, next_q, begin_q)
    (conv,) = vmem_call(functools.partial(carry_kernel, False), [wide_shape], [hold], **scan_cost)(local, decay, mix, begin_h)

    def starts_of(which):
        begin = which * rows + jnp.arange(subs, dtype=jnp.int32) * BLK_A
        return begin // width * width

    def picks(begin_span, of_span):
        spots = (starts_of(begin_span)[:, None] - context_back[None, :]).reshape(-1, 1)
        return (spots == of_span * rows + jnp.arange(rows, dtype=jnp.int32)[None, :]).astype(bf16)

    own_pick, next_pick = picks(span, span), picks(span + 1, span)
    to_next = jnp.dot(next_pick, joined((local if spans == 2 else conv).astype(bf16)))
    from_last = shift_span(to_next, 1)
    context = gather_tp(jnp.dot(own_pick, joined(conv.astype(bf16))) + from_last)
    context = context.reshape(tp, ctx_rows, spans, block).transpose(1, 2, 0, 3).reshape(ctx_rows, model)
    valid = (starts_of(span)[:, None] >= context_back[None, :]).astype(f32)
    wide = (width > BLK_A).astype(jnp.int32).reshape(1)

    qkv = jnp.dot(lowered, qkv_w, preferred_element_type=f32).astype(bf16)
    ctx_kv = jnp.dot(context, qkv_w[:, mine:], preferred_element_type=f32).astype(bf16)
    pairs = rows * (CTX + rows) * mine
    (mixed,) = vmem_call(
        functools.partial(attend_kernel, heads, scale), [((rows, mine), bf16)], smem=1, flops=4 * pairs, moved=rows * mine * 8
    )(wide, valid, qkv, ctx_kv)
    branch = jnp.dot(mixed, out_w, preferred_element_type=f32).astype(bf16)
    first_sum = activations + scatter_tp(branch)

    scaled_two, inverse_two = norm_parts(first_sum)
    normal_two = gather_tp((scaled_two * gain_two + bias_two).astype(bf16))
    pre_gate = jnp.dot(normal_two, up_w, preferred_element_type=f32)
    hidden, slope = gelu_parts(pre_gate)
    hidden = hidden.astype(bf16)
    grad_pre = (dot(cot_span, down_w, 1, 1) * slope).astype(bf16)
    grad_norm_two = scatter_tp(dot(grad_pre, up_w, 1, 1).astype(bf16))
    result = first_sum + scatter_tp(jnp.dot(hidden, down_w, preferred_element_type=f32).astype(bf16))
    grad_down = dot(hidden, cot_span, 0, 0)
    grad_up = dot(normal_two, grad_pre, 0, 0)

    grad_first = cotangent.astype(f32) + norm_back(grad_norm_two, scaled_two, inverse_two, gain_two)
    grad_branch = gather_tp(grad_first.astype(bf16))
    grad_mixed = dot(grad_branch, out_w, 1, 1).astype(bf16)
    grad_out = dot(mixed, grad_branch, 0, 0)
    grad_qkv, grad_ctx = vmem_call(
        functools.partial(attend_back_kernel, heads, scale),
        [((rows, 3 * mine), bf16), ((ctx_rows, 2 * mine), f32)],
        [pltpu.VMEM((rows, 2 * mine), f32)],
        smem=1,
        flops=10 * pairs,
        moved=rows * mine * 16,
    )(wide, valid, qkv, ctx_kv, grad_mixed)
    grad_lowered = scatter_tp(dot(grad_qkv, qkv_w, 1, 1).astype(bf16))
    grad_ctx_low = grad_ctx.astype(bf16)
    grad_qkv_w = dot(lowered, grad_qkv, 0, 0)
    grad_qkv_w = jnp.concatenate([grad_qkv_w[:, :mine], grad_qkv_w[:, mine:] + dot(context, grad_ctx_low, 0, 0)], axis=1)

    grad_context = dot(grad_ctx_low, qkv_w[:, mine:], 1, 1).astype(bf16)
    grad_context = grad_context.reshape(ctx_rows, spans, tp, block).transpose(2, 0, 1, 3)
    grad_context = sum(b.astype(f32) for b in exchange_tp(grad_context)).astype(bf16).reshape(ctx_rows, channels)
    from_next = shift_span(grad_context, -1)
    grad_states = lane_groups(dot(own_pick, grad_context, 0, 0) + dot(next_pick, from_next, 0, 0))
    grad_local, grad_end = vmem_call(
        functools.partial(scan_kernel, True, False), [wide_shape, state_shape], [hold] * 2, **scan_cost
    )(grad_states, decay, mix, skip)
    if spans == 2:
        grad_begin = shift_span(grad_end, -1)
    else:
        grad_begin = jnp.zeros_like(grad_end)
        ends = lax.all_gather(grad_end, "span", axis=0)
        for other in range(spans - 1, 0, -1):
            grad_begin = jnp.where(other > span, jump * grad_begin + ends[other], grad_begin)
    (grad_conv,) = vmem_call(functools.partial(carry_kernel, True), [wide_shape], [hold], **scan_cost)(
        grad_local, decay, mix, grad_begin
    )
    sum_w, sum_q, sum_skip = vmem_call(
        sums_kernel, [state_shape, state_shape, ((1, channels), f32)], [pltpu.VMEM((8, CHUNKS, LANES), f32)] * 4, **scan_cost
    )(channel_in, grad_states, decay, begin_h, begin_q)
    back = exchange_tp(joined(grad_conv.astype(bf16)).reshape(tp, tokens, channels))
    grad_normal = grad_lowered.reshape(tokens, spans, tp, block)
    for d, part in enumerate(back):
        part = part.astype(f32).reshape(tokens, spans, 1, block)
        grad_normal = grad_normal + jnp.where(
            jnp.arange(tp)[None, None, :, None] == place ^ d, jnp.broadcast_to(part, grad_normal.shape), 0.0
        )
    grad_normal = grad_normal.reshape(tokens, model)
    grad_inputs = grad_first + norm_back(grad_normal, scaled_one, inverse_one, gain_one)

    lines = jnp.stack(
        [
            jnp.sum(grad_normal * scaled_one, axis=0),
            jnp.sum(grad_normal, axis=0),
            jnp.sum(grad_norm_two * scaled_two, axis=0),
            jnp.sum(grad_norm_two, axis=0),
        ]
    )
    lines = lines.reshape(4, spans, tp, block).transpose(2, 0, 1, 3)
    lines = sum(exchange_tp(lines))
    sums = jnp.concatenate([sum_w, sum_q, sum_skip]).reshape(-1, spans, block)
    small = jnp.concatenate([lines, sums])
    small = halve(small, "span", 1)[:, 0]
    small = jnp.sum(widen(widen(small[None], "core", 0), "y", 0), axis=0)
    rate_own, in_own, out_own = decay_rate.T, input_map.T, output_map.T
    grad_mix, grad_skip = small[4 : 4 + states], small[4 + 2 * states]
    grad_speed = -(out_own * in_own * step_size) * small[4 + states : 4 + 2 * states]
    grad_rate = (grad_speed * step_size).T
    grad_in = (grad_mix * out_own * step_size).T
    grad_outward = (grad_mix * in_own * step_size).T
    grad_step = jnp.sum(grad_mix * out_own * in_own + grad_speed * rate_own, axis=0)

    def spread_rows(g, dim_):
        if lax.axis_size("y") == 2:
            return widen(widen(g, "y", dim_), "core", dim_)
        return widen(g, ("y", "core"), dim_)

    def reduce_dp(g, dim_):
        if lax.axis_size("y") == 2:
            return halve(halve(g, "core", dim_), "y", dim_)
        return halve(g, ("y", "core"), dim_)

    def to_rows(g):
        g = reduce_dp(g.astype(bf16).reshape(spans, -1, model), 1)
        return spread_rows(halve(g, "span", 0)[0], 0).astype(f32)

    def to_columns(g, cuts):
        g = reduce_dp(g.astype(bf16).reshape(spans, tp, block, -1), 2)
        g = halve(g, "span", 0)[0]
        g = lax.all_to_all(g, "tp", split_axis=0, concat_axis=0, tiled=True)
        g = g.reshape((tp, -1) + cuts)
        return spread_rows(jnp.moveaxis(g, 0, -2).reshape(g.shape[1], -1), 0)

    grad_w_down = to_rows(grad_down)
    grad_w_up = to_columns(grad_up, (spans, ff_block)).astype(f32)
    if aligned:
        grad_w_out = to_rows(grad_out)
    else:
        full = jnp.zeros((heads, tp, dim, model), bf16)
        full = lax.dynamic_update_index_in_dim(full, grad_out.astype(bf16).reshape(heads, dim, model), place, 1)
        grad_w_out = lax.psum_scatter(full.reshape(model, model), ("span", "tp"), scatter_dimension=0, tiled=True)
        grad_w_out = lax.psum(grad_w_out, ("y", "core")).astype(f32)
    grads = to_columns(grad_qkv_w, (3, heads, dim)).reshape(block, 3, model).astype(f32)
    return (
        result[None],
        grad_inputs[None],
        small[0],
        small[1],
        grads[:, 0],
        grads[:, 1],
        grads[:, 2],
        grad_w_out,
        small[2],
        small[3],
        grad_w_up,
        grad_w_down,
        grad_rate,
        grad_in,
        grad_outward,
        grad_step,
        grad_skip,
    )


def solution(mesh):
    dp_ways, seq_ways = mesh.shape["dp"], mesh.shape["seq"]
    dp, seq = ("y", "core"), ("span", "tp")
    lone, flat, cut = P(), P(seq), P(seq, None)
    data = P(dp, seq, None)
    in_specs = (data, data, P(dp), lone, flat, flat, cut, cut, cut, cut, flat, flat, cut, cut, cut, cut, cut, flat, flat)
    out_specs = (data, data, flat, flat, cut, cut, cut, cut, flat, flat, cut, cut, cut, cut, cut, flat, flat)

    def run(activations, *others):
        tp = BLK_B // (activations.shape[1] // seq_ways)
        fine = Mesh(mesh.devices.reshape(dp_ways // 2, 2, seq_ways // tp, tp), dp + seq)
        whole = jax.shard_map(body, mesh=fine, in_specs=in_specs, out_specs=out_specs, check_vma=False)
        return whole(activations, *others)

    return run
```

```python
import functools
import math

import jax
import jax.numpy as jnp
from jax import lax
from jax.experimental import pallas as pl
from jax.experimental.pallas import tpu as pltpu
from jax.sharding import Mesh
from jax.sharding import PartitionSpec as P

HEADS = 8
CTX = 128
BLK_A = 256
BLK_B = 512
TP = 4
TOKENS = 128
LANES = 128
UNITS = 256
STATES = 16
CHUNKS = 8
NEG = -1e30
f32 = jnp.float32
bf16 = jnp.bfloat16
PARAMS = pltpu.CompilerParams(vmem_limit_bytes=48 * 1024 * 1024)
SWAP = [(0, 1), (1, 0)]


SPAN, PLACE, ROW, CORE, WIDE = range(5)


def call(kernel, outs, *args, scratch=(), loose=(), after=(), flops=0, moved=0):
    count = len(args)
    vmem, free = pl.BlockSpec(memory_space=pltpu.VMEM), pl.BlockSpec(memory_space=pl.ANY)
    specs = [pl.BlockSpec(memory_space=pltpu.SMEM)] + [free if i in loose else vmem for i in range(1, count)] + [free] * len(after)

    def inner(*refs):
        kernel(*refs[:count], *refs[count + len(after) :])

    return pl.pallas_call(
        inner,
        out_shape=[jax.ShapeDtypeStruct(shape, kind) for shape, kind in outs],
        in_specs=specs,
        out_specs=[vmem] * len(outs),
        scratch_shapes=list(scratch),
        compiler_params=PARAMS,
        cost_estimate=pl.CostEstimate(flops=flops, bytes_accessed=moved, transcendentals=0),
    )(*args, *after)


def part(index, size):
    return pl.ds(pl.multiple_of(index * size, size), size)


def dot(a, b, ca, cb):
    return lax.dot_general(a, b, (((ca,), (cb,)), ((), ())), preferred_element_type=f32)


def wide(ref):
    return ref[...].astype(f32)


def share_kernel(scal, wq, wk, wv, up, out, qkv_send, up_send, out_send, sems):
    span, core = scal[SPAN], scal[CORE]
    copies = []
    for rank in range(TP):
        for m, w in enumerate((wq, wk, wv)):
            copies.append((w.at[:, part(core * TP + rank, LANES)], qkv_send.at[rank, :, pl.ds(m * LANES, LANES)]))
        for s in range(2):
            there = ((s ^ span) * TP + rank) * 2 + core
            copies.append((up.at[:, part(there, UNITS)], up_send.at[rank, :, pl.ds(s * UNITS, UNITS)]))
    copies.append((out.at[part(core, 64), :], out_send))
    copies = [pltpu.make_async_copy(a, b, sems.at[i]) for i, (a, b) in enumerate(copies)]
    for copy in copies:
        copy.start()
    for copy in copies:
        copy.wait()


def norm_rows(x):
    center = x - jnp.mean(x, axis=1, keepdims=True)
    inverse = lax.rsqrt(jnp.mean(center * center, axis=1, keepdims=True) + 1e-05)
    return center * inverse, inverse


def turned_norm(scal, scaled, vec, which, low_ref):
    blocks = vec.shape[0]
    for r in range(blocks):
        n = r ^ (scal[SPAN] * (blocks // 2))
        line = vec[n].astype(f32)
        value = scaled[:, part(n, LANES)] * line[which : which + 1] + line[which + 1 : which + 2]
        low_ref[:, pl.ds(r * LANES, LANES)] = value.astype(bf16)


def norm_one_kernel(scal, x, vec, low, scaled):
    scaled[...], _ = norm_rows(x[...])
    turned_norm(scal, scaled, vec, 0, low)


def norm_two_kernel(scal, x, own, a, b, c, vec, total, low, scaled):
    first = x[...] + ((wide(own) + wide(a)) + (wide(b) + wide(c)))
    total[...] = first
    scaled[...], _ = norm_rows(first)
    turned_norm(scal, scaled, vec, 2, low)


def line_of(vec, which):
    return jnp.concatenate([vec[n].astype(f32)[which : which + 1] for n in range(vec.shape[0])], axis=1)


def norm_back(grad, scaled, inverse, gain):
    e = grad * gain
    return inverse * (e - jnp.mean(e, axis=1, keepdims=True) - scaled * jnp.mean(e * scaled, axis=1, keepdims=True))


def unturned(scal, out, parts):
    half = out.shape[1] // 2
    for s in range(2):
        lanes = pl.ds(s * half, half)
        out[:, part(s ^ scal[SPAN], half)] = sum(p[:, lanes].astype(f32) for p in parts)


def norm_two_back_kernel(scal, total, own, a, b, c, cot, vec, grad_first, low, lines, grad):
    unturned(scal, grad, (own, a, b, c))
    scaled, inverse = norm_rows(total[...])
    value = cot[...].astype(f32) + norm_back(grad[...], scaled, inverse, line_of(vec, 2))
    grad_first[...] = value
    low[...] = value.astype(bf16)
    lines[0:1, :] = jnp.sum(grad[...] * scaled, axis=0, keepdims=True)
    lines[1:2, :] = jnp.sum(grad[...], axis=0, keepdims=True)
    lines[2:8, :] = jnp.zeros((6, lines.shape[1]), f32)


def last_kernel(scal, x, vec, grad_first, own, a, b, c, p0, p1, p2, p3, lines_two, out, lines, grad, turned):
    place = scal[PLACE]
    turned[...] = (wide(own) + wide(a)) + (wide(b) + wide(c))
    for j, p in enumerate((p0, p1, p2, p3)):
        for s in range(2):
            lanes = part(s * TP + (place ^ j), LANES)
            turned[:, lanes] = turned[:, lanes] + p[:, pl.ds(s * LANES, LANES)].astype(f32)
    unturned(scal, grad, (turned,))
    scaled, inverse = norm_rows(x[...])
    out[...] = grad_first[...] + norm_back(grad[...], scaled, inverse, line_of(vec, 0))
    gain = jnp.sum(grad[...] * scaled, axis=0, keepdims=True)
    bias = jnp.sum(grad[...], axis=0, keepdims=True)
    for n in range(lines.shape[0]):
        lanes = slice(n * LANES, (n + 1) * LANES)
        lines[n, 0:1, :] = gain[:, lanes]
        lines[n, 1:2, :] = bias[:, lanes]
        lines[n, 2:4, :] = lines_two[0:2, lanes]
        lines[n, 4:8, :] = jnp.zeros((4, LANES), f32)


def spread(row):
    return jnp.broadcast_to(row, (CHUNKS, LANES))


def power(base, times):
    for _ in range(int(math.log2(times))):
        base = base * base
    return base


def total_of(parts):
    while len(parts) > 1:
        parts = [parts[i] + parts[i + 1] for i in range(0, len(parts), 2)]
    return parts[0]


def one_hot(spots, rows):
    return (spots[...] == lax.broadcasted_iota(jnp.int32, (spots.shape[0], rows), 1)).astype(bf16)


def own_channels(scal, xs, parts):
    place = scal[PLACE]
    for j, x in enumerate(parts):
        for s in range(2):
            xs[s, part(place ^ j, TOKENS), :] = x[:, part(s * TP + place, LANES)].astype(f32)


def scan(reverse, xs, a_ref, w_ref, skips, y_ref, end, sh, ih, sq=None):
    states = a_ref.shape[0]
    steps = xs.shape[1] // CHUNKS

    def at(step):
        return pl.ds(steps - 1 - step if reverse else step, CHUNKS, stride=steps)

    for s in range(xs.shape[0]):
        cols = pl.ds(s * LANES, LANES)
        rate = [spread(a_ref[n : n + 1, cols]) for n in range(states)]
        ih[0] = jnp.zeros((CHUNKS, LANES), f32)
        zero = ih[0]

        def local(step, carry):
            x = xs[s, at(step), :]
            if sq is not None:
                h, q = carry
                q = tuple(a * (u + v) for a, u, v in zip(rate, q, h))
            else:
                (h,) = carry
            h = tuple(a * v + x for a, v in zip(rate, h))
            return (h, q) if sq is not None else (h,)

        done = lax.fori_loop(0, steps, local, ((zero,) * states,) * (1 if sq is None else 2), unroll=4)
        for n in range(states):
            sh[n] = done[0][n]
            if sq is not None:
                sq[n] = done[1][n]
        jump = power(a_ref[:, cols], steps)
        hold = jnp.zeros((states, LANES), f32)
        hold_q = jnp.zeros((states, LANES), f32)
        for k in range(CHUNKS):
            k = CHUNKS - 1 - k if reverse else k
            ih[:, k, :] = hold
            if sq is not None:
                hold_q = jump * (hold_q + float(steps) * hold) + sq[:, k, :]
            hold = jump * hold + sh[:, k, :]
        end(s, hold, hold_q)
        weight = [spread(w_ref[n : n + 1, cols]) for n in range(states)]
        skip = spread(skips[s][49:50, :])

        def emit(step, h):
            x = xs[s, at(step), :]
            h = tuple(a * v + x for a, v in zip(rate, h))
            y_ref[s, at(step), :] = total_of([w * v for w, v in zip(weight, h)]) + skip * x
            return h

        lax.fori_loop(0, steps, emit, tuple(ih[n] for n in range(states)), unroll=4)


def scan_kernel(scal, x0, x1, x2, x3, ssm0, ssm1, spots, y, to_next, ends, decay, mix, xs, low, sh, sq, ih):
    own_channels(scal, xs, (x0, x1, x2, x3))
    n = decay.shape[0]
    for s, ssm in enumerate((ssm0, ssm1)):
        cols = pl.ds(s * LANES, LANES)
        step = ssm[48:49, :]
        decay[:, cols] = jnp.exp(-step * ssm[0:n, :])
        mix[:, cols] = ssm[32:48, :] * ssm[16:32, :] * step

    def end(s, h, q):
        other = pl.ds((1 - s) * LANES, LANES)
        ends[0:n, other] = h
        ends[n : 2 * n, other] = q

    scan(False, xs, decay, mix, (ssm0, ssm1), y, end, sh, ih, sq)
    for s in range(2):
        low[:, pl.ds((1 - s) * LANES, LANES)] = y[s].astype(bf16)
    to_next[...] = dot(one_hot(spots, low.shape[0]), low[...], 1, 0).astype(bf16)


def carry(reverse, y_ref, a_ref, w_ref, h_ref, out, ih):
    states = a_ref.shape[0]
    steps = y_ref.shape[1] // CHUNKS

    def at(step):
        return pl.ds(steps - 1 - step if reverse else step, CHUNKS, stride=steps)

    for s in range(y_ref.shape[0]):
        cols = pl.ds(s * LANES, LANES)
        rate = [spread(a_ref[n : n + 1, cols]) for n in range(states)]
        jump = power(a_ref[:, cols], steps)
        hold = w_ref[:, cols] * h_ref[0:states, cols]
        for k in range(CHUNKS):
            ih[:, CHUNKS - 1 - k if reverse else k, :] = hold
            hold = jump * hold

        def emit(step, h):
            h = tuple(a * v for a, v in zip(rate, h))
            out[s, at(step), :] = y_ref[s, at(step), :] + total_of(list(h))
            return h

        lax.fori_loop(0, steps, emit, tuple(ih[n] for n in range(states)), unroll=4)


def carry_kernel(scal, y, decay, mix, begin, from_last, spots, up, down, context, up_again, down_send, ih, ys, low, sem):
    copy = pltpu.make_async_copy(down.at[part(scal[CORE] * 2 + scal[ROW], LANES), :], down_send, sem)
    copy.start()
    carry(False, y, decay, mix, begin, ys, ih)
    for s in range(2):
        low[:, pl.ds(s * LANES, LANES)] = ys[s].astype(bf16)
    context[...] = (dot(one_hot(spots, low.shape[0]), low[...], 1, 0) + wide(from_last)).astype(bf16)
    up_again[...] = up[...]
    copy.wait()


def scan_back_kernel(scal, own, from_next, own_spots, next_spots, ssm0, ssm1, decay, mix, grad, y, ends, sh, ih):
    rows = y.shape[1]
    value = dot(one_hot(own_spots, rows), own[...], 0, 0) + dot(one_hot(next_spots, rows), from_next[...], 0, 0)
    for s in range(2):
        grad[s] = value[:, s * LANES : (s + 1) * LANES]

    def end(s, h, q):
        ends[:, pl.ds((1 - s) * LANES, LANES)] = h

    scan(True, grad, decay, mix, (ssm0, ssm1), y, end, sh, ih)


def carry_back_kernel(scal, y, decay, mix, begin, o0, o1, o2, o3, ih, ys):
    carry(True, y, decay, mix, begin, ys, ih)
    for j, out in enumerate((o0, o1, o2, o3)):
        for s in range(2):
            out[:, pl.ds(s * LANES, LANES)] = ys[s, part(scal[PLACE] ^ j, TOKENS), :].astype(bf16)


def sums_kernel(scal, x0, x1, x2, x3, gs, a_ref, begin, out, xs, sh, sv, ih, iq):
    own_channels(scal, xs, (x0, x1, x2, x3))
    states = a_ref.shape[0]
    steps = xs.shape[1] // CHUNKS
    group = 8
    out[2 * states :, :] = jnp.zeros((out.shape[0] - 2 * states, out.shape[1]), f32)
    for s in range(xs.shape[0]):
        cols = pl.ds(s * LANES, LANES)
        for base in range(0, states, group):
            some, more = pl.ds(base, group), pl.ds(states + base, group)
            rate = [spread(a_ref[n : n + 1, cols]) for n in range(base, base + group)]
            ih[0] = jnp.zeros((CHUNKS, LANES), f32)
            zero = ih[0]

            def local(step, carried):
                h, q = carried
                x = xs[s, pl.ds(step, CHUNKS, stride=steps), :]
                q = tuple(a * (u + v) for a, u, v in zip(rate, q, h))
                return tuple(a * v + x for a, v in zip(rate, h)), q

            h, q = lax.fori_loop(0, steps, local, ((zero,) * group,) * 2, unroll=4)
            for n in range(group):
                sh[n] = h[n]
                sv[n] = q[n]
            jump = power(a_ref[some, cols], steps)
            hold, hold_q = begin[some, cols], begin[more, cols]
            for k in range(CHUNKS):
                ih[:, k, :] = hold
                iq[:, k, :] = hold_q
                hold_q = jump * (hold_q + float(steps) * hold) + sv[:, k, :]
                hold = jump * hold + sh[:, k, :]

            def gain(step, carried):
                h, q, sw, sq = carried
                at = pl.ds(step, CHUNKS, stride=steps)
                x, g = xs[s, at, :], gs[s, at, :]
                q = tuple(a * (u + v) for a, u, v in zip(rate, q, h))
                h = tuple(a * v + x for a, v in zip(rate, h))
                sw = tuple(u + g * v for u, v in zip(sw, h))
                sq = tuple(u + g * v for u, v in zip(sq, q))
                return h, q, sw, sq

            first = (tuple(ih[n] for n in range(group)), tuple(iq[n] for n in range(group)), (zero,) * group, (zero,) * group)
            _, _, sw, sq = lax.fori_loop(0, steps, gain, first, unroll=2)
            for n in range(group):
                out[base + n : base + n + 1, cols] = jnp.sum(sw[n], axis=0, keepdims=True)
                out[states + base + n : states + base + n + 1, cols] = jnp.sum(sq[n], axis=0, keepdims=True)
        out[2 * states : 2 * states + 1, cols] = jnp.sum(xs[s] * gs[s], axis=0, keepdims=True)


def qkv_kernel(scal, x0, x1, x2, x3, w00, w10, w01, w11, w, qkv):
    for s, j, ref in ((0, 0, w00), (1, 0, w10), (0, 1, w01), (1, 1, w11)):
        for rank in range(TP):
            for m in range(3):
                w[pl.ds((s * TP + rank) * LANES, LANES), pl.ds((2 * m + j) * LANES, LANES)] = ref[rank, :, pl.ds(m * LANES, LANES)]
    for j, x in enumerate((x0, x1, x2, x3)):
        qkv[part(scal[PLACE] ^ j, TOKENS), :] = dot(x[...], w[...], 1, 0).astype(bf16)


def masks(size, is_wide, ok_ref, sub):
    rows = lax.broadcasted_iota(jnp.int32, (size, size), 0)
    cols = lax.broadcasted_iota(jnp.int32, (size, size), 1)
    return ok_ref[sub : sub + 1, :] > 0.0, is_wide > 0, cols <= rows


def out_of_order(out_ref, lanes, value, sub, place):
    each = value.shape[0] // TOKENS
    for i in range(each):
        out_ref[part((sub * each + i) ^ place, TOKENS), lanes] = value[i * TOKENS : (i + 1) * TOKENS]


def probabilities(q, ctx_k, k_ref, size, sub, lanes, mask, scale):
    context, earlier, own = mask
    parts = [jnp.where(context, dot(q, ctx_k, 1, 1) * scale, NEG)]
    for other in range(sub):
        keys = k_ref[pl.ds(other * size, size), lanes]
        parts.append(jnp.where(earlier, dot(q, keys, 1, 1) * scale, NEG))
    parts.append(jnp.where(own, dot(q, k_ref[pl.ds(sub * size, size), lanes], 1, 1) * scale, NEG))
    top = functools.reduce(jnp.maximum, [jnp.max(s, axis=1, keepdims=True) for s in parts])
    parts = [jnp.exp(s - top) for s in parts]
    inverse = 1.0 / sum(jnp.sum(s, axis=1, keepdims=True) for s in parts)
    return [s * inverse for s in parts]


def attend_kernel(scal, ok, qkv, c0, c1, c2, c3, w, out_own, out_0, out_1, mixed, ckv, out_w, b0, b1, b2, b3):
    place, core = scal[PLACE], scal[CORE]
    width = qkv.shape[1] // 3
    dim = LANES
    own = core ^ scal[SPAN]
    out_w[part(own, dim), :] = out_own[...]
    out_w[part((1 - own) * 2 + core, 64), :] = out_0[...]
    out_w[part((1 - own) * 2 + 1 - core, 64), :] = out_1[...]
    total = None
    for j, c in enumerate((c0, c1, c2, c3)):
        for s in range(2):
            term = dot(c[:, pl.ds(s * LANES, LANES)], w[part(s * TP + (place ^ j), LANES), pl.ds(width, 2 * width)], 1, 0)
            total = term if total is None else total + term
    ckv[...] = total.astype(bf16)
    subs = ok.shape[0]
    size = qkv.shape[0] // subs
    scale = dim ** (-0.5)
    for sub in range(subs):
        mask = masks(size, scal[WIDE], ok, sub)
        here = pl.ds(sub * size, size)
        for h in range(width // dim):
            lq, lk, lv = (pl.ds(i * width + h * dim, dim) for i in range(3))
            ck = ckv[pl.ds(sub * CTX, CTX), pl.ds(h * dim, dim)]
            cv = ckv[pl.ds(sub * CTX, CTX), pl.ds(width + h * dim, dim)]
            probs = probabilities(qkv[here, lq], ck, qkv, size, sub, lk, mask, scale)
            value = dot(probs[0].astype(bf16), cv, 1, 0)
            for other in range(sub + 1):
                value += dot(probs[1 + other].astype(bf16), qkv[pl.ds(other * size, size), lv], 1, 0)
            out_of_order(mixed, pl.ds(h * dim, dim), value.astype(bf16), sub, place)
    for j, b in enumerate((b0, b1, b2, b3)):
        b[...] = dot(mixed[pl.ds(j * TOKENS, TOKENS), :], out_w[...], 1, 0).astype(bf16)


def attend_back_kernel(scal, ok, qkv, ckv, g0, g1, g2, g3, out_w, w, out, ctx, x0, x1, x2, x3, gms, acc):
    place = scal[PLACE]
    width = qkv.shape[1] // 3
    dim = LANES
    subs = ok.shape[0]
    size = qkv.shape[0] // subs
    scale = dim ** (-0.5)
    for j, g in enumerate((g0, g1, g2, g3)):
        gms[part(place ^ j, TOKENS), :] = dot(g[...], out_w[...], 1, 1).astype(bf16)
    acc[...] = jnp.zeros_like(acc)
    for sub in range(subs):
        mask = masks(size, scal[WIDE], ok, sub)
        here = pl.ds(sub * size, size)
        cs = pl.ds(sub * CTX, CTX)
        for h in range(width // dim):
            lq, lk, lv = (pl.ds(i * width + h * dim, dim) for i in range(3))
            lh, lhv = pl.ds(h * dim, dim), pl.ds(width + h * dim, dim)
            ck, cv = ckv[cs, lh], ckv[cs, lhv]
            q, gm = qkv[here, lq], gms[here, lh]
            probs = probabilities(q, ck, qkv, size, sub, lk, mask, scale)
            values = [cv] + [qkv[pl.ds(o * size, size), lv] for o in range(sub + 1)]
            keys = [ck] + [qkv[pl.ds(o * size, size), lk] for o in range(sub + 1)]
            grads = [dot(gm, v, 1, 1) for v in values]
            inner = sum(jnp.sum(p * g, axis=1, keepdims=True) for p, g in zip(probs, grads))
            scores = [(p * (g - inner)).astype(bf16) for p, g in zip(probs, grads)]
            grad_q = sum(dot(s, k, 1, 0) for s, k in zip(scores, keys))
            out_of_order(out, lq, (grad_q * scale).astype(bf16), sub, place)
            ctx[cs, lh] = (dot(scores[0], q, 0, 0) * scale).astype(bf16)
            ctx[cs, lhv] = dot(probs[0].astype(bf16), gm, 0, 0).astype(bf16)
            for o in range(sub + 1):
                there = pl.ds(o * size, size)
                acc[there, lh] += dot(scores[1 + o], q, 0, 0) * scale
                acc[there, lhv] += dot(probs[1 + o].astype(bf16), gm, 0, 0)
    for sub in range(subs):
        out_of_order(out, pl.ds(width, 2 * width), acc[pl.ds(sub * size, size), :].astype(bf16), sub, place)
    for j, x in enumerate((x0, x1, x2, x3)):
        for s in range(2):
            rows = part(s * TP + (place ^ j), LANES)
            x[:, pl.ds(s * LANES, LANES)] = dot(ctx[...], w[rows, pl.ds(width, 2 * width)], 1, 1).astype(bf16)


def context_sum_kernel(scal, own, a, b, c, total, turned):
    value = ((wide(own) + wide(a)) + (wide(b) + wide(c))).astype(bf16)
    total[...] = value
    for s in range(2):
        turned[:, pl.ds((1 - s) * LANES, LANES)] = value[:, s * LANES : (s + 1) * LANES]


def attend_weights_kernel(scal, x0, x1, x2, x3, c0, c1, c2, c3, gqkv, gctx, mixed, g0, g1, g2, g3, q_send, q_keep, o_send, o_keep, rows, acc):
    place, core = scal[PLACE], scal[CORE]
    width = gqkv.shape[1] // 3
    for j, x in enumerate((x0, x1, x2, x3)):
        rows[pl.ds(j * TOKENS, TOKENS), :] = x[...]
    half = rows.shape[1] // 2
    for s in range(2):
        acc[pl.ds(s * half, half), :] = dot(rows[:, pl.ds(s * half, half)], gqkv[...], 0, 0)
    for j, c in enumerate((c0, c1, c2, c3)):
        for s in range(2):
            there = part(s * TP + (place ^ j), LANES)
            acc[there, pl.ds(width, 2 * width)] += dot(c[:, pl.ds(s * LANES, LANES)], gctx[...], 0, 0)
    for m in range(3):
        lanes = pl.ds(m * LANES, LANES)
        q_keep[:, lanes] = acc[:, pl.ds(2 * m * LANES, LANES)].astype(bf16)
        q_send[:, lanes] = acc[:, pl.ds((2 * m + 1) * LANES, LANES)].astype(bf16)
    for j, g in enumerate((g0, g1, g2, g3)):
        rows[pl.ds(j * TOKENS, TOKENS), :] = g[...]
    acc2 = dot(mixed[...], rows[...], 0, 0)
    acc[0:width, :] = acc2[:, : acc.shape[1]]
    acc[width : 2 * width, 0 : acc2.shape[1] - acc.shape[1]] = acc2[:, acc.shape[1] :]
    first, rest = acc.shape[1], acc2.shape[1] - acc.shape[1]
    for s in range(2):
        head = core ^ scal[SPAN] ^ s
        for ref, side in ((o_keep, core), (o_send, 1 - core)):
            at = head * 2 + side
            ref[pl.ds(s * 64, 64), 0:first] = acc[part(at, 64), :].astype(bf16)
            ref[pl.ds(s * 64, 64), first:] = acc[pl.ds(pl.multiple_of(width + at * 64, 64), 64), 0:rest].astype(bf16)


def units_kernel(scal, cot0, cot1, cot2, cot3, u00, u10, u01, u11, down, d00, d01, d10, d11, up_w, down_w, ahead, cot):
    row, core = scal[ROW], scal[CORE]
    half = up_w.shape[0] // 2
    for s, j, ref in ((0, 0, u00), (1, 0, u10), (0, 1, u01), (1, 1, u11)):
        for rank in range(TP):
            for k in range(2):
                up_w[pl.ds(s * half + rank * LANES, LANES), pl.ds((s ^ k) * half + j * UNITS, UNITS)] = ref[rank, :, pl.ds(k * UNITS, UNITS)]
    for j in range(2):
        down_w[pl.ds(j * UNITS, UNITS), :] = down[part(core ^ j, UNITS), :]
    for j, k, ref in ((0, 0, d00), (0, 1, d01), (1, 0, d10), (1, 1, d11)):
        down_w[pl.ds(pl.multiple_of(half + j * UNITS + (row ^ k) * LANES, LANES), LANES), :] = ref[...]
    for j, c in enumerate((cot0, cot1, cot2, cot3)):
        cot[pl.ds(j * TOKENS, TOKENS), :] = c[...]
    for i in range(4):
        tile = pl.ds(i * UNITS, UNITS)
        ahead[:, tile] = dot(cot[...], down_w[tile, :], 1, 1)


def gelu_parts(a):
    c = math.sqrt(2.0 / math.pi)
    t = jnp.tanh(c * (a + 0.044715 * a * a * a))
    half = 0.5 * (1.0 + t)
    return a * half, half + 0.5 * a * (1.0 - t * t) * c * (1.0 + 3 * 0.044715 * a * a)


def hidden_kernel(scal, n0, n1, n2, n3, up_w, ahead, o0, o1, o2, o3, h0, h1, p0, p1, rows, pre):
    for j, n in enumerate((n0, n1, n2, n3)):
        rows[pl.ds(j * TOKENS, TOKENS), :] = n[...]
    for i in range(4):
        s, j = divmod(i, 2)
        tile, lanes = pl.ds(i * UNITS, UNITS), pl.ds(s * UNITS, UNITS)
        act, slope = gelu_parts(dot(rows[...], up_w[:, tile], 1, 0))
        low = (ahead[:, tile] * slope).astype(bf16)
        (h0, h1)[j][:, lanes] = act.astype(bf16)
        (p0, p1)[j][:, lanes] = low
        pre[:, tile] = low
    for j, out in enumerate((o0, o1, o2, o3)):
        out[...] = dot(pre[pl.ds(j * TOKENS, TOKENS), :], up_w[...], 1, 1).astype(bf16)


def result_kernel(scal, h0, h1, down_w, o0, o1, o2, o3):
    for j, out in enumerate((o0, o1, o2, o3)):
        here = pl.ds(j * TOKENS, TOKENS)
        total = None
        for s in range(2):
            for k, h in enumerate((h0, h1)):
                term = dot(h[here, pl.ds(s * UNITS, UNITS)], down_w[pl.ds((2 * s + k) * UNITS, UNITS), :], 1, 0)
                total = term if total is None else total + term
        out[...] = total.astype(bf16)


def units_weights_kernel(scal, rows, cot, h0, h1, p0, p1, down_send, down_keep, up_send, up_keep):
    for h, p, down, up in ((h1, p1, down_send, up_send), (h0, p0, down_keep, up_keep)):
        for i in range(2):
            tile = pl.ds(i * UNITS, UNITS)
            down[tile, :] = dot(h[:, tile], cot[...], 0, 0).astype(bf16)
        for i in range(4):
            tile = pl.ds(i * UNITS, UNITS)
            up[tile, :] = dot(rows[:, tile], p[...], 0, 0).astype(bf16)


def units_one_kernel(scal, down, down_got, up, up_got, d_send, d_keep, u_send, u_keep):
    row = scal[ROW]
    for s in range(2):
        for ref, side in ((d_keep, row), (d_send, 1 - row)):
            there = part(2 * s + side, LANES)
            ref[pl.ds(s * LANES, LANES), :] = (wide(down.at[there, :]) + wide(down_got.at[there, :])).astype(bf16)
    half = u_keep.shape[0]
    u_keep[...] = (wide(up.at[pl.ds(0, half), :]) + wide(up_got.at[pl.ds(0, half), :])).astype(bf16)
    for s in range(2):
        there = (pl.ds(half, half), pl.ds(s * UNITS, UNITS))
        u_send[:, pl.ds((1 - s) * UNITS, UNITS)] = (wide(up.at[there]) + wide(up_got.at[there])).astype(bf16)


def units_two_kernel(scal, down, down_got, up, up_got, d_send, d_keep, u_send, u_keep):
    row = scal[ROW]
    for ref, s in ((d_keep, 0), (d_send, 1)):
        there = pl.ds(s * LANES, LANES)
        ref[...] = (wide(down.at[there, :]) + wide(down_got.at[there, :])).astype(bf16)
    for s in range(2):
        for ref, side in ((u_keep, row), (u_send, 1 - row)):
            there = part(2 * s + side, LANES)
            ref[:, pl.ds(s * LANES, LANES)] = (wide(up.at[:, there]) + wide(up_got.at[:, there])).astype(bf16)


def units_three_kernel(scal, down, down_got, up, up_got, low, x0, x1, x2, x3):
    low[...] = (wide(down) + wide(down_got)).astype(bf16)
    for j, x in enumerate((x0, x1, x2, x3)):
        there = part(scal[PLACE] ^ j, LANES)
        x[...] = (wide(up.at[there, :]) + wide(up_got.at[there, :])).astype(bf16)


def units_four_kernel(scal, low, x0, x1, x2, x3, out):
    out[0:LANES, :] = low[...]
    for j, x in enumerate((x0, x1, x2, x3)):
        out[LANES : 2 * LANES, part(scal[PLACE] ^ j, UNITS)] = x[...]


def units_home_kernel(scal, b00, b01, b10, b11, up, down):
    span, row, core = scal[SPAN], scal[ROW], scal[CORE]
    for j, k, ref in ((0, 0, b00), (0, 1, b01), (1, 0, b10), (1, 1, b11)):
        quarter = (core ^ j) * 2 + (row ^ k)
        down[part(quarter, LANES), :] = ref[0:LANES, :].astype(f32)
        for rank in range(TP):
            for s in range(2):
                there = ((s ^ span) * TP + rank) * 4 + quarter
                up[:, part(there, LANES)] = ref[LANES : 2 * LANES, pl.ds(rank * UNITS + s * LANES, LANES)].astype(f32)


def heads_one_kernel(scal, q, q_got, o, o_got, q_send, q_keep, o_send, o_keep):
    row = scal[ROW]
    for n in range(q.shape[0] // LANES):
        for ref, side in ((q_keep, row), (q_send, 1 - row)):
            there = part(2 * n + side, 64)
            ref[pl.ds(n * 64, 64), :] = (wide(q.at[there, :]) + wide(q_got.at[there, :])).astype(bf16)
    for s in range(2):
        for ref, side in ((o_keep, row), (o_send, 1 - row)):
            there = part(2 * s + side, 32)
            ref[pl.ds(s * 32, 32), :] = (wide(o.at[there, :]) + wide(o_got.at[there, :])).astype(bf16)


def heads_two_kernel(scal, q, q_got, o, o_got, q_send, q_keep, o_send, o_keep):
    half = q_keep.shape[0]
    for ref, s in ((q_keep, 0), (q_send, 1)):
        there = pl.ds(s * half, half)
        ref[...] = (wide(q.at[there, :]) + wide(q_got.at[there, :])).astype(bf16)
    for ref, s in ((o_keep, 0), (o_send, 1)):
        there = pl.ds(s * 32, 32)
        ref[...] = (wide(o.at[there, :]) + wide(o_got.at[there, :])).astype(bf16)


def heads_three_kernel(scal, q, q_got, o, o_got, low, x0, x1, x2, x3):
    low[...] = (wide(o) + wide(o_got)).astype(bf16)
    for j, x in enumerate((x0, x1, x2, x3)):
        there = part(scal[PLACE] ^ j, 64)
        x[...] = (wide(q.at[there, :]) + wide(q_got.at[there, :])).astype(bf16)


def heads_four_kernel(scal, low, x0, x1, x2, x3, out):
    width = x0.shape[1]
    half = low.shape[1] // 2
    for j, x in enumerate((x0, x1, x2, x3)):
        out[:, part(scal[PLACE] ^ j, width)] = x[...]
    for i in range(2):
        out[pl.ds(i * 32, 32), pl.ds(TP * width, half)] = low[:, pl.ds(i * half, half)]


def heads_home_kernel(scal, b00, b01, b10, b11, gq, gk, gv, go):
    row, core = scal[ROW], scal[CORE]
    width = 3 * LANES
    half = go.shape[1] // 2
    for j, k, ref in ((0, 0, b00), (0, 1, b01), (1, 0, b10), (1, 1, b11)):
        for rank in range(TP):
            for m, out in enumerate((gq, gk, gv)):
                lanes = pl.ds(rank * width + m * LANES, LANES)
                out[part(row ^ k, 64), part((core ^ j) * TP + rank, LANES)] = ref[:, lanes].astype(f32)
        there = part((core ^ j) * 2 + (row ^ k), 32)
        for i in range(2):
            go[there, pl.ds(i * half, half)] = ref[pl.ds(i * 32, 32), pl.ds(TP * width, half)].astype(f32)


def swap(x, axis):
    return lax.ppermute(x, axis, SWAP)


def across(x, d):
    return lax.ppermute(x, "tp", [(i, i ^ d) for i in range(TP)])


def gathered(x):
    return [x] + [across(x, d) for d in range(1, TP)]


def traded(parts):
    return [parts[0]] + [across(parts[d], d) for d in range(1, TP)]


def traded_ranks(x):
    return lax.all_to_all(x, "tp", split_axis=0, concat_axis=0, tiled=True)


def by_spans(
    activations,
    cotangent,
    block_sizes,
    context_back,
    first_gain,
    first_bias,
    w_query,
    w_key,
    w_value,
    w_out,
    second_gain,
    second_bias,
    w_up,
    w_down,
    decay_rate,
    input_map,
    output_map,
    step_size,
    skip_gain,
):
    span, place, row, core = (lax.axis_index(a).astype(jnp.int32) for a in ("span", "tp", "y", "core"))
    activations, cotangent, width = activations[0], cotangent[0], block_sizes[0]
    model = activations.shape[1]
    rows = TP * TOKENS
    subs = rows // BLK_A
    ctx_rows = subs * CTX
    mine = 2 * LANES
    half = model // 2
    scal = jnp.stack([span, place, row, core, (width > BLK_A).astype(jnp.int32)])
    tile = lambda n, m, kind=bf16: ((n, m), kind)
    block, piece = tile(TOKENS, model), tile(TOKENS, mine)

    vec = jnp.stack([first_gain, first_bias, second_gain, second_bias])
    vec = lax.all_to_all(jnp.broadcast_to(vec, (2 * TP,) + vec.shape), ("span", "tp"), split_axis=0, concat_axis=0, tiled=True)
    ssm = jnp.concatenate([decay_rate.T, input_map.T, output_map.T, step_size[None], skip_gain[None]])
    ssm_far = swap(ssm, "span")

    def starts_of(which):
        begin = which * rows + jnp.arange(subs, dtype=jnp.int32) * BLK_A
        return begin // width * width

    own_spots = ((starts_of(span) - span * rows)[:, None] - context_back[None, :]).reshape(ctx_rows, 1)
    next_spots = ((starts_of(span + 1) - span * rows)[:, None] - context_back[None, :]).reshape(ctx_rows, 1)
    valid = (starts_of(span)[:, None] >= context_back[None, :]).astype(f32)

    qkv_part, up_part, out_part = call(
        share_kernel,
        [((TP, TOKENS, 3 * LANES), bf16), ((TP, TOKENS, 2 * UNITS), bf16), tile(64, model)],
        *(scal, w_query, w_key, w_value, w_up, w_out),
        scratch=[pltpu.SemaphoreType.DMA((TP * 5 + 1,))],
        loose=range(1, 6),
    )
    qkv_part = traded_ranks(qkv_part)
    qkv_far = swap(qkv_part, "span")
    qkv_parts = [qkv_part, qkv_far, swap(qkv_part, "core"), swap(qkv_far, "core")]
    out_far = swap(out_part, "span")
    out_parts = [w_out, out_far, swap(out_far, "core")]
    up_part = traded_ranks(up_part)

    (low,) = call(norm_one_kernel, [block], scal, activations, vec, scratch=[pltpu.VMEM((TOKENS, model), f32)])
    lowered = gathered(low)
    hold, channels = pltpu.VMEM((STATES, CHUNKS, LANES), f32), pltpu.VMEM((2, rows, LANES), f32)
    channel_out = ((2, rows, LANES), f32)
    low_channels = pltpu.VMEM((rows, mine), bf16)
    cost = dict(flops=rows * mine * STATES * 8, moved=rows * mine * 8)
    local, to_next, ends, decay, mix = call(
        scan_kernel,
        [channel_out, tile(ctx_rows, mine), tile(2 * STATES, mine, f32), tile(STATES, mine, f32), tile(STATES, mine, f32)],
        *(scal, *lowered, ssm, ssm_far, next_spots),
        scratch=[channels, low_channels, hold, hold, hold],
        **cost,
    )
    forward = [(0, 1)]
    begin, from_last = lax.ppermute(ends, "span", forward), lax.ppermute(to_next, "span", forward)
    context, up_part, down_part = call(
        carry_kernel,
        [tile(ctx_rows, mine), ((TP, TOKENS, 2 * UNITS), bf16), block],
        *(scal, local, decay, mix, begin, from_last, own_spots, up_part, w_down),
        scratch=[hold, channels, low_channels, pltpu.SemaphoreType.DMA],
        loose=(8,),
        **cost,
    )
    context = gathered(context)
    cot_parts = gathered(cotangent)
    qkv_w, qkv = call(qkv_kernel, [tile(model, 3 * mine), tile(rows, 3 * mine)], scal, *lowered, *qkv_parts, flops=2 * rows * model * 3 * mine)

    down_far = swap(down_part, "span")
    up_far = swap(up_part, "span")
    down_beside = swap(down_far, "y")
    down_parts = [down_far, down_beside, swap(down_far, "core"), swap(down_beside, "core")]
    up_parts = [up_part, up_far, swap(up_part, "core"), swap(up_far, "core")]

    pairs = rows * (CTX + rows) * mine
    mixed, ctx_kv, out_w, *branch = call(
        attend_kernel,
        [tile(rows, mine), tile(ctx_rows, 2 * mine), tile(mine, model)] + [block] * TP,
        *(scal, valid, qkv, *context, qkv_w, *out_parts),
        flops=4 * pairs,
        moved=rows * mine * 8,
    )
    wide_scratch = pltpu.VMEM((TOKENS, model), f32)
    first_sum, low = call(norm_two_kernel, [tile(TOKENS, model, f32), block], scal, activations, *traded(branch), vec, scratch=[wide_scratch])

    square = tile(model, model)
    up_w, down_w, ahead, cot_span = call(
        units_kernel, [square, square, tile(rows, model, f32), tile(rows, model)], scal, *cot_parts, *up_parts, w_down, *down_parts
    )
    normal = gathered(low)
    side = tile(rows, half)
    *grad_norm, h0, h1, p0, p1, normal_span = call(
        hidden_kernel,
        [block] * TP + [side] * 4 + [tile(rows, model)],
        *(scal, *normal, up_w, ahead),
        scratch=[pltpu.VMEM((rows, model), bf16)],
        flops=4 * rows * model * model,
    )
    down_send, down_keep, up_send, up_keep = call(
        units_weights_kernel,
        [tile(half, model), tile(half, model), tile(model, half), tile(model, half)],
        *(scal, normal_span, cot_span, h0, h1, p0, p1),
        flops=4 * rows * model * model,
    )
    quarter = tile(half // 2, model)
    d_send, d_keep, u_send, u_keep = call(
        units_one_kernel,
        [quarter, quarter, tile(half, half), tile(half, half)],
        *(scal, down_keep, swap(down_send, "core"), up_keep, swap(up_send, "core")),
    )
    grad_first, low, lines_two = call(
        norm_two_back_kernel,
        [tile(TOKENS, model, f32), block, tile(8, model, f32)],
        *(scal, first_sum, *traded(grad_norm), cotangent, vec),
        scratch=[wide_scratch],
        after=(d_send,),
    )
    branch_back = gathered(low)

    grad_qkv, grad_ctx, *back = call(
        attend_back_kernel,
        [tile(rows, 3 * mine), tile(ctx_rows, 2 * mine)] + [tile(ctx_rows, mine)] * TP,
        *(scal, valid, qkv, ctx_kv, *branch_back, out_w, qkv_w),
        scratch=[pltpu.VMEM((rows, mine), bf16), pltpu.VMEM((rows, 2 * mine), f32)],
        flops=10 * pairs,
        moved=rows * mine * 16,
    )
    grad_context, turned = call(context_sum_kernel, [tile(ctx_rows, mine)] * 2, scal, *traded(back))
    from_next = lax.ppermute(turned, "span", [(1, 0)])
    d_send, d_keep, u_send, u_keep = call(
        units_two_kernel,
        [block, block, tile(half, mine), tile(half, mine)],
        *(scal, d_keep, swap(d_send, "y"), u_keep, swap(u_send, "span")),
        after=(grad_ctx,),
    )
    q_send, q_keep, o_send, o_keep = call(
        attend_weights_kernel,
        [tile(model, 3 * LANES)] * 2 + [tile(LANES, model)] * 2,
        *(scal, *lowered, *context, grad_qkv, grad_ctx, mixed, *branch_back),
        scratch=[pltpu.VMEM((rows, model), bf16), pltpu.VMEM((model, 3 * mine), f32)],
        flops=2 * rows * model * 4 * mine,
    )
    q_send, q_keep, o_send, o_keep = call(
        heads_one_kernel,
        [tile(half, 3 * LANES)] * 2 + [tile(64, model)] * 2,
        *(scal, q_keep, swap(q_send, "core"), o_keep, swap(o_send, "core")),
    )
    grad_lowered = [dot(grad_qkv[j * TOKENS : (j + 1) * TOKENS], qkv_w, 1, 1).astype(bf16) for j in range(TP)]
    grad_lowered = traded(grad_lowered)
    result_parts = call(result_kernel, [block] * TP, scal, h0, h1, down_w, after=(grad_ctx,), flops=2 * rows * model * model)
    result_parts = traded(result_parts)

    grad_states, grad_local, grad_ends = call(
        scan_back_kernel,
        [channel_out, channel_out, tile(STATES, mine, f32)],
        *(scal, grad_context, from_next, own_spots, next_spots, ssm, ssm_far, decay, mix),
        scratch=[hold, hold],
        after=(d_send, q_send),
        **cost,
    )
    grad_begin = lax.ppermute(grad_ends, "span", [(1, 0)])
    grad_low, *u_parts = call(
        units_three_kernel,
        [block] + [piece] * TP,
        *(scal, d_keep, swap(d_send, "span"), u_keep, swap(u_send, "y")),
        after=(grad_ends,),
    )
    grad_conv = call(
        carry_back_kernel,
        [piece] * TP,
        *(scal, grad_local, decay, mix, grad_begin),
        scratch=[hold, channels],
        after=(grad_low,),
        **cost,
    )
    grad_conv = traded(grad_conv)
    q_send, q_keep, o_send, o_keep = call(
        heads_two_kernel,
        [tile(UNITS, 3 * LANES)] * 2 + [tile(32, model)] * 2,
        *(scal, q_keep, swap(q_send, "y"), o_keep, swap(o_send, "y")),
        after=(grad_conv[0],),
    )
    (sums,) = call(
        sums_kernel,
        [tile(40, mine, f32)],
        *(scal, *lowered, grad_states, decay, begin),
        scratch=[channels] + [pltpu.VMEM((8, CHUNKS, LANES), f32)] * 4,
        after=(q_send,),
        **cost,
    )
    (u_all,) = call(units_four_kernel, [tile(2 * LANES, model)], scal, grad_low, *traded(u_parts), after=(sums,))
    u_beside = swap(u_all, "y")
    result = first_sum + sum(x.astype(f32) for x in result_parts)
    grad_inputs, lines = call(
        last_kernel,
        [tile(TOKENS, model, f32), ((2 * TP, 8, LANES), f32)],
        *(scal, activations, vec, grad_first, *grad_lowered, *grad_conv, lines_two),
        scratch=[wide_scratch] * 2,
        after=(u_all,),
    )
    o_low, *q_parts = call(
        heads_three_kernel,
        [tile(32, model)] + [tile(64, 3 * LANES)] * TP,
        *(scal, q_keep, swap(q_send, "span"), o_keep, swap(o_send, "span")),
        after=(lines,),
    )
    (q_all,) = call(heads_four_kernel, [tile(64, 2 * model)], scal, o_low, *traded(q_parts))
    q_beside = swap(q_all, "y")
    grad_up, grad_down = call(
        units_home_kernel,
        [tile(LANES, 4 * model, f32), tile(half, model, f32)],
        *(scal, u_all, u_beside, swap(u_all, "core"), swap(u_beside, "core")),
    )
    home = tile(LANES, model, f32)
    grad_query, grad_key, grad_value, grad_out = call(
        heads_home_kernel, [home] * 4, scal, q_all, q_beside, swap(q_all, "core"), swap(q_beside, "core")
    )

    lines = lax.all_to_all(lines, ("span", "tp"), split_axis=0, concat_axis=0, tiled=True)
    lines = jnp.sum(lines, axis=0)
    sums = sums[:, :LANES] + swap(sums[:, LANES:], "span")
    small = jnp.concatenate([lines, sums])
    small = small + swap(small, "y")
    small = small + swap(small, "core")
    lines, sums = small[:8], small[8:]
    grad_mix, grad_skip = sums[:STATES].T, sums[2 * STATES]
    step = step_size[:, None]
    grad_speed = -(output_map * input_map * step) * sums[STATES : 2 * STATES].T
    grad_step = jnp.sum(grad_mix * output_map * input_map + grad_speed * decay_rate, axis=1)
    return (
        result[None],
        grad_inputs[None],
        lines[0],
        lines[1],
        grad_query,
        grad_key,
        grad_value,
        grad_out,
        lines[2],
        lines[3],
        grad_up,
        grad_down,
        grad_speed * step,
        grad_mix * output_map * step,
        grad_mix * input_map * step,
        grad_step,
        grad_skip,
    )


def from_behind(x, axis, by):
    peers = lax.axis_size(axis)
    pairs = [(i, i + by) for i in range(peers) if 0 <= i + by < peers]
    return lax.ppermute(x, axis, pairs)


def smooth_gate(values):
    return jax.nn.gelu(values, approximate=True)


def ssm_kernel(decay_rate, input_map, output_map, step_size, length):
    offsets = jnp.arange(length).astype(jnp.float32)
    weight = output_map * input_map * step_size[:, None]
    decay_speed = step_size[:, None] * decay_rate
    total_sum = jnp.zeros((decay_rate.shape[0], length), jnp.float32)
    for state_index in range(decay_rate.shape[1]):
        total_sum = total_sum + weight[:, state_index : state_index + 1] * jnp.exp(
            -decay_speed[:, state_index : state_index + 1] * offsets[None, :]
        )
    return total_sum


def phase_table(row_count, col_count, period):
    first_ids = jnp.arange(row_count, dtype=jnp.int32)[:, None]
    second_ids = jnp.arange(col_count, dtype=jnp.int32)[None, :]
    angles = (first_ids * second_ids % period).astype(jnp.float32) * (2.0 * math.pi / period)
    return (jnp.cos(angles), jnp.sin(angles))


def exact_einsum(form, left_side, right_side):
    return jnp.einsum(form, left_side, right_side, precision=lax.Precision.HIGHEST)


def spectrum(signal, low_len, high_len):
    row_count = signal.shape[0]
    total_len = low_len * high_len
    grid_rows = signal.reshape(row_count, high_len, low_len)
    cos_high, sin_high = phase_table(high_len, high_len, high_len)
    real_part = exact_einsum("rmn,mk->rkn", grid_rows, cos_high)
    imag_part = -exact_einsum("rmn,mk->rkn", grid_rows, sin_high)
    cos_twist, sin_twist = phase_table(high_len, low_len, total_len)
    real_part, imag_part = (
        real_part * cos_twist + imag_part * sin_twist,
        imag_part * cos_twist - real_part * sin_twist,
    )
    cos_low, sin_low = phase_table(low_len, low_len, low_len)
    out_real = exact_einsum("rkn,nj->rkj", real_part, cos_low) + exact_einsum(
        "rkn,nj->rkj", imag_part, sin_low
    )
    out_imag = exact_einsum("rkn,nj->rkj", imag_part, cos_low) - exact_einsum(
        "rkn,nj->rkj", real_part, sin_low
    )
    return (out_real, out_imag)


def signal_of(real_part, imag_part, low_len, high_len, keep_len):
    row_count = real_part.shape[0]
    total_len = low_len * high_len
    cos_low, sin_low = phase_table(low_len, low_len, low_len)
    mid_real = exact_einsum("rkj,nj->rkn", real_part, cos_low) - exact_einsum(
        "rkj,nj->rkn", imag_part, sin_low
    )
    mid_imag = exact_einsum("rkj,nj->rkn", real_part, sin_low) + exact_einsum(
        "rkj,nj->rkn", imag_part, cos_low
    )
    cos_twist, sin_twist = phase_table(high_len, low_len, total_len)
    turn_real = mid_real * cos_twist - mid_imag * sin_twist
    turn_imag = mid_real * sin_twist + mid_imag * cos_twist
    cos_high, sin_high = phase_table(high_len, high_len, high_len)
    grid_rows = exact_einsum("rkn,km->rmn", turn_real, cos_high) - exact_einsum(
        "rkn,km->rmn", turn_imag, sin_high
    )
    return grid_rows.reshape(row_count, total_len)[:, :keep_len] / total_len


def padded(values):
    return jnp.concatenate([values, jnp.zeros_like(values)], axis=-1)


def norm_parts(values):
    center = values - jnp.mean(values, axis=-1, keepdims=True)
    inverse_dev = lax.rsqrt(jnp.mean(center * center, axis=-1, keepdims=True) + 1e-05)
    return (center * inverse_dev, inverse_dev)


def plain_norm_back(grad_values, scaled, inverse_dev, gain_vector):
    weighted = grad_values * gain_vector.astype(jnp.float32)
    return inverse_dev * (
        weighted
        - jnp.mean(weighted, axis=-1, keepdims=True)
        - scaled * jnp.mean(weighted * scaled, axis=-1, keepdims=True)
    )


def matmul(left_side, right_side):
    return jnp.einsum("...i,ij->...j", left_side, right_side, preferred_element_type=jnp.float32)


def matmul_t(left_side, right_side):
    return jnp.einsum("...j,ij->...i", left_side, right_side, preferred_element_type=jnp.float32)


def outer_sum(left_side, right_side):
    return jnp.einsum(
        "ri,rj->ij",
        left_side.reshape(-1, left_side.shape[-1]),
        right_side.reshape(-1, right_side.shape[-1]),
        preferred_element_type=jnp.float32,
    )


def take_rows(rows_table, row_ids):
    return jnp.take(rows_table, row_ids, axis=0)


def plain(
    activations,
    cotangent,
    block_sizes,
    context_back,
    first_gain,
    first_bias,
    w_query,
    w_key,
    w_value,
    w_out,
    second_gain,
    second_bias,
    w_up,
    w_down,
    decay_rate,
    input_map,
    output_map,
    step_size,
    skip_gain,
):
    seq_ways = lax.axis_size("seq")
    place = lax.axis_index("seq")
    seq_count, tokens, model_width = activations.shape
    channels = decay_rate.shape[0]
    length = tokens * seq_ways
    sub_len = min(BLK_A, tokens)
    sub_count = tokens // sub_len
    shift_count = max(BLK_B // tokens - 1, 0)
    head_dim = model_width // HEADS
    score_scale = head_dim ** (-0.5)
    per_dev = sub_count * CTX
    low_len = 2 * seq_ways
    (
        gain_one,
        bias_one,
        query_full,
        key_full,
        value_full,
        out_full,
        gain_two,
        bias_two,
        up_full,
        down_full,
    ) = (
        lax.all_gather(first_gain, "seq", axis=0, tiled=True),
        lax.all_gather(first_bias, "seq", axis=0, tiled=True),
        lax.all_gather(w_query, "seq", axis=0, tiled=True),
        lax.all_gather(w_key, "seq", axis=0, tiled=True),
        lax.all_gather(w_value, "seq", axis=0, tiled=True),
        lax.all_gather(w_out, "seq", axis=0, tiled=True),
        lax.all_gather(second_gain, "seq", axis=0, tiled=True),
        lax.all_gather(second_bias, "seq", axis=0, tiled=True),
        lax.all_gather(w_up, "seq", axis=0, tiled=True),
        lax.all_gather(w_down, "seq", axis=0, tiled=True),
    )
    scaled_one, inverse_one = norm_parts(activations)
    lowered = (scaled_one * gain_one.astype(jnp.float32) + bias_one.astype(jnp.float32)).astype(
        jnp.bfloat16
    )
    by_channel = lax.all_to_all(
        jnp.swapaxes(lowered, 1, 2), "seq", split_axis=1, concat_axis=2, tiled=True
    )
    channel_in = by_channel.astype(jnp.float32)
    kernel, kernel_pull = jax.vjp(
        lambda a, b, c, e: ssm_kernel(a, b, c, e, length),
        decay_rate,
        input_map,
        output_map,
        step_size,
    )
    input_real, input_imag = spectrum(padded(channel_in.reshape(-1, length)), low_len, tokens)
    input_real = input_real.reshape(seq_count, channels, tokens, low_len)
    input_imag = input_imag.reshape(seq_count, channels, tokens, low_len)
    kernel_real, kernel_imag = spectrum(padded(kernel), low_len, tokens)
    conv_real = input_real * kernel_real - input_imag * kernel_imag
    conv_imag = input_real * kernel_imag + input_imag * kernel_real
    convolved = signal_of(
        conv_real.reshape(-1, tokens, low_len),
        conv_imag.reshape(-1, tokens, low_len),
        low_len,
        tokens,
        length,
    )
    states = convolved.reshape(seq_count, channels, length) + skip_gain[None, :, None] * channel_in
    targets = (
        jnp.arange(seq_ways, dtype=jnp.int32)[:, None] * tokens
        + jnp.arange(sub_count, dtype=jnp.int32)[None, :] * sub_len
    )
    sizes_three = block_sizes[:, None, None]
    block_start = targets[None] // sizes_three * sizes_three
    positions = block_start[..., None] - context_back
    valid_all = positions >= 0
    picks = jnp.maximum(positions, 0).reshape(seq_count, -1)
    position_major = jnp.swapaxes(states, 1, 2)
    picked = jax.vmap(take_rows)(position_major, picks)
    picked = jnp.where(valid_all.reshape(seq_count, -1, 1), picked, 0.0).astype(jnp.bfloat16)
    picked = jnp.swapaxes(picked, 1, 2)
    arrived = lax.all_to_all(
        picked.reshape(seq_count, channels, seq_ways, per_dev),
        "seq",
        split_axis=2,
        concat_axis=1,
        tiled=True,
    )
    context = jnp.swapaxes(arrived.reshape(seq_count, model_width, per_dev), 1, 2)
    own_valid = lax.dynamic_index_in_dim(valid_all, place, axis=1, keepdims=False).reshape(
        seq_count, per_dev
    )
    queries = matmul(lowered, query_full).astype(jnp.bfloat16)
    keys_own = matmul(lowered, key_full).astype(jnp.bfloat16)
    values_own = matmul(lowered, value_full).astype(jnp.bfloat16)
    ctx_keys = matmul(context, key_full).astype(jnp.bfloat16)
    ctx_values = matmul(context, value_full).astype(jnp.bfloat16)
    key_parts = [ctx_keys]
    value_parts = [ctx_values]
    key_places = []
    token_ids = jnp.arange(tokens, dtype=jnp.int32)
    for distance in range(shift_count, 0, -1):
        far_keys, far_values = from_behind((keys_own, values_own), "seq", distance)
        key_parts.append(far_keys)
        value_parts.append(far_values)
        key_places.append((place - distance) * tokens + token_ids)
    key_parts.append(keys_own)
    value_parts.append(values_own)
    key_places.append(place * tokens + token_ids)
    all_keys = jnp.concatenate(key_parts, axis=1)
    all_values = jnp.concatenate(value_parts, axis=1)
    key_pos = jnp.concatenate(key_places)
    query_pos = place * tokens + token_ids
    same_block = key_pos[None, None, :] // sizes_three == query_pos[None, :, None] // sizes_three
    causal = key_pos[None, None, :] <= query_pos[None, :, None]
    ctx_allowed = (
        (token_ids // sub_len)[:, None] == (jnp.arange(per_dev, dtype=jnp.int32) // CTX)[None, :]
    )[None] & own_valid[:, None, :]
    allowed = jnp.concatenate([ctx_allowed, same_block & causal], axis=2)

    def split_heads(values):
        return values.reshape(values.shape[0], values.shape[1], HEADS, head_dim)

    def scores_of():
        raw_scores = (
            jnp.einsum(
                "sqhd,skhd->shqk",
                split_heads(queries),
                split_heads(all_keys),
                preferred_element_type=jnp.float32,
            )
            * score_scale
        )
        return jnp.where(allowed[:, None], raw_scores, -1e30)

    scores = scores_of()
    row_top = jnp.max(scores, axis=-1, keepdims=True)
    log_total = row_top + jnp.log(jnp.sum(jnp.exp(scores - row_top), axis=-1, keepdims=True))
    probs_low = jnp.exp(scores - log_total).astype(jnp.bfloat16)
    attended = jnp.einsum(
        "shqk,skhd->sqhd", probs_low, split_heads(all_values), preferred_element_type=jnp.float32
    )
    mixed_out = attended.reshape(seq_count, tokens, model_width).astype(jnp.bfloat16)
    first_sum = activations + matmul(mixed_out, out_full)
    scaled_two, inverse_two = norm_parts(first_sum)
    normal_two = (scaled_two * gain_two.astype(jnp.float32) + bias_two.astype(jnp.float32)).astype(
        jnp.bfloat16
    )
    pre_gate = matmul(normal_two, up_full)
    hidden, gate_pull = jax.vjp(smooth_gate, pre_gate)
    hidden_low = hidden.astype(jnp.bfloat16)
    result = first_sum + matmul(hidden_low, down_full)
    grad_down = outer_sum(hidden_low, cotangent)
    grad_hidden = matmul_t(cotangent, down_full)
    grad_pre = gate_pull(grad_hidden)[0].astype(jnp.bfloat16)
    grad_up = outer_sum(normal_two, grad_pre)
    grad_norm_two = matmul_t(grad_pre, up_full)
    grad_gain_two = jnp.sum(grad_norm_two * scaled_two, axis=(0, 1))
    grad_bias_two = jnp.sum(grad_norm_two, axis=(0, 1))
    grad_first = cotangent.astype(jnp.float32) + plain_norm_back(
        grad_norm_two, scaled_two, inverse_two, gain_two
    )
    grad_branch = grad_first.astype(jnp.bfloat16)
    grad_out = outer_sum(mixed_out, grad_branch)
    grad_mixed = split_heads(matmul_t(grad_branch, out_full).astype(jnp.bfloat16))
    scores = scores_of()
    probabilities = jnp.exp(scores - log_total)
    probs_low = probabilities.astype(jnp.bfloat16)
    grad_probs = jnp.einsum(
        "sqhd,skhd->shqk", grad_mixed, split_heads(all_values), preferred_element_type=jnp.float32
    )
    grad_all_values = jnp.einsum(
        "shqk,sqhd->skhd", probs_low, grad_mixed, preferred_element_type=jnp.float32
    )
    grad_scores = (
        probabilities * (grad_probs - jnp.sum(probabilities * grad_probs, axis=-1, keepdims=True))
    ).astype(jnp.bfloat16)
    grad_queries = (
        jnp.einsum(
            "shqk,skhd->sqhd",
            grad_scores,
            split_heads(all_keys),
            preferred_element_type=jnp.float32,
        )
        * score_scale
    )
    grad_queries = grad_queries.reshape(seq_count, tokens, model_width).astype(jnp.bfloat16)
    grad_all_keys = (
        jnp.einsum(
            "shqk,sqhd->skhd", grad_scores, split_heads(queries), preferred_element_type=jnp.float32
        )
        * score_scale
    )
    grad_all_keys = grad_all_keys.reshape(seq_count, -1, model_width)
    grad_all_values = grad_all_values.reshape(seq_count, -1, model_width)
    grad_ctx_keys = grad_all_keys[:, :per_dev]
    grad_ctx_values = grad_all_values[:, :per_dev]
    grad_keys = grad_all_keys[:, -tokens:]
    grad_values = grad_all_values[:, -tokens:]
    for distance in range(shift_count, 0, -1):
        begin = per_dev + (shift_count - distance) * tokens
        back_keys, back_values = (
            from_behind(
                grad_all_keys[:, begin : begin + tokens].astype(jnp.bfloat16), "seq", -distance
            ).astype(jnp.float32),
            from_behind(
                grad_all_values[:, begin : begin + tokens].astype(jnp.bfloat16), "seq", -distance
            ).astype(jnp.float32),
        )
        grad_keys = grad_keys + back_keys
        grad_values = grad_values + back_values
    grad_keys_low = grad_keys.astype(jnp.bfloat16)
    grad_values_low = grad_values.astype(jnp.bfloat16)
    context_wide = context.astype(jnp.float32)
    grad_query_w = outer_sum(lowered, grad_queries)
    grad_key_w = outer_sum(lowered, grad_keys_low) + outer_sum(context_wide, grad_ctx_keys)
    grad_value_w = outer_sum(lowered, grad_values_low) + outer_sum(context_wide, grad_ctx_values)
    grad_normal_one = (
        matmul_t(grad_queries, query_full)
        + matmul_t(grad_keys_low, key_full)
        + matmul_t(grad_values_low, value_full)
    )
    grad_context = matmul_t(grad_ctx_keys, key_full) + matmul_t(grad_ctx_values, value_full)
    sent_back = jnp.swapaxes(grad_context, 1, 2).reshape(seq_count, model_width, 1, per_dev)
    returned = lax.all_to_all(
        sent_back.astype(jnp.bfloat16), "seq", split_axis=1, concat_axis=2, tiled=True
    ).astype(sent_back.dtype)
    returned = jnp.where(
        valid_all.reshape(seq_count, 1, -1), returned.reshape(seq_count, channels, -1), 0.0
    )
    segment_ids = (jnp.arange(seq_count, dtype=jnp.int32)[:, None] * length + picks).reshape(-1)
    flat_rows = jnp.swapaxes(returned, 1, 2).reshape(-1, channels)
    grad_states = jax.ops.segment_sum(flat_rows, segment_ids, num_segments=seq_count * length)
    grad_states = jnp.swapaxes(grad_states.reshape(seq_count, length, channels), 1, 2)
    grad_real, grad_imag = spectrum(padded(grad_states.reshape(-1, length)), low_len, tokens)
    grad_real = grad_real.reshape(seq_count, channels, tokens, low_len)
    grad_imag = grad_imag.reshape(seq_count, channels, tokens, low_len)
    back_real = grad_real * kernel_real + grad_imag * kernel_imag
    back_imag = grad_imag * kernel_real - grad_real * kernel_imag
    grad_conv = signal_of(
        back_real.reshape(-1, tokens, low_len),
        back_imag.reshape(-1, tokens, low_len),
        low_len,
        tokens,
        length,
    )
    grad_conv = grad_conv.reshape(seq_count, channels, length)
    corr_real = jnp.sum(grad_real * input_real + grad_imag * input_imag, axis=0)
    corr_imag = jnp.sum(grad_imag * input_real - grad_real * input_imag, axis=0)
    grad_kernel = signal_of(corr_real, corr_imag, low_len, tokens, length)
    grad_rate, grad_in_map, grad_out_map, grad_step = kernel_pull(grad_kernel)
    grad_skip = jnp.sum(grad_states * channel_in, axis=(0, 2))
    grad_channel = grad_conv + skip_gain[None, :, None] * grad_states
    back_tokens = lax.all_to_all(
        grad_channel.astype(jnp.bfloat16), "seq", split_axis=2, concat_axis=1, tiled=True
    ).astype(grad_channel.dtype)
    grad_normal_one = grad_normal_one + jnp.swapaxes(back_tokens, 1, 2)
    grad_gain_one = jnp.sum(grad_normal_one * scaled_one, axis=(0, 1))
    grad_bias_one = jnp.sum(grad_normal_one, axis=(0, 1))
    grad_inputs = grad_first + plain_norm_back(grad_normal_one, scaled_one, inverse_one, gain_one)
    shares = (
        lax.psum_scatter(
            grad_gain_one.astype(jnp.bfloat16), "seq", scatter_dimension=0, tiled=True
        ).astype(jnp.float32),
        lax.psum_scatter(
            grad_bias_one.astype(jnp.bfloat16), "seq", scatter_dimension=0, tiled=True
        ).astype(jnp.float32),
        lax.psum_scatter(
            grad_query_w.astype(jnp.bfloat16), "seq", scatter_dimension=0, tiled=True
        ).astype(jnp.float32),
        lax.psum_scatter(
            grad_key_w.astype(jnp.bfloat16), "seq", scatter_dimension=0, tiled=True
        ).astype(jnp.float32),
        lax.psum_scatter(
            grad_value_w.astype(jnp.bfloat16), "seq", scatter_dimension=0, tiled=True
        ).astype(jnp.float32),
        lax.psum_scatter(
            grad_out.astype(jnp.bfloat16), "seq", scatter_dimension=0, tiled=True
        ).astype(jnp.float32),
        lax.psum_scatter(
            grad_gain_two.astype(jnp.bfloat16), "seq", scatter_dimension=0, tiled=True
        ).astype(jnp.float32),
        lax.psum_scatter(
            grad_bias_two.astype(jnp.bfloat16), "seq", scatter_dimension=0, tiled=True
        ).astype(jnp.float32),
        lax.psum_scatter(
            grad_up.astype(jnp.bfloat16), "seq", scatter_dimension=0, tiled=True
        ).astype(jnp.float32),
        lax.psum_scatter(
            grad_down.astype(jnp.bfloat16), "seq", scatter_dimension=0, tiled=True
        ).astype(jnp.float32),
    )
    summed = (
        lax.psum(shares[0].astype(jnp.bfloat16), "dp").astype(jnp.float32),
        lax.psum(shares[1].astype(jnp.bfloat16), "dp").astype(jnp.float32),
        lax.psum(shares[2].astype(jnp.bfloat16), "dp").astype(jnp.float32),
        lax.psum(shares[3].astype(jnp.bfloat16), "dp").astype(jnp.float32),
        lax.psum(shares[4].astype(jnp.bfloat16), "dp").astype(jnp.float32),
        lax.psum(shares[5].astype(jnp.bfloat16), "dp").astype(jnp.float32),
        lax.psum(shares[6].astype(jnp.bfloat16), "dp").astype(jnp.float32),
        lax.psum(shares[7].astype(jnp.bfloat16), "dp").astype(jnp.float32),
        lax.psum(shares[8].astype(jnp.bfloat16), "dp").astype(jnp.float32),
        lax.psum(shares[9].astype(jnp.bfloat16), "dp").astype(jnp.float32),
        lax.psum(grad_rate.astype(jnp.bfloat16), "dp").astype(jnp.float32),
        lax.psum(grad_in_map.astype(jnp.bfloat16), "dp").astype(jnp.float32),
        lax.psum(grad_out_map.astype(jnp.bfloat16), "dp").astype(jnp.float32),
        lax.psum(grad_step.astype(jnp.bfloat16), "dp").astype(jnp.float32),
        lax.psum(grad_skip.astype(jnp.bfloat16), "dp").astype(jnp.float32),
    )
    summed = tuple(summed)
    return (
        result,
        grad_inputs,
        summed[0],
        summed[1],
        summed[2],
        summed[3],
        summed[4],
        summed[5],
        summed[6],
        summed[7],
        summed[8],
        summed[9],
        summed[10],
        summed[11],
        summed[12],
        summed[13],
        summed[14],
    )


def solution(mesh):
    dp_ways, seq_ways = mesh.shape["dp"], mesh.shape["seq"]
    lone, data, flat, cut = P(), P("dp", "seq", None), P("seq"), P("seq", None)
    in_specs = (data, data, P("dp"), lone, flat, flat, cut, cut, cut, cut, flat, flat, cut, cut, cut, cut, cut, flat, flat)
    out_specs = (data, data, flat, flat, cut, cut, cut, cut, flat, flat, cut, cut, cut, cut, cut, flat, flat)

    def run(activations, *others):
        seqs, length, model = activations.shape
        tokens = length // seq_ways
        if (seqs, dp_ways, seq_ways, tokens, model) != (4, 4, 2 * TP, TOKENS, HEADS * LANES):
            return jax.shard_map(plain, mesh=mesh, in_specs=in_specs, out_specs=out_specs, check_vma=False)(activations, *others)
        fine = Mesh(mesh.devices.reshape(2, 2, 2, TP), ("y", "core", "span", "tp"))
        names = {"dp": ("y", "core"), "seq": ("span", "tp")}
        split = lambda specs: tuple(P(*(names.get(a) for a in spec)) for spec in specs)
        whole = jax.shard_map(by_spans, mesh=fine, in_specs=split(in_specs), out_specs=split(out_specs), check_vma=False)
        return whole(activations, *others)

    return run
```

```python
import functools
import math

import jax
import jax.numpy as jnp
from jax import lax
from jax.experimental import pallas as pl
from jax.experimental.pallas import tpu as pltpu
from jax.sharding import Mesh
from jax.sharding import PartitionSpec as P

HEADS = 8
CTX = 128
BLK_A = 256
BLK_B = 512
TP = 4
TOKENS = 128
LANES = 128
UNITS = 256
STATES = 16
CHUNKS = 8
NEG = -1e30
f32 = jnp.float32
bf16 = jnp.bfloat16
LIMIT = 24
SWAP = [(0, 1), (1, 0)]
PER_US = 16000000000
MICROSECONDS = {
    "share_heads_kernel": 1.5,
    "share_units_kernel": 3.0,
    "norm_one_kernel": 0.85,
    "scan_kernel": 4.6,
    "carry_kernel": 2.0,
    "qkv_kernel": 2.3,
    "attend_kernel": 4.0,
    "norm_two_kernel": 1.0,
    "units_kernel": 3.0,
    "hidden_kernel": 5.4,
    "units_weights_kernel": 3.0,
    "units_one_kernel": 1.1,
    "norm_two_back_kernel": 1.2,
    "attend_back_kernel": 4.8,
    "attend_weights_kernel": 2.4,
    "context_sum_kernel": 0.65,
    "heads_one_kernel": 0.8,
    "units_two_kernel": 0.8,
    "result_kernel": 1.8,
    "scan_back_kernel": 4.0,
    "units_three_kernel": 0.7,
    "carry_back_kernel": 1.9,
    "heads_two_kernel": 0.9,
    "sums_kernel": 4.5,
    "units_four_kernel": 0.6,
    "last_kernel": 2.1,
    "heads_three_kernel": 0.6,
    "heads_four_kernel": 0.6,
    "units_home_kernel": 3.0,
    "heads_home_kernel": 2.1,
    "pack_kernel": 0.6,
}


SPAN, PLACE, ROW, CORE, WIDE = range(5)


def call(kernel, outs, *args, scratch=(), loose=(), after=(), limit=LIMIT):
    count = len(args)
    vmem, free = pl.BlockSpec(memory_space=pltpu.VMEM), pl.BlockSpec(memory_space=pl.ANY)
    specs = [pl.BlockSpec(memory_space=pltpu.SMEM)] + [free if i in loose else vmem for i in range(1, count)] + [free] * len(after)

    def inner(*refs):
        kernel(*refs[:count], *refs[count + len(after) :])

    return pl.pallas_call(
        inner,
        out_shape=[jax.ShapeDtypeStruct(shape, kind) for shape, kind in outs],
        in_specs=specs,
        out_specs=[vmem] * len(outs),
        scratch_shapes=list(scratch),
        compiler_params=pltpu.CompilerParams(vmem_limit_bytes=limit * 1024 * 1024),
        cost_estimate=pl.CostEstimate(flops=int(MICROSECONDS[kernel.__name__] * PER_US), bytes_accessed=0, transcendentals=0),
    )(*args, *after)


def part(index, size):
    return pl.ds(pl.multiple_of(index * size, size), size)


def channel_part(scal, s, rank):
    return part((s ^ scal[SPAN]) * TP + rank, LANES)


def dot(a, b, ca, cb):
    return lax.dot_general(a, b, (((ca,), (cb,)), ((), ())), preferred_element_type=f32)


def wide(ref):
    return ref[...].astype(f32)


def send_all(copies, sems):
    copies = [pltpu.make_async_copy(a, b, sems.at[i]) for i, (a, b) in enumerate(copies)]
    for copy in copies:
        copy.start()
    for copy in copies:
        copy.wait()


def share_heads_kernel(scal, wq, wk, wv, out, down, qkv_send, out_send, down_send, sems):
    core = scal[CORE]
    copies = [
        pltpu.make_async_copy(out.at[part(core, 64), :], out_send, sems.at[0]),
        pltpu.make_async_copy(down.at[part(core * 2 + scal[ROW], LANES), :], down_send, sems.at[1]),
    ]
    for copy in copies:
        copy.start()
    for rank in range(TP):
        for m, w in enumerate((wq, wk, wv)):
            value = w[:, part(core * TP + rank, LANES)]
            for s in range(2):
                qkv_send[s * TP + rank, :, pl.ds(m * LANES, LANES)] = value
    for copy in copies:
        copy.wait()


def share_units_kernel(scal, up, up_send, sems):
    copies = []
    for to in range(2 * TP):
        for s in range(2):
            there = (s * TP + to % TP) * 2 + scal[CORE]
            copies.append((up.at[:, part(there, UNITS)], up_send.at[to, :, pl.ds(s * UNITS, UNITS)]))
    send_all(copies, sems)


def pack_kernel(scal, rate, inward, outward, step, skip, out):
    states = rate.shape[1]
    for i, ref in enumerate((rate, inward, outward)):
        out[i * states : (i + 1) * states, :] = ref[...].T
    out[3 * states : 3 * states + 1, :] = step[...]
    out[3 * states + 1 : 3 * states + 2, :] = skip[...]
    out[3 * states + 2 :, :] = jnp.zeros((out.shape[0] - 3 * states - 2, LANES), f32)


def norm_rows(x):
    center = x - jnp.mean(x, axis=1, keepdims=True)
    inverse = lax.rsqrt(jnp.mean(center * center, axis=1, keepdims=True) + 1e-05)
    return center * inverse, inverse


def line_of(vec, which):
    return jnp.concatenate([vec[n].astype(f32)[which : which + 1] for n in range(vec.shape[0])], axis=1)


def norm_one_kernel(scal, x, vec, low):
    scaled, _ = norm_rows(x[...])
    low[...] = (scaled * line_of(vec, 0) + line_of(vec, 1)).astype(bf16)


def sum_of(own, a, b, c):
    return (wide(own) + wide(a)) + (wide(b) + wide(c))


def norm_two_kernel(scal, x, own, a, b, c, vec, total, low):
    first = x[...] + sum_of(own, a, b, c)
    total[...] = first
    scaled, _ = norm_rows(first)
    low[...] = (scaled * line_of(vec, 2) + line_of(vec, 3)).astype(bf16)


def norm_back(grad, scaled, inverse, gain):
    e = grad * gain
    return inverse * (e - jnp.mean(e, axis=1, keepdims=True) - scaled * jnp.mean(e * scaled, axis=1, keepdims=True))


def norm_two_back_kernel(scal, total, own, a, b, c, cot, vec, grad_first, low, lines):
    grad = sum_of(own, a, b, c)
    scaled, inverse = norm_rows(total[...])
    value = cot[...].astype(f32) + norm_back(grad, scaled, inverse, line_of(vec, 2))
    grad_first[...] = value
    low[...] = value.astype(bf16)
    lines[0:1, :] = jnp.sum(grad * scaled, axis=0, keepdims=True)
    lines[1:2, :] = jnp.sum(grad, axis=0, keepdims=True)
    lines[2:8, :] = jnp.zeros((6, lines.shape[1]), f32)


def last_kernel(scal, x, vec, grad_first, own, a, b, c, p0, p1, p2, p3, lines_two, out, lines, grad):
    grad[...] = sum_of(own, a, b, c)
    for j, p in enumerate((p0, p1, p2, p3)):
        for s in range(2):
            lanes = channel_part(scal, s, scal[PLACE] ^ j)
            grad[:, lanes] = grad[:, lanes] + p[:, pl.ds(s * LANES, LANES)].astype(f32)
    scaled, inverse = norm_rows(x[...])
    out[...] = grad_first[...] + norm_back(grad[...], scaled, inverse, line_of(vec, 0))
    gain = jnp.sum(grad[...] * scaled, axis=0, keepdims=True)
    bias = jnp.sum(grad[...], axis=0, keepdims=True)
    for n in range(lines.shape[0]):
        lanes = slice(n * LANES, (n + 1) * LANES)
        lines[n, 0:1, :] = gain[:, lanes]
        lines[n, 1:2, :] = bias[:, lanes]
        lines[n, 2:4, :] = lines_two[0:2, lanes]
        lines[n, 4:8, :] = jnp.zeros((4, LANES), f32)


def spread(row):
    return jnp.broadcast_to(row, (CHUNKS, LANES))


def power(base, times):
    for _ in range(int(math.log2(times))):
        base = base * base
    return base


def total_of(parts):
    while len(parts) > 1:
        parts = [parts[i] + parts[i + 1] for i in range(0, len(parts), 2)]
    return parts[0]


def one_hot(spots, rows):
    return (spots[...] == lax.broadcasted_iota(jnp.int32, (spots.shape[0], rows), 1)).astype(bf16)


def own_channels(scal, xs, parts):
    place = scal[PLACE]
    for j, x in enumerate(parts):
        for s in range(2):
            xs[s, part(place ^ j, TOKENS), :] = x[:, channel_part(scal, s, place)].astype(f32)


def scan(reverse, xs, a_ref, w_ref, skips, y_ref, end, sh, ih, sq=None, kept=None):
    states = a_ref.shape[0]
    steps = xs.shape[1] // CHUNKS

    def at(step):
        return pl.ds(steps - 1 - step if reverse else step, CHUNKS, stride=steps)

    for s in range(xs.shape[0]):
        cols = pl.ds(s * LANES, LANES)
        rate = [spread(a_ref[n : n + 1, cols]) for n in range(states)]
        ih[0] = jnp.zeros((CHUNKS, LANES), f32)
        zero = ih[0]

        def local(step, carry):
            x = xs[s, at(step), :]
            if sq is not None:
                h, q = carry
                q = tuple(a * (u + v) for a, u, v in zip(rate, q, h))
            else:
                (h,) = carry
            h = tuple(a * v + x for a, v in zip(rate, h))
            return (h, q) if sq is not None else (h,)

        done = lax.fori_loop(0, steps, local, ((zero,) * states,) * (1 if sq is None else 2), unroll=4)
        for n in range(states):
            sh[n] = done[0][n]
            if sq is not None:
                sq[n] = done[1][n]
        jump = power(a_ref[:, cols], steps)
        hold = jnp.zeros((states, LANES), f32)
        hold_q = jnp.zeros((states, LANES), f32)
        for k in range(CHUNKS):
            k = CHUNKS - 1 - k if reverse else k
            ih[:, k, :] = hold
            if sq is not None:
                hold_q = jump * (hold_q + float(steps) * hold) + sq[:, k, :]
            hold = jump * hold + sh[:, k, :]
        if kept is not None:
            kept[0, s] = sh[...]
            kept[1, s] = sq[...]
        end(s, hold, hold_q)
        weight = [spread(w_ref[n : n + 1, cols]) for n in range(states)]
        skip = spread(skips[s][49:50, :])

        def emit(step, h):
            x = xs[s, at(step), :]
            h = tuple(a * v + x for a, v in zip(rate, h))
            y_ref[s, at(step), :] = total_of([w * v for w, v in zip(weight, h)]) + skip * x
            return h

        lax.fori_loop(0, steps, emit, tuple(ih[n] for n in range(states)), unroll=4)


def scan_kernel(scal, x0, x1, x2, x3, ssm0, ssm1, spots, y, to_next, ends, decay, mix, kept, xs, low, sh, sq, ih):
    own_channels(scal, xs, (x0, x1, x2, x3))
    n = decay.shape[0]
    for s, ssm in enumerate((ssm0, ssm1)):
        cols = pl.ds(s * LANES, LANES)
        step = ssm[48:49, :]
        decay[:, cols] = jnp.exp(-step * ssm[0:n, :])
        mix[:, cols] = ssm[32:48, :] * ssm[16:32, :] * step

    def end(s, h, q):
        other = pl.ds((1 - s) * LANES, LANES)
        ends[0:n, other] = h
        ends[n : 2 * n, other] = q

    scan(False, xs, decay, mix, (ssm0, ssm1), y, end, sh, ih, sq, kept)
    for s in range(2):
        low[:, pl.ds((1 - s) * LANES, LANES)] = y[s].astype(bf16)
    to_next[...] = dot(one_hot(spots, low.shape[0]), low[...], 1, 0).astype(bf16)


def carry(reverse, y_ref, a_ref, w_ref, h_ref, out, ih):
    states = a_ref.shape[0]
    steps = y_ref.shape[1] // CHUNKS

    def at(step):
        return pl.ds(steps - 1 - step if reverse else step, CHUNKS, stride=steps)

    for s in range(y_ref.shape[0]):
        cols = pl.ds(s * LANES, LANES)
        rate = [spread(a_ref[n : n + 1, cols]) for n in range(states)]
        jump = power(a_ref[:, cols], steps)
        hold = w_ref[:, cols] * h_ref[0:states, cols]
        for k in range(CHUNKS):
            ih[:, CHUNKS - 1 - k if reverse else k, :] = hold
            hold = jump * hold

        def emit(step, h):
            h = tuple(a * v for a, v in zip(rate, h))
            out[s, at(step), :] = y_ref[s, at(step), :] + total_of(list(h))
            return h

        lax.fori_loop(0, steps, emit, tuple(ih[n] for n in range(states)), unroll=4)


def carry_kernel(scal, y, decay, mix, begin, from_last, spots, context, ih, ys, low):
    carry(False, y, decay, mix, begin, ys, ih)
    for s in range(2):
        low[:, pl.ds(s * LANES, LANES)] = ys[s].astype(bf16)
    context[...] = (dot(one_hot(spots, low.shape[0]), low[...], 1, 0) + wide(from_last)).astype(bf16)


def scan_back_kernel(scal, own, from_next, own_spots, next_spots, ssm0, ssm1, decay, mix, grad, y, ends, sh, ih):
    rows = y.shape[1]
    value = dot(one_hot(own_spots, rows), own[...], 0, 0) + dot(one_hot(next_spots, rows), from_next[...], 0, 0)
    for s in range(2):
        grad[s] = value[:, s * LANES : (s + 1) * LANES]

    def end(s, h, q):
        ends[:, pl.ds((1 - s) * LANES, LANES)] = h

    scan(True, grad, decay, mix, (ssm0, ssm1), y, end, sh, ih)


def carry_back_kernel(scal, y, decay, mix, begin, o0, o1, o2, o3, ih, ys):
    carry(True, y, decay, mix, begin, ys, ih)
    for j, out in enumerate((o0, o1, o2, o3)):
        for s in range(2):
            out[:, pl.ds(s * LANES, LANES)] = ys[s, part(scal[PLACE] ^ j, TOKENS), :].astype(bf16)


def sums_kernel(scal, x0, x1, x2, x3, gs, a_ref, begin, kept, out, xs, ih, iq):
    own_channels(scal, xs, (x0, x1, x2, x3))
    states = a_ref.shape[0]
    steps = xs.shape[1] // CHUNKS
    group = 8
    out[2 * states :, :] = jnp.zeros((out.shape[0] - 2 * states, out.shape[1]), f32)
    for s in range(xs.shape[0]):
        cols = pl.ds(s * LANES, LANES)
        jump = power(a_ref[:, cols], steps)
        hold, hold_q = begin[0:states, cols], begin[states : 2 * states, cols]
        for k in range(CHUNKS):
            ih[:, k, :] = hold
            iq[:, k, :] = hold_q
            hold_q = jump * (hold_q + float(steps) * hold) + kept[1, s, :, k, :]
            hold = jump * hold + kept[0, s, :, k, :]
        for base in range(0, states, group):
            rate = [spread(a_ref[n : n + 1, cols]) for n in range(base, base + group)]

            def gain(step, carried):
                h, q, sw, sq = carried
                at = pl.ds(step, CHUNKS, stride=steps)
                x, g = xs[s, at, :], gs[s, at, :]
                q = tuple(a * (u + v) for a, u, v in zip(rate, q, h))
                h = tuple(a * v + x for a, v in zip(rate, h))
                sw = tuple(u + g * v for u, v in zip(sw, h))
                sq = tuple(u + g * v for u, v in zip(sq, q))
                return h, q, sw, sq

            first = tuple(ih[base + n] for n in range(group)), tuple(iq[base + n] for n in range(group))
            none = tuple(v * 0.0 for v in first[0])
            _, _, sw, sq = lax.fori_loop(0, steps, gain, first + (none, none), unroll=2)
            for n in range(group):
                out[base + n : base + n + 1, cols] = jnp.sum(sw[n], axis=0, keepdims=True)
                out[states + base + n : states + base + n + 1, cols] = jnp.sum(sq[n], axis=0, keepdims=True)
        out[2 * states : 2 * states + 1, cols] = jnp.sum(xs[s] * gs[s], axis=0, keepdims=True)


def qkv_kernel(scal, x0, x1, x2, x3, w0, w1, w, qkv):
    for j, ref in enumerate((w0, w1)):
        for n in range(2 * TP):
            for m in range(3):
                w[pl.ds(n * LANES, LANES), pl.ds((2 * m + j) * LANES, LANES)] = ref[n, :, pl.ds(m * LANES, LANES)]
    for j, x in enumerate((x0, x1, x2, x3)):
        qkv[part(scal[PLACE] ^ j, TOKENS), :] = dot(x[...], w[...], 1, 0).astype(bf16)


def masks(size, is_wide, ok_ref, sub):
    rows = lax.broadcasted_iota(jnp.int32, (size, size), 0)
    cols = lax.broadcasted_iota(jnp.int32, (size, size), 1)
    return ok_ref[sub : sub + 1, :] > 0.0, is_wide > 0, cols <= rows


def out_of_order(out_ref, lanes, value, sub, place):
    each = value.shape[0] // TOKENS
    for i in range(each):
        out_ref[part((sub * each + i) ^ place, TOKENS), lanes] = value[i * TOKENS : (i + 1) * TOKENS]


def probabilities(q, ctx_k, k_ref, size, sub, lanes, mask, scale):
    context, earlier, own = mask
    parts = [jnp.where(context, dot(q, ctx_k, 1, 1) * scale, NEG)]
    for other in range(sub):
        keys = k_ref[pl.ds(other * size, size), lanes]
        parts.append(jnp.where(earlier, dot(q, keys, 1, 1) * scale, NEG))
    parts.append(jnp.where(own, dot(q, k_ref[pl.ds(sub * size, size), lanes], 1, 1) * scale, NEG))
    top = functools.reduce(jnp.maximum, [jnp.max(s, axis=1, keepdims=True) for s in parts])
    parts = [jnp.exp(s - top) for s in parts]
    inverse = 1.0 / sum(jnp.sum(s, axis=1, keepdims=True) for s in parts)
    return [s * inverse for s in parts]


def attend_kernel(scal, ok, qkv, c0, c1, c2, c3, w, out_own, out_0, out_1, mixed, ckv, out_w, b0, b1, b2, b3):
    place, core = scal[PLACE], scal[CORE]
    width = qkv.shape[1] // 3
    dim = LANES
    own = core ^ scal[SPAN]
    out_w[part(own, dim), :] = out_own[...]
    out_w[part((1 - own) * 2 + core, 64), :] = out_0[...]
    out_w[part((1 - own) * 2 + 1 - core, 64), :] = out_1[...]
    total = None
    for j, c in enumerate((c0, c1, c2, c3)):
        for s in range(2):
            term = dot(c[:, pl.ds(s * LANES, LANES)], w[channel_part(scal, s, place ^ j), pl.ds(width, 2 * width)], 1, 0)
            total = term if total is None else total + term
    ckv[...] = total.astype(bf16)
    subs = ok.shape[0]
    size = qkv.shape[0] // subs
    scale = dim ** (-0.5)
    for sub in range(subs):
        mask = masks(size, scal[WIDE], ok, sub)
        here = pl.ds(sub * size, size)
        for h in range(width // dim):
            lq, lk, lv = (pl.ds(i * width + h * dim, dim) for i in range(3))
            ck = ckv[pl.ds(sub * CTX, CTX), pl.ds(h * dim, dim)]
            cv = ckv[pl.ds(sub * CTX, CTX), pl.ds(width + h * dim, dim)]
            probs = probabilities(qkv[here, lq], ck, qkv, size, sub, lk, mask, scale)
            value = dot(probs[0].astype(bf16), cv, 1, 0)
            for other in range(sub + 1):
                value += dot(probs[1 + other].astype(bf16), qkv[pl.ds(other * size, size), lv], 1, 0)
            out_of_order(mixed, pl.ds(h * dim, dim), value.astype(bf16), sub, place)
    for j, b in enumerate((b0, b1, b2, b3)):
        b[...] = dot(mixed[pl.ds(j * TOKENS, TOKENS), :], out_w[...], 1, 0).astype(bf16)


def attend_back_kernel(scal, ok, qkv, ckv, g0, g1, g2, g3, out_w, w, out, ctx, x0, x1, x2, x3, gms, acc):
    place = scal[PLACE]
    width = qkv.shape[1] // 3
    dim = LANES
    subs = ok.shape[0]
    size = qkv.shape[0] // subs
    scale = dim ** (-0.5)
    for j, g in enumerate((g0, g1, g2, g3)):
        gms[part(place ^ j, TOKENS), :] = dot(g[...], out_w[...], 1, 1).astype(bf16)
    acc[...] = jnp.zeros_like(acc)
    for sub in range(subs):
        mask = masks(size, scal[WIDE], ok, sub)
        here = pl.ds(sub * size, size)
        cs = pl.ds(sub * CTX, CTX)
        for h in range(width // dim):
            lq, lk, lv = (pl.ds(i * width + h * dim, dim) for i in range(3))
            lh, lhv = pl.ds(h * dim, dim), pl.ds(width + h * dim, dim)
            ck, cv = ckv[cs, lh], ckv[cs, lhv]
            q, gm = qkv[here, lq], gms[here, lh]
            probs = probabilities(q, ck, qkv, size, sub, lk, mask, scale)
            values = [cv] + [qkv[pl.ds(o * size, size), lv] for o in range(sub + 1)]
            keys = [ck] + [qkv[pl.ds(o * size, size), lk] for o in range(sub + 1)]
            grads = [dot(gm, v, 1, 1) for v in values]
            inner = sum(jnp.sum(p * g, axis=1, keepdims=True) for p, g in zip(probs, grads))
            scores = [(p * (g - inner)).astype(bf16) for p, g in zip(probs, grads)]
            grad_q = sum(dot(s, k, 1, 0) for s, k in zip(scores, keys))
            out_of_order(out, lq, (grad_q * scale).astype(bf16), sub, place)
            ctx[cs, lh] = (dot(scores[0], q, 0, 0) * scale).astype(bf16)
            ctx[cs, lhv] = dot(probs[0].astype(bf16), gm, 0, 0).astype(bf16)
            for o in range(sub + 1):
                there = pl.ds(o * size, size)
                acc[there, lh] += dot(scores[1 + o], q, 0, 0) * scale
                acc[there, lhv] += dot(probs[1 + o].astype(bf16), gm, 0, 0)
    for sub in range(subs):
        out_of_order(out, pl.ds(width, 2 * width), acc[pl.ds(sub * size, size), :].astype(bf16), sub, place)
    for j, x in enumerate((x0, x1, x2, x3)):
        for s in range(2):
            rows = channel_part(scal, s, place ^ j)
            x[:, pl.ds(s * LANES, LANES)] = dot(ctx[...], w[rows, pl.ds(width, 2 * width)], 1, 1).astype(bf16)


def context_sum_kernel(scal, own, a, b, c, total, turned):
    value = ((wide(own) + wide(a)) + (wide(b) + wide(c))).astype(bf16)
    total[...] = value
    for s in range(2):
        turned[:, pl.ds((1 - s) * LANES, LANES)] = value[:, s * LANES : (s + 1) * LANES]


def attend_weights_kernel(scal, x0, x1, x2, x3, c0, c1, c2, c3, gqkv, gctx, mixed, g0, g1, g2, g3, send, keep, rows, acc, acc_out):
    place, core = scal[PLACE], scal[CORE]
    for j, x in enumerate((x0, x1, x2, x3)):
        rows[pl.ds(j * TOKENS, TOKENS), :] = x[...]
    width = gqkv.shape[1] // 3
    half = rows.shape[1] // 2
    for s in range(2):
        acc[pl.ds(s * half, half), :] = dot(rows[:, pl.ds(s * half, half)], gqkv[...], 0, 0)
    for j, c in enumerate((c0, c1, c2, c3)):
        for s in range(2):
            there = channel_part(scal, s, place ^ j)
            acc[there, pl.ds(width, 2 * width)] += dot(c[:, pl.ds(s * LANES, LANES)], gctx[...], 0, 0)
    size = acc.shape[0]
    for m in range(3):
        keep[pl.ds(m * size, size), :] = acc[:, pl.ds(2 * m * LANES, LANES)].astype(bf16)
        send[pl.ds(m * size, size), :] = acc[:, pl.ds((2 * m + 1) * LANES, LANES)].astype(bf16)
    for j, g in enumerate((g0, g1, g2, g3)):
        rows[pl.ds(j * TOKENS, TOKENS), :] = g[...]
    acc_out[...] = dot(mixed[...], rows[...], 0, 0)
    for s in range(2):
        head = core ^ scal[SPAN] ^ s
        for ref, side in ((keep, core), (send, 1 - core)):
            for i in range(2 * TP):
                there = pl.ds(3 * size + i * LANES + s * 64, 64)
                ref[there, :] = acc_out[part(head * 2 + side, 64), pl.ds(i * LANES, LANES)].astype(bf16)


def units_kernel(scal, c0, c1, c2, c3, u0, u1, own, d00, d01, d10, d11, up_w, down_w, ahead, rows):
    span, core, row = scal[SPAN], scal[CORE], scal[ROW]
    half = up_w.shape[0] // 2
    for j, ref in enumerate((u0, u1)):
        for n in range(2 * TP):
            for s in range(2):
                up_w[pl.ds(n * LANES, LANES), pl.ds(s * half + j * UNITS, UNITS)] = ref[n, :, pl.ds(s * UNITS, UNITS)]
    for j in range(2):
        down_w[part(span * 2 + j, UNITS), :] = own[part(core ^ j, UNITS), :]
    for j, k, ref in ((0, 0, d00), (0, 1, d01), (1, 0, d10), (1, 1, d11)):
        down_w[part(((1 - span) * 2 + j) * 2 + (row ^ k), LANES), :] = ref[...]
    for j, c in enumerate((c0, c1, c2, c3)):
        rows[pl.ds(j * TOKENS, TOKENS), :] = c[...]
    for i in range(4):
        tile = pl.ds(i * UNITS, UNITS)
        ahead[:, tile] = dot(rows[...], down_w[tile, :], 1, 1)


def gelu_parts(a):
    c = math.sqrt(2.0 / math.pi)
    t = jnp.tanh(c * (a + 0.044715 * a * a * a))
    half = 0.5 * (1.0 + t)
    return a * half, half + 0.5 * a * (1.0 - t * t) * c * (1.0 + 3 * 0.044715 * a * a)


def hidden_kernel(scal, n0, n1, n2, n3, up_w, ahead, o0, o1, o2, o3, h0, h1, p0, p1, rows, pre):
    for j, n in enumerate((n0, n1, n2, n3)):
        rows[pl.ds(j * TOKENS, TOKENS), :] = n[...]
    for i in range(4):
        s, j = divmod(i, 2)
        tile, lanes = pl.ds(i * UNITS, UNITS), pl.ds(s * UNITS, UNITS)
        act, slope = gelu_parts(dot(rows[...], up_w[:, tile], 1, 0))
        low = (ahead[:, tile] * slope).astype(bf16)
        (h0, h1)[j][:, lanes] = act.astype(bf16)
        (p0, p1)[j][:, lanes] = low
        pre[:, tile] = low
    for j, out in enumerate((o0, o1, o2, o3)):
        out[...] = dot(pre[pl.ds(j * TOKENS, TOKENS), :], up_w[...], 1, 1).astype(bf16)


def result_kernel(scal, h0, h1, down_w, o0, o1, o2, o3):
    for j, out in enumerate((o0, o1, o2, o3)):
        here = pl.ds(j * TOKENS, TOKENS)
        total = None
        for s in range(2):
            for k, h in enumerate((h0, h1)):
                term = dot(h[here, pl.ds(s * UNITS, UNITS)], down_w[pl.ds((2 * s + k) * UNITS, UNITS), :], 1, 0)
                total = term if total is None else total + term
        out[...] = total.astype(bf16)


def units_weights_kernel(scal, rows, cot, h0, h1, p0, p1, d_send, u_send, d_keep, u_keep):
    half = h0.shape[1]
    for h, p, down, up in ((h1, p1, d_send, u_send), (h0, p0, d_keep, u_keep)):
        for i in range(2):
            tile = pl.ds(i * UNITS, UNITS)
            down[tile, :] = dot(h[:, tile], cot[...], 0, 0).astype(bf16)
        for i in range(4):
            s, n = divmod(i, 2)
            there = (pl.ds(n * UNITS, UNITS), pl.ds(s * half, half))
            up[there] = dot(rows[:, pl.ds(i * UNITS, UNITS)], p[...], 0, 0).astype(bf16)


def units_one_kernel(scal, down, down_got, up, up_got, d_send, d_keep, u_send, u_keep):
    row = scal[ROW]
    half = u_keep.shape[0]
    for s in range(2):
        for ref, side in ((d_keep, row), (d_send, 1 - row)):
            there = part(2 * s + side, LANES)
            ref[pl.ds(s * LANES, LANES), :] = (wide(down.at[there, :]) + wide(down_got.at[there, :])).astype(bf16)
    for ref, side in ((u_keep, scal[SPAN]), (u_send, 1 - scal[SPAN])):
        there = part(side, half)
        ref[...] = (wide(up.at[:, there]) + wide(up_got.at[:, there])).astype(bf16)


def units_two_kernel(scal, down, down_got, up, up_got, d_send, d_keep, u_send, u_keep):
    row = scal[ROW]
    for ref, s in ((d_keep, scal[SPAN]), (d_send, 1 - scal[SPAN])):
        there = part(s, LANES)
        ref[...] = (wide(down.at[there, :]) + wide(down_got.at[there, :])).astype(bf16)
    for s in range(2):
        for ref, side in ((u_keep, row), (u_send, 1 - row)):
            there = part(2 * s + side, LANES)
            ref[:, pl.ds(s * LANES, LANES)] = (wide(up.at[:, there]) + wide(up_got.at[:, there])).astype(bf16)


def units_three_kernel(scal, up, up_got, x0, x1, x2, x3):
    for j, x in enumerate((x0, x1, x2, x3)):
        there = part(scal[PLACE] ^ j, LANES)
        x[...] = (wide(up.at[there, :]) + wide(up_got.at[there, :])).astype(bf16)


def units_four_kernel(scal, down, down_got, x0, x1, x2, x3, out):
    out[0:LANES, :] = (wide(down) + wide(down_got)).astype(bf16)
    for j, x in enumerate((x0, x1, x2, x3)):
        out[LANES : 2 * LANES, part(scal[PLACE] ^ j, UNITS)] = x[...]


def units_home_kernel(scal, b00, b01, b10, b11, up, down):
    row, core = scal[ROW], scal[CORE]
    for j, k, ref in ((0, 0, b00), (0, 1, b01), (1, 0, b10), (1, 1, b11)):
        quarter = (core ^ j) * 2 + (row ^ k)
        down[part(quarter, LANES), :] = ref[0:LANES, :].astype(f32)
        for rank in range(TP):
            for s in range(2):
                there = (s * TP + rank) * 4 + quarter
                up[:, part(there, LANES)] = ref[LANES : 2 * LANES, pl.ds(rank * UNITS + s * LANES, LANES)].astype(f32)


def heads_one_kernel(scal, own, got, send, keep):
    row = scal[ROW]
    for n in range(own.shape[0] // 64 // 2):
        for ref, side in ((keep, row), (send, 1 - row)):
            size = 64 if n < 3 * 2 * TP else 32
            pairs = 1 if size == 64 else 2
            for i in range(pairs):
                at = part((2 * n + side) if pairs == 1 else (4 * n + 2 * i + side), size)
                there = pl.ds(n * 64 + i * 32, size)
                ref[there, :] = (wide(own.at[at, :]) + wide(got.at[at, :])).astype(bf16)


def heads_two_kernel(scal, own, got, send, keep):
    quarter = TP * 64
    for m in range(3):
        for ref, s in ((keep, scal[SPAN]), (send, 1 - scal[SPAN])):
            at = part(2 * m + s, quarter)
            ref[pl.ds(m * quarter, quarter), :] = (wide(own.at[at, :]) + wide(got.at[at, :])).astype(bf16)
    for i in range(2 * TP):
        for ref, s in ((keep, 0), (send, 1)):
            at = pl.ds(6 * quarter + i * 64 + s * 32, 32)
            ref[pl.ds(3 * quarter + i * 32, 32), :] = (wide(own.at[at, :]) + wide(got.at[at, :])).astype(bf16)


def heads_three_kernel(scal, own, got, low, x0, x1, x2, x3):
    quarter = TP * 64
    at = pl.ds(3 * quarter, low.shape[0])
    low[...] = (wide(own.at[at, :]) + wide(got.at[at, :])).astype(bf16)
    for j, x in enumerate((x0, x1, x2, x3)):
        for m in range(3):
            at = part(m * TP + (scal[PLACE] ^ j), 64)
            x[:, pl.ds(m * LANES, LANES)] = (wide(own.at[at, :]) + wide(got.at[at, :])).astype(bf16)


def heads_four_kernel(scal, low, x0, x1, x2, x3, out):
    width = x0.shape[1]
    for j, x in enumerate((x0, x1, x2, x3)):
        out[:, part(scal[PLACE] ^ j, width)] = x[...]
    for i in range(2 * TP):
        there = (pl.ds(i // TP * 32, 32), pl.ds(TP * width + i % TP * LANES, LANES))
        out[there] = low[pl.ds(i * 32, 32), :]


def heads_home_kernel(scal, b00, b01, b10, b11, gq, gk, gv, go):
    row, core = scal[ROW], scal[CORE]
    width = 3 * LANES
    half = go.shape[1] // 2
    for j, k, ref in ((0, 0, b00), (0, 1, b01), (1, 0, b10), (1, 1, b11)):
        for rank in range(TP):
            for m, out in enumerate((gq, gk, gv)):
                lanes = pl.ds(rank * width + m * LANES, LANES)
                out[part(row ^ k, 64), part((core ^ j) * TP + rank, LANES)] = ref[:, lanes].astype(f32)
        there = part((core ^ j) * 2 + (row ^ k), 32)
        for i in range(2):
            go[there, pl.ds(i * half, half)] = ref[pl.ds(i * 32, 32), pl.ds(TP * width, half)].astype(f32)


def swap(x, axis):
    return lax.ppermute(x, axis, SWAP)


def across(x, d):
    return lax.ppermute(x, "tp", [(i, i ^ d) for i in range(TP)])


def gathered(x):
    return [x] + [across(x, d) for d in range(1, TP)]


def traded(parts):
    return [parts[0]] + [across(parts[d], d) for d in range(1, TP)]


def traded_all(x):
    return lax.all_to_all(x, ("span", "tp"), split_axis=0, concat_axis=0, tiled=True)


def hold_until(x, spent, *others):
    x, *others = lax.optimization_barrier((x,) + others)
    spent.extend(others)
    return x


def by_spans(
    activations,
    cotangent,
    block_sizes,
    context_back,
    first_gain,
    first_bias,
    w_query,
    w_key,
    w_value,
    w_out,
    second_gain,
    second_bias,
    w_up,
    w_down,
    decay_rate,
    input_map,
    output_map,
    step_size,
    skip_gain,
):
    span, place, row, core = (lax.axis_index(a).astype(jnp.int32) for a in ("span", "tp", "y", "core"))
    activations, cotangent, width = activations[0], cotangent[0], block_sizes[0]
    model = activations.shape[1]
    rows = TP * TOKENS
    subs = rows // BLK_A
    ctx_rows = subs * CTX
    mine = 2 * LANES
    half = model // 2
    scal = jnp.stack([span, place, row, core, (width > BLK_A).astype(jnp.int32)])
    tile = lambda n, m, kind=bf16: ((n, m), kind)
    block, piece = tile(TOKENS, model), tile(TOKENS, mine)

    vec = jnp.stack([first_gain, first_bias, second_gain, second_bias])
    vec = traded_all(jnp.broadcast_to(vec, (2 * TP,) + vec.shape))
    spent = []

    def starts_of(which):
        begin = which * rows + jnp.arange(subs, dtype=jnp.int32) * BLK_A
        return begin // width * width

    own_spots = ((starts_of(span) - span * rows)[:, None] - context_back[None, :]).reshape(ctx_rows, 1)
    next_spots = ((starts_of(span + 1) - span * rows)[:, None] - context_back[None, :]).reshape(ctx_rows, 1)
    valid = (starts_of(span)[:, None] >= context_back[None, :]).astype(f32)

    (low,) = call(norm_one_kernel, [block], scal, activations, vec)
    lowered = gathered(low)
    (ssm,) = call(
        pack_kernel, [tile(56, LANES, f32)], scal, decay_rate, input_map, output_map, step_size[None], skip_gain[None], after=(low,)
    )
    ssm_far = swap(ssm, "span")
    qkv_part, out_part, down_part = call(
        share_heads_kernel,
        [((2 * TP, TOKENS, 3 * LANES), bf16), tile(64, model), block],
        *(scal, w_query, w_key, w_value, w_out, w_down),
        scratch=[pltpu.SemaphoreType.DMA((2,))],
        loose=(4, 5),
        after=(low,),
    )
    down_far, out_far = swap(down_part, "span"), swap(out_part, "span")
    down_beside = swap(down_far, "y")
    hold, channels = pltpu.VMEM((STATES, CHUNKS, LANES), f32), pltpu.VMEM((2, rows, LANES), f32)
    channel_out, kept = ((2, rows, LANES), f32), ((2, 2, STATES, CHUNKS, LANES), f32)
    low_channels = pltpu.VMEM((rows, mine), bf16)
    local, to_next, ends, decay, mix, kept = call(
        scan_kernel,
        [channel_out, tile(ctx_rows, mine), tile(2 * STATES, mine, f32), tile(STATES, mine, f32), tile(STATES, mine, f32), kept],
        *(scal, *lowered, ssm, ssm_far, next_spots),
        after=(down_far,),
        scratch=[channels, low_channels, hold, hold, hold],
    )
    forward = [(0, 1)]
    begin, from_last = lax.ppermute(ends, "span", forward), lax.ppermute(to_next, "span", forward)
    cot_parts = gathered(hold_until(cotangent, spent, ends))
    qkv_part = traded_all(hold_until(qkv_part, spent, ends))
    (context,) = call(
        carry_kernel,
        [tile(ctx_rows, mine)],
        *(scal, local, decay, mix, begin, from_last, own_spots),
        after=(out_far, down_beside),
        scratch=[hold, channels, low_channels],
    )
    context = gathered(context)
    out_parts = [w_out, out_far, swap(hold_until(out_far, spent, context[1]), "core")]
    qkv_beside = swap(hold_until(qkv_part, spent, *context[1:]), "core")
    down_parts = [down_far, down_beside]
    qkv_w, qkv = call(qkv_kernel, [tile(model, 3 * mine), tile(rows, 3 * mine)], scal, *lowered, qkv_part, qkv_beside)

    (up_part,) = call(
        share_units_kernel,
        [((2 * TP, TOKENS, 2 * UNITS), bf16)],
        *(scal, w_up),
        scratch=[pltpu.SemaphoreType.DMA((4 * TP,))],
        loose=(1,),
        after=(qkv,),
        limit=60,
    )
    up_part = traded_all(up_part)
    down_parts += [swap(hold_until(d, spent, qkv), "core") for d in down_parts]

    mixed, ctx_kv, out_w, *branch = call(
        attend_kernel,
        [tile(rows, mine), tile(ctx_rows, 2 * mine), tile(mine, model)] + [block] * TP,
        *(scal, valid, qkv, *context, qkv_w, *out_parts),
        after=tuple(cot_parts[1:]),
    )
    first_sum, low = call(norm_two_kernel, [tile(TOKENS, model, f32), block], scal, activations, *traded(branch), vec)
    up_beside = swap(hold_until(up_part, spent, first_sum), "core")

    square = tile(model, model)
    up_w, down_w, ahead, cot_span = call(
        units_kernel, [square, square, tile(rows, model, f32), tile(rows, model)], scal, *cot_parts, up_part, up_beside, w_down, *down_parts
    )
    normal = gathered(low)
    side = tile(rows, half)
    *grad_norm, h0, h1, p0, p1, normal_span = call(
        hidden_kernel,
        [block] * TP + [side] * 4 + [tile(rows, model)],
        *(scal, *normal, up_w, ahead),
        scratch=[pltpu.VMEM((rows, model), bf16)],
    )
    grad_norm = traded(grad_norm)
    flat = tile(half, model)
    down_send, up_send, down_keep, up_keep = call(
        units_weights_kernel,
        [flat] * 4,
        *(scal, normal_span, cot_span, h0, h1, p0, p1),
    )
    quarter = tile(half // 2, model)
    d_send, d_keep, u_send, u_keep = call(
        units_one_kernel,
        [quarter, quarter, tile(half, half), tile(half, half)],
        *(scal, down_keep, swap(down_send, "core"), up_keep, swap(up_send, "core")),
    )
    grad_first, low, lines_two = call(
        norm_two_back_kernel,
        [tile(TOKENS, model, f32), block, tile(8, model, f32)],
        *(scal, first_sum, *grad_norm, cotangent, vec),
    )
    branch_back = gathered(low)
    d_send, d_keep, u_send, u_keep = call(
        units_two_kernel,
        [block, block, tile(half, mine), tile(half, mine)],
        *(scal, d_keep, swap(d_send, "y"), u_keep, swap(u_send, "span")),
    )

    grad_qkv, grad_ctx, *back = call(
        attend_back_kernel,
        [tile(rows, 3 * mine), tile(ctx_rows, 2 * mine)] + [tile(ctx_rows, mine)] * TP,
        *(scal, valid, qkv, ctx_kv, *branch_back, out_w, qkv_w),
        scratch=[pltpu.VMEM((rows, mine), bf16), pltpu.VMEM((rows, 2 * mine), f32)],
    )
    back = traded(back)
    grad_context, turned = call(context_sum_kernel, [tile(ctx_rows, mine)] * 2, scal, *back, after=(u_send,))
    from_next = lax.ppermute(turned, "span", [(1, 0)])
    d_send = hold_until(d_send, spent, from_next)
    heads = tile(4 * model, LANES)
    heads_send, heads_keep = call(
        attend_weights_kernel,
        [heads] * 2,
        *(scal, *lowered, *context, grad_qkv, grad_ctx, mixed, *branch_back),
        scratch=[pltpu.VMEM((rows, model), bf16), pltpu.VMEM((model, 3 * mine), f32), pltpu.VMEM((mine, model), f32)],
        after=(turned,),
    )
    heads = tile(2 * model, LANES)
    heads_send, heads_keep = call(
        heads_one_kernel, [heads] * 2, scal, heads_keep, swap(heads_send, "core")
    )
    grad_lowered = hold_until(grad_qkv, spent, turned)
    grad_lowered = [dot(grad_lowered[j * TOKENS : (j + 1) * TOKENS], qkv_w, 1, 1).astype(bf16) for j in range(TP)]
    grad_lowered = traded(grad_lowered)

    u_parts = call(units_three_kernel, [piece] * TP, scal, u_keep, swap(u_send, "y"))

    grad_states, grad_local, grad_ends = call(
        scan_back_kernel,
        [channel_out, channel_out, tile(STATES, mine, f32)],
        *(scal, grad_context, from_next, own_spots, next_spots, ssm, ssm_far, decay, mix),
        scratch=[hold, hold],
        after=(heads_send, u_parts[0]),
    )
    grad_begin = lax.ppermute(grad_ends, "span", [(1, 0)])
    heads = tile(model, LANES)
    heads_send, heads_keep = call(heads_two_kernel, [heads] * 2, scal, heads_keep, swap(heads_send, "y"), after=(grad_ends,))
    (sums,) = call(
        sums_kernel,
        [tile(40, mine, f32)],
        *(scal, *lowered, grad_states, decay, begin, kept),
        scratch=[channels, hold, hold],
        after=(grad_ends,),
    )
    grad_conv = call(
        carry_back_kernel,
        [piece] * TP,
        *(scal, grad_local, decay, mix, grad_begin),
        scratch=[hold, channels],
        after=(heads_send, sums, *grad_lowered[1:]),
    )
    grad_conv = traded(grad_conv)
    (u_all,) = call(units_four_kernel, [tile(2 * LANES, model)], scal, d_keep, swap(d_send, "span"), *traded(u_parts))
    out_low, *q_parts = call(
        heads_three_kernel,
        [tile(2 * LANES, LANES)] + [tile(64, 3 * LANES)] * TP,
        *(scal, heads_keep, swap(heads_send, "span")),
    )
    grad_inputs, lines = call(
        last_kernel,
        [tile(TOKENS, model, f32), ((2 * TP, 8, LANES), f32)],
        *(scal, activations, vec, grad_first, *grad_lowered, *grad_conv, lines_two),
        scratch=[pltpu.VMEM((TOKENS, model), f32)],
        after=(u_all, out_low),
    )
    u_beside = swap(u_all, "y")
    result_parts = call(result_kernel, [block] * TP, scal, h0, h1, down_w, after=(lines,))
    result_parts = traded(result_parts)
    result = first_sum + sum(x.astype(f32) for x in result_parts)
    grad_up, grad_down = call(
        units_home_kernel,
        [tile(LANES, 4 * model, f32), tile(half, model, f32)],
        *(scal, u_all, u_beside, swap(u_all, "core"), swap(u_beside, "core")),
        after=(lines,),
    )
    (q_all,) = call(heads_four_kernel, [tile(64, 2 * model)], scal, out_low, *traded(q_parts), after=(grad_up,))
    q_beside = swap(q_all, "y")
    home = tile(LANES, model, f32)
    grad_query, grad_key, grad_value, grad_out = call(
        heads_home_kernel, [home] * 4, scal, q_all, q_beside, swap(q_all, "core"), swap(q_beside, "core"), after=tuple(spent)
    )

    lines = traded_all(lines)
    lines = jnp.sum(lines, axis=0)
    sums = sums[:, :LANES] + swap(sums[:, LANES:], "span")
    small = jnp.concatenate([lines, sums])
    small = small + swap(small, "y")
    small = small + swap(small, "core")
    lines, sums = small[:8], small[8:]
    grad_mix, grad_skip = sums[:STATES].T, sums[2 * STATES]
    step = step_size[:, None]
    grad_speed = -(output_map * input_map * step) * sums[STATES : 2 * STATES].T
    grad_step = jnp.sum(grad_mix * output_map * input_map + grad_speed * decay_rate, axis=1)
    return (
        result[None],
        grad_inputs[None],
        lines[0],
        lines[1],
        grad_query,
        grad_key,
        grad_value,
        grad_out,
        lines[2],
        lines[3],
        grad_up,
        grad_down,
        grad_speed * step,
        grad_mix * output_map * step,
        grad_mix * input_map * step,
        grad_step,
        grad_skip,
    )


def from_behind(x, axis, by):
    peers = lax.axis_size(axis)
    pairs = [(i, i + by) for i in range(peers) if 0 <= i + by < peers]
    return lax.ppermute(x, axis, pairs)


def smooth_gate(values):
    return jax.nn.gelu(values, approximate=True)


def ssm_kernel(decay_rate, input_map, output_map, step_size, length):
    offsets = jnp.arange(length).astype(jnp.float32)
    weight = output_map * input_map * step_size[:, None]
    decay_speed = step_size[:, None] * decay_rate
    total_sum = jnp.zeros((decay_rate.shape[0], length), jnp.float32)
    for state_index in range(decay_rate.shape[1]):
        total_sum = total_sum + weight[:, state_index : state_index + 1] * jnp.exp(
            -decay_speed[:, state_index : state_index + 1] * offsets[None, :]
        )
    return total_sum


def phase_table(row_count, col_count, period):
    first_ids = jnp.arange(row_count, dtype=jnp.int32)[:, None]
    second_ids = jnp.arange(col_count, dtype=jnp.int32)[None, :]
    angles = (first_ids * second_ids % period).astype(jnp.float32) * (2.0 * math.pi / period)
    return (jnp.cos(angles), jnp.sin(angles))


def exact_einsum(form, left_side, right_side):
    return jnp.einsum(form, left_side, right_side, precision=lax.Precision.HIGHEST)


def spectrum(signal, low_len, high_len):
    row_count = signal.shape[0]
    total_len = low_len * high_len
    grid_rows = signal.reshape(row_count, high_len, low_len)
    cos_high, sin_high = phase_table(high_len, high_len, high_len)
    real_part = exact_einsum("rmn,mk->rkn", grid_rows, cos_high)
    imag_part = -exact_einsum("rmn,mk->rkn", grid_rows, sin_high)
    cos_twist, sin_twist = phase_table(high_len, low_len, total_len)
    real_part, imag_part = (
        real_part * cos_twist + imag_part * sin_twist,
        imag_part * cos_twist - real_part * sin_twist,
    )
    cos_low, sin_low = phase_table(low_len, low_len, low_len)
    out_real = exact_einsum("rkn,nj->rkj", real_part, cos_low) + exact_einsum(
        "rkn,nj->rkj", imag_part, sin_low
    )
    out_imag = exact_einsum("rkn,nj->rkj", imag_part, cos_low) - exact_einsum(
        "rkn,nj->rkj", real_part, sin_low
    )
    return (out_real, out_imag)


def signal_of(real_part, imag_part, low_len, high_len, keep_len):
    row_count = real_part.shape[0]
    total_len = low_len * high_len
    cos_low, sin_low = phase_table(low_len, low_len, low_len)
    mid_real = exact_einsum("rkj,nj->rkn", real_part, cos_low) - exact_einsum(
        "rkj,nj->rkn", imag_part, sin_low
    )
    mid_imag = exact_einsum("rkj,nj->rkn", real_part, sin_low) + exact_einsum(
        "rkj,nj->rkn", imag_part, cos_low
    )
    cos_twist, sin_twist = phase_table(high_len, low_len, total_len)
    turn_real = mid_real * cos_twist - mid_imag * sin_twist
    turn_imag = mid_real * sin_twist + mid_imag * cos_twist
    cos_high, sin_high = phase_table(high_len, high_len, high_len)
    grid_rows = exact_einsum("rkn,km->rmn", turn_real, cos_high) - exact_einsum(
        "rkn,km->rmn", turn_imag, sin_high
    )
    return grid_rows.reshape(row_count, total_len)[:, :keep_len] / total_len


def padded(values):
    return jnp.concatenate([values, jnp.zeros_like(values)], axis=-1)


def norm_parts(values):
    center = values - jnp.mean(values, axis=-1, keepdims=True)
    inverse_dev = lax.rsqrt(jnp.mean(center * center, axis=-1, keepdims=True) + 1e-05)
    return (center * inverse_dev, inverse_dev)


def plain_norm_back(grad_values, scaled, inverse_dev, gain_vector):
    weighted = grad_values * gain_vector.astype(jnp.float32)
    return inverse_dev * (
        weighted
        - jnp.mean(weighted, axis=-1, keepdims=True)
        - scaled * jnp.mean(weighted * scaled, axis=-1, keepdims=True)
    )


def matmul(left_side, right_side):
    return jnp.einsum("...i,ij->...j", left_side, right_side, preferred_element_type=jnp.float32)


def matmul_t(left_side, right_side):
    return jnp.einsum("...j,ij->...i", left_side, right_side, preferred_element_type=jnp.float32)


def outer_sum(left_side, right_side):
    return jnp.einsum(
        "ri,rj->ij",
        left_side.reshape(-1, left_side.shape[-1]),
        right_side.reshape(-1, right_side.shape[-1]),
        preferred_element_type=jnp.float32,
    )


def take_rows(rows_table, row_ids):
    return jnp.take(rows_table, row_ids, axis=0)


def plain(
    activations,
    cotangent,
    block_sizes,
    context_back,
    first_gain,
    first_bias,
    w_query,
    w_key,
    w_value,
    w_out,
    second_gain,
    second_bias,
    w_up,
    w_down,
    decay_rate,
    input_map,
    output_map,
    step_size,
    skip_gain,
):
    seq_ways = lax.axis_size("seq")
    place = lax.axis_index("seq")
    seq_count, tokens, model_width = activations.shape
    channels = decay_rate.shape[0]
    length = tokens * seq_ways
    sub_len = min(BLK_A, tokens)
    sub_count = tokens // sub_len
    shift_count = max(BLK_B // tokens - 1, 0)
    head_dim = model_width // HEADS
    score_scale = head_dim ** (-0.5)
    per_dev = sub_count * CTX
    low_len = 2 * seq_ways
    (
        gain_one,
        bias_one,
        query_full,
        key_full,
        value_full,
        out_full,
        gain_two,
        bias_two,
        up_full,
        down_full,
    ) = (
        lax.all_gather(first_gain, "seq", axis=0, tiled=True),
        lax.all_gather(first_bias, "seq", axis=0, tiled=True),
        lax.all_gather(w_query, "seq", axis=0, tiled=True),
        lax.all_gather(w_key, "seq", axis=0, tiled=True),
        lax.all_gather(w_value, "seq", axis=0, tiled=True),
        lax.all_gather(w_out, "seq", axis=0, tiled=True),
        lax.all_gather(second_gain, "seq", axis=0, tiled=True),
        lax.all_gather(second_bias, "seq", axis=0, tiled=True),
        lax.all_gather(w_up, "seq", axis=0, tiled=True),
        lax.all_gather(w_down, "seq", axis=0, tiled=True),
    )
    scaled_one, inverse_one = norm_parts(activations)
    lowered = (scaled_one * gain_one.astype(jnp.float32) + bias_one.astype(jnp.float32)).astype(
        jnp.bfloat16
    )
    by_channel = lax.all_to_all(
        jnp.swapaxes(lowered, 1, 2), "seq", split_axis=1, concat_axis=2, tiled=True
    )
    channel_in = by_channel.astype(jnp.float32)
    kernel, kernel_pull = jax.vjp(
        lambda a, b, c, e: ssm_kernel(a, b, c, e, length),
        decay_rate,
        input_map,
        output_map,
        step_size,
    )
    input_real, input_imag = spectrum(padded(channel_in.reshape(-1, length)), low_len, tokens)
    input_real = input_real.reshape(seq_count, channels, tokens, low_len)
    input_imag = input_imag.reshape(seq_count, channels, tokens, low_len)
    kernel_real, kernel_imag = spectrum(padded(kernel), low_len, tokens)
    conv_real = input_real * kernel_real - input_imag * kernel_imag
    conv_imag = input_real * kernel_imag + input_imag * kernel_real
    convolved = signal_of(
        conv_real.reshape(-1, tokens, low_len),
        conv_imag.reshape(-1, tokens, low_len),
        low_len,
        tokens,
        length,
    )
    states = convolved.reshape(seq_count, channels, length) + skip_gain[None, :, None] * channel_in
    targets = (
        jnp.arange(seq_ways, dtype=jnp.int32)[:, None] * tokens
        + jnp.arange(sub_count, dtype=jnp.int32)[None, :] * sub_len
    )
    sizes_three = block_sizes[:, None, None]
    block_start = targets[None] // sizes_three * sizes_three
    positions = block_start[..., None] - context_back
    valid_all = positions >= 0
    picks = jnp.maximum(positions, 0).reshape(seq_count, -1)
    position_major = jnp.swapaxes(states, 1, 2)
    picked = jax.vmap(take_rows)(position_major, picks)
    picked = jnp.where(valid_all.reshape(seq_count, -1, 1), picked, 0.0).astype(jnp.bfloat16)
    picked = jnp.swapaxes(picked, 1, 2)
    arrived = lax.all_to_all(
        picked.reshape(seq_count, channels, seq_ways, per_dev),
        "seq",
        split_axis=2,
        concat_axis=1,
        tiled=True,
    )
    context = jnp.swapaxes(arrived.reshape(seq_count, model_width, per_dev), 1, 2)
    own_valid = lax.dynamic_index_in_dim(valid_all, place, axis=1, keepdims=False).reshape(
        seq_count, per_dev
    )
    queries = matmul(lowered, query_full).astype(jnp.bfloat16)
    keys_own = matmul(lowered, key_full).astype(jnp.bfloat16)
    values_own = matmul(lowered, value_full).astype(jnp.bfloat16)
    ctx_keys = matmul(context, key_full).astype(jnp.bfloat16)
    ctx_values = matmul(context, value_full).astype(jnp.bfloat16)
    key_parts = [ctx_keys]
    value_parts = [ctx_values]
    key_places = []
    token_ids = jnp.arange(tokens, dtype=jnp.int32)
    for distance in range(shift_count, 0, -1):
        far_keys, far_values = from_behind((keys_own, values_own), "seq", distance)
        key_parts.append(far_keys)
        value_parts.append(far_values)
        key_places.append((place - distance) * tokens + token_ids)
    key_parts.append(keys_own)
    value_parts.append(values_own)
    key_places.append(place * tokens + token_ids)
    all_keys = jnp.concatenate(key_parts, axis=1)
    all_values = jnp.concatenate(value_parts, axis=1)
    key_pos = jnp.concatenate(key_places)
    query_pos = place * tokens + token_ids
    same_block = key_pos[None, None, :] // sizes_three == query_pos[None, :, None] // sizes_three
    causal = key_pos[None, None, :] <= query_pos[None, :, None]
    ctx_allowed = (
        (token_ids // sub_len)[:, None] == (jnp.arange(per_dev, dtype=jnp.int32) // CTX)[None, :]
    )[None] & own_valid[:, None, :]
    allowed = jnp.concatenate([ctx_allowed, same_block & causal], axis=2)

    def split_heads(values):
        return values.reshape(values.shape[0], values.shape[1], HEADS, head_dim)

    def scores_of():
        raw_scores = (
            jnp.einsum(
                "sqhd,skhd->shqk",
                split_heads(queries),
                split_heads(all_keys),
                preferred_element_type=jnp.float32,
            )
            * score_scale
        )
        return jnp.where(allowed[:, None], raw_scores, -1e30)

    scores = scores_of()
    row_top = jnp.max(scores, axis=-1, keepdims=True)
    log_total = row_top + jnp.log(jnp.sum(jnp.exp(scores - row_top), axis=-1, keepdims=True))
    probs_low = jnp.exp(scores - log_total).astype(jnp.bfloat16)
    attended = jnp.einsum(
        "shqk,skhd->sqhd", probs_low, split_heads(all_values), preferred_element_type=jnp.float32
    )
    mixed_out = attended.reshape(seq_count, tokens, model_width).astype(jnp.bfloat16)
    first_sum = activations + matmul(mixed_out, out_full)
    scaled_two, inverse_two = norm_parts(first_sum)
    normal_two = (scaled_two * gain_two.astype(jnp.float32) + bias_two.astype(jnp.float32)).astype(
        jnp.bfloat16
    )
    pre_gate = matmul(normal_two, up_full)
    hidden, gate_pull = jax.vjp(smooth_gate, pre_gate)
    hidden_low = hidden.astype(jnp.bfloat16)
    result = first_sum + matmul(hidden_low, down_full)
    grad_down = outer_sum(hidden_low, cotangent)
    grad_hidden = matmul_t(cotangent, down_full)
    grad_pre = gate_pull(grad_hidden)[0].astype(jnp.bfloat16)
    grad_up = outer_sum(normal_two, grad_pre)
    grad_norm_two = matmul_t(grad_pre, up_full)
    grad_gain_two = jnp.sum(grad_norm_two * scaled_two, axis=(0, 1))
    grad_bias_two = jnp.sum(grad_norm_two, axis=(0, 1))
    grad_first = cotangent.astype(jnp.float32) + plain_norm_back(
        grad_norm_two, scaled_two, inverse_two, gain_two
    )
    grad_branch = grad_first.astype(jnp.bfloat16)
    grad_out = outer_sum(mixed_out, grad_branch)
    grad_mixed = split_heads(matmul_t(grad_branch, out_full).astype(jnp.bfloat16))
    scores = scores_of()
    probabilities = jnp.exp(scores - log_total)
    probs_low = probabilities.astype(jnp.bfloat16)
    grad_probs = jnp.einsum(
        "sqhd,skhd->shqk", grad_mixed, split_heads(all_values), preferred_element_type=jnp.float32
    )
    grad_all_values = jnp.einsum(
        "shqk,sqhd->skhd", probs_low, grad_mixed, preferred_element_type=jnp.float32
    )
    grad_scores = (
        probabilities * (grad_probs - jnp.sum(probabilities * grad_probs, axis=-1, keepdims=True))
    ).astype(jnp.bfloat16)
    grad_queries = (
        jnp.einsum(
            "shqk,skhd->sqhd",
            grad_scores,
            split_heads(all_keys),
            preferred_element_type=jnp.float32,
        )
        * score_scale
    )
    grad_queries = grad_queries.reshape(seq_count, tokens, model_width).astype(jnp.bfloat16)
    grad_all_keys = (
        jnp.einsum(
            "shqk,sqhd->skhd", grad_scores, split_heads(queries), preferred_element_type=jnp.float32
        )
        * score_scale
    )
    grad_all_keys = grad_all_keys.reshape(seq_count, -1, model_width)
    grad_all_values = grad_all_values.reshape(seq_count, -1, model_width)
    grad_ctx_keys = grad_all_keys[:, :per_dev]
    grad_ctx_values = grad_all_values[:, :per_dev]
    grad_keys = grad_all_keys[:, -tokens:]
    grad_values = grad_all_values[:, -tokens:]
    for distance in range(shift_count, 0, -1):
        begin = per_dev + (shift_count - distance) * tokens
        back_keys, back_values = (
            from_behind(
                grad_all_keys[:, begin : begin + tokens].astype(jnp.bfloat16), "seq", -distance
            ).astype(jnp.float32),
            from_behind(
                grad_all_values[:, begin : begin + tokens].astype(jnp.bfloat16), "seq", -distance
            ).astype(jnp.float32),
        )
        grad_keys = grad_keys + back_keys
        grad_values = grad_values + back_values
    grad_keys_low = grad_keys.astype(jnp.bfloat16)
    grad_values_low = grad_values.astype(jnp.bfloat16)
    context_wide = context.astype(jnp.float32)
    grad_query_w = outer_sum(lowered, grad_queries)
    grad_key_w = outer_sum(lowered, grad_keys_low) + outer_sum(context_wide, grad_ctx_keys)
    grad_value_w = outer_sum(lowered, grad_values_low) + outer_sum(context_wide, grad_ctx_values)
    grad_normal_one = (
        matmul_t(grad_queries, query_full)
        + matmul_t(grad_keys_low, key_full)
        + matmul_t(grad_values_low, value_full)
    )
    grad_context = matmul_t(grad_ctx_keys, key_full) + matmul_t(grad_ctx_values, value_full)
    sent_back = jnp.swapaxes(grad_context, 1, 2).reshape(seq_count, model_width, 1, per_dev)
    returned = lax.all_to_all(
        sent_back.astype(jnp.bfloat16), "seq", split_axis=1, concat_axis=2, tiled=True
    ).astype(sent_back.dtype)
    returned = jnp.where(
        valid_all.reshape(seq_count, 1, -1), returned.reshape(seq_count, channels, -1), 0.0
    )
    segment_ids = (jnp.arange(seq_count, dtype=jnp.int32)[:, None] * length + picks).reshape(-1)
    flat_rows = jnp.swapaxes(returned, 1, 2).reshape(-1, channels)
    grad_states = jax.ops.segment_sum(flat_rows, segment_ids, num_segments=seq_count * length)
    grad_states = jnp.swapaxes(grad_states.reshape(seq_count, length, channels), 1, 2)
    grad_real, grad_imag = spectrum(padded(grad_states.reshape(-1, length)), low_len, tokens)
    grad_real = grad_real.reshape(seq_count, channels, tokens, low_len)
    grad_imag = grad_imag.reshape(seq_count, channels, tokens, low_len)
    back_real = grad_real * kernel_real + grad_imag * kernel_imag
    back_imag = grad_imag * kernel_real - grad_real * kernel_imag
    grad_conv = signal_of(
        back_real.reshape(-1, tokens, low_len),
        back_imag.reshape(-1, tokens, low_len),
        low_len,
        tokens,
        length,
    )
    grad_conv = grad_conv.reshape(seq_count, channels, length)
    corr_real = jnp.sum(grad_real * input_real + grad_imag * input_imag, axis=0)
    corr_imag = jnp.sum(grad_imag * input_real - grad_real * input_imag, axis=0)
    grad_kernel = signal_of(corr_real, corr_imag, low_len, tokens, length)
    grad_rate, grad_in_map, grad_out_map, grad_step = kernel_pull(grad_kernel)
    grad_skip = jnp.sum(grad_states * channel_in, axis=(0, 2))
    grad_channel = grad_conv + skip_gain[None, :, None] * grad_states
    back_tokens = lax.all_to_all(
        grad_channel.astype(jnp.bfloat16), "seq", split_axis=2, concat_axis=1, tiled=True
    ).astype(grad_channel.dtype)
    grad_normal_one = grad_normal_one + jnp.swapaxes(back_tokens, 1, 2)
    grad_gain_one = jnp.sum(grad_normal_one * scaled_one, axis=(0, 1))
    grad_bias_one = jnp.sum(grad_normal_one, axis=(0, 1))
    grad_inputs = grad_first + plain_norm_back(grad_normal_one, scaled_one, inverse_one, gain_one)
    shares = (
        lax.psum_scatter(
            grad_gain_one.astype(jnp.bfloat16), "seq", scatter_dimension=0, tiled=True
        ).astype(jnp.float32),
        lax.psum_scatter(
            grad_bias_one.astype(jnp.bfloat16), "seq", scatter_dimension=0, tiled=True
        ).astype(jnp.float32),
        lax.psum_scatter(
            grad_query_w.astype(jnp.bfloat16), "seq", scatter_dimension=0, tiled=True
        ).astype(jnp.float32),
        lax.psum_scatter(
            grad_key_w.astype(jnp.bfloat16), "seq", scatter_dimension=0, tiled=True
        ).astype(jnp.float32),
        lax.psum_scatter(
            grad_value_w.astype(jnp.bfloat16), "seq", scatter_dimension=0, tiled=True
        ).astype(jnp.float32),
        lax.psum_scatter(
            grad_out.astype(jnp.bfloat16), "seq", scatter_dimension=0, tiled=True
        ).astype(jnp.float32),
        lax.psum_scatter(
            grad_gain_two.astype(jnp.bfloat16), "seq", scatter_dimension=0, tiled=True
        ).astype(jnp.float32),
        lax.psum_scatter(
            grad_bias_two.astype(jnp.bfloat16), "seq", scatter_dimension=0, tiled=True
        ).astype(jnp.float32),
        lax.psum_scatter(
            grad_up.astype(jnp.bfloat16), "seq", scatter_dimension=0, tiled=True
        ).astype(jnp.float32),
        lax.psum_scatter(
            grad_down.astype(jnp.bfloat16), "seq", scatter_dimension=0, tiled=True
        ).astype(jnp.float32),
    )
    summed = (
        lax.psum(shares[0].astype(jnp.bfloat16), "dp").astype(jnp.float32),
        lax.psum(shares[1].astype(jnp.bfloat16), "dp").astype(jnp.float32),
        lax.psum(shares[2].astype(jnp.bfloat16), "dp").astype(jnp.float32),
        lax.psum(shares[3].astype(jnp.bfloat16), "dp").astype(jnp.float32),
        lax.psum(shares[4].astype(jnp.bfloat16), "dp").astype(jnp.float32),
        lax.psum(shares[5].astype(jnp.bfloat16), "dp").astype(jnp.float32),
        lax.psum(shares[6].astype(jnp.bfloat16), "dp").astype(jnp.float32),
        lax.psum(shares[7].astype(jnp.bfloat16), "dp").astype(jnp.float32),
        lax.psum(shares[8].astype(jnp.bfloat16), "dp").astype(jnp.float32),
        lax.psum(shares[9].astype(jnp.bfloat16), "dp").astype(jnp.float32),
        lax.psum(grad_rate.astype(jnp.bfloat16), "dp").astype(jnp.float32),
        lax.psum(grad_in_map.astype(jnp.bfloat16), "dp").astype(jnp.float32),
        lax.psum(grad_out_map.astype(jnp.bfloat16), "dp").astype(jnp.float32),
        lax.psum(grad_step.astype(jnp.bfloat16), "dp").astype(jnp.float32),
        lax.psum(grad_skip.astype(jnp.bfloat16), "dp").astype(jnp.float32),
    )
    summed = tuple(summed)
    return (
        result,
        grad_inputs,
        summed[0],
        summed[1],
        summed[2],
        summed[3],
        summed[4],
        summed[5],
        summed[6],
        summed[7],
        summed[8],
        summed[9],
        summed[10],
        summed[11],
        summed[12],
        summed[13],
        summed[14],
    )


def solution(mesh):
    dp_ways, seq_ways = mesh.shape["dp"], mesh.shape["seq"]
    lone, data, flat, cut = P(), P("dp", "seq", None), P("seq"), P("seq", None)
    in_specs = (data, data, P("dp"), lone, flat, flat, cut, cut, cut, cut, flat, flat, cut, cut, cut, cut, cut, flat, flat)
    out_specs = (data, data, flat, flat, cut, cut, cut, cut, flat, flat, cut, cut, cut, cut, cut, flat, flat)

    def run(activations, *others):
        seqs, length, model = activations.shape
        tokens = length // seq_ways
        if (seqs, dp_ways, seq_ways, tokens, model) != (4, 4, 2 * TP, TOKENS, HEADS * LANES):
            return jax.shard_map(plain, mesh=mesh, in_specs=in_specs, out_specs=out_specs, check_vma=False)(activations, *others)
        fine = Mesh(mesh.devices.reshape(2, 2, 2, TP), ("y", "core", "span", "tp"))
        names = {"dp": ("y", "core"), "seq": ("span", "tp")}
        split = lambda specs: tuple(P(*(names.get(a) for a in spec)) for spec in specs)
        whole = jax.shard_map(by_spans, mesh=fine, in_specs=split(in_specs), out_specs=split(out_specs), check_vma=False)
        return whole(activations, *others)

    return run
```

```python
import functools
import math

import jax
import jax.numpy as jnp
from jax import lax
from jax.experimental import pallas as pl
from jax.experimental.pallas import tpu as pltpu
from jax.sharding import Mesh
from jax.sharding import PartitionSpec as P

HEADS = 8
CTX = 128
BLK_A = 256
BLK_B = 512
TP = 4
TOKENS = 128
LANES = 128
UNITS = 256
STATES = 16
CHUNKS = 8
NEG = -1e30
f32 = jnp.float32
bf16 = jnp.bfloat16
LIMIT = 24
SWAP = [(0, 1), (1, 0)]
PER_US = 16000000000
MICROSECONDS = {
    "norm_one_kernel": 0.85,
    "scan_kernel": 4.6,
    "carry_kernel": 2.0,
    "qkv_kernel": 2.3,
    "attend_kernel": 4.0,
    "norm_two_kernel": 1.0,
    "units_kernel": 3.0,
    "hidden_kernel": 5.4,
    "units_weights_kernel": 3.0,
    "units_one_kernel": 1.1,
    "norm_two_back_kernel": 1.2,
    "attend_back_kernel": 4.8,
    "attend_weights_kernel": 2.4,
    "context_sum_kernel": 0.65,
    "heads_one_kernel": 0.8,
    "units_two_kernel": 0.8,
    "result_kernel": 1.8,
    "scan_back_kernel": 4.0,
    "units_three_kernel": 0.7,
    "carry_back_kernel": 1.9,
    "heads_two_kernel": 0.9,
    "sums_kernel": 4.5,
    "units_four_kernel": 0.6,
    "last_kernel": 2.1,
    "heads_three_kernel": 0.6,
    "heads_four_kernel": 0.6,
    "units_home_kernel": 3.0,
    "heads_home_kernel": 2.1,
    "pack_kernel": 0.7,
    "lines_kernel": 0.5,
    "lowered_back_kernel": 1.7,
    "share_kernel": 2.5,
    "lines_sum_kernel": 0.5,
}


SPAN, PLACE, ROW, CORE, WIDE = range(5)


def call(kernel, outs, *args, scratch=(), loose=(), after=(), limit=LIMIT):
    count = len(args)
    vmem, free = pl.BlockSpec(memory_space=pltpu.VMEM), pl.BlockSpec(memory_space=pl.ANY)
    specs = [pl.BlockSpec(memory_space=pltpu.SMEM)] + [free if i in loose else vmem for i in range(1, count)] + [free] * len(after)

    def inner(*refs):
        kernel(*refs[:count], *refs[count + len(after) :])

    return pl.pallas_call(
        inner,
        out_shape=[jax.ShapeDtypeStruct(shape, kind) for shape, kind in outs],
        in_specs=specs,
        out_specs=[vmem] * len(outs),
        scratch_shapes=list(scratch),
        compiler_params=pltpu.CompilerParams(vmem_limit_bytes=limit * 1024 * 1024),
        cost_estimate=pl.CostEstimate(flops=int(MICROSECONDS[kernel.__name__] * PER_US), bytes_accessed=0, transcendentals=0),
    )(*args, *after)


def part(index, size):
    return pl.ds(pl.multiple_of(index * size, size), size)


def channel_part(scal, s, rank):
    return part((s ^ scal[SPAN]) * TP + rank, LANES)


def dot(a, b, ca, cb):
    return lax.dot_general(a, b, (((ca,), (cb,)), ((), ())), preferred_element_type=f32)


def wide(ref):
    return ref[...].astype(f32)


def send_all(copies, sems):
    copies = [pltpu.make_async_copy(a, b, sems.at[i]) for i, (a, b) in enumerate(copies)]
    for copy in copies:
        copy.start()
    for copy in copies:
        copy.wait()


def share_kernel(scal, wq, wk, wv, out, down, up, send, out_send, down_send, sems):
    core, row = scal[CORE], scal[ROW]
    copies = [(out.at[part(core, 64), :], out_send), (down.at[part(core * 2 + row, LANES), :], down_send)]
    for to in range(2 * TP):
        for s in range(2):
            there = ((s * TP + to % TP) * 2 + core) * 2 + row
            copies.append((up.at[:, part(there, LANES)], send.at[to, pl.ds(s * TOKENS, TOKENS), :]))
    copies = [pltpu.make_async_copy(a, b, sems.at[i]) for i, (a, b) in enumerate(copies)]
    for copy in copies:
        copy.start()
    for rank in range(TP):
        for m, w in enumerate((wq, wk, wv)):
            value = w[part(row, 64), part(core * TP + rank, LANES)]
            for s in range(2):
                send[s * TP + rank, pl.ds(2 * TOKENS + m * 64, 64), :] = value
    for copy in copies:
        copy.wait()


def pack_kernel(scal, rate, inward, outward, step, skip, g1, b1, g2, b2, out, vecs, sems):
    places = [pl.ds(i * STATES, STATES) for i in range(3)] + [pl.ds(3 * STATES + i, 1) for i in range(2)]
    copies = [(ref, out.at[at, :]) for ref, at in zip((rate, inward, outward, step, skip), places)]
    copies += [(ref, vecs.at[i]) for i, ref in enumerate((g1, b1, g2, b2))]
    copies = [pltpu.make_async_copy(a, b, sems.at[i]) for i, (a, b) in enumerate(copies)]
    for copy in copies:
        copy.start()
    for copy in copies:
        copy.wait()
    for i in range(4):
        out[3 * STATES + 2 + i : 3 * STATES + 3 + i, :] = vecs[i].astype(f32)
    out[3 * STATES + 6 :, :] = jnp.zeros((out.shape[0] - 3 * STATES - 6, LANES), f32)


def lines_kernel(scal, own, far, vec):
    for ref, s in ((own, scal[SPAN]), (far, 1 - scal[SPAN])):
        vec[part(s, 8), :] = jnp.concatenate([ref[50:54, :], jnp.zeros((4, LANES), f32)], axis=0)


def norm_rows(x):
    center = x - jnp.mean(x, axis=1, keepdims=True)
    inverse = lax.rsqrt(jnp.mean(center * center, axis=1, keepdims=True) + 1e-05)
    return center * inverse, inverse


def gather_lines(scal, vecs, lines):
    for j, vec in enumerate(vecs):
        for s in range(2):
            lines[:, part(s * TP + (scal[PLACE] ^ j), LANES)] = vec[s * 8 : s * 8 + 8, :]


def norm_one_kernel(scal, x, v0, v1, v2, v3, low, lines):
    gather_lines(scal, (v0, v1, v2, v3), lines)
    scaled, _ = norm_rows(x[...])
    low[...] = (scaled * lines[0:1, :] + lines[1:2, :]).astype(bf16)


def sum_of(own, a, b, c):
    return (wide(own) + wide(a)) + (wide(b) + wide(c))


def norm_two_kernel(scal, x, own, a, b, c, vec, total, low):
    first = x[...] + sum_of(own, a, b, c)
    total[...] = first
    scaled, _ = norm_rows(first)
    low[...] = (scaled * vec[2:3, :] + vec[3:4, :]).astype(bf16)


def norm_back(grad, scaled, inverse, gain):
    e = grad * gain
    return inverse * (e - jnp.mean(e, axis=1, keepdims=True) - scaled * jnp.mean(e * scaled, axis=1, keepdims=True))


def norm_two_back_kernel(scal, total, own, a, b, c, cot, vec, grad_first, low, lines):
    grad = sum_of(own, a, b, c)
    scaled, inverse = norm_rows(total[...])
    value = cot[...].astype(f32) + norm_back(grad, scaled, inverse, vec[2:3, :])
    grad_first[...] = value
    low[...] = value.astype(bf16)
    lines[0:1, :] = jnp.sum(grad * scaled, axis=0, keepdims=True)
    lines[1:2, :] = jnp.sum(grad, axis=0, keepdims=True)
    lines[2:8, :] = jnp.zeros((6, lines.shape[1]), f32)


def last_kernel(scal, x, vec, grad_first, own, a, b, c, p0, p1, p2, p3, lines_two, out, lines, grad):
    grad[...] = sum_of(own, a, b, c)
    for j, p in enumerate((p0, p1, p2, p3)):
        for s in range(2):
            lanes = channel_part(scal, s, scal[PLACE] ^ j)
            grad[:, lanes] = grad[:, lanes] + p[:, pl.ds(s * LANES, LANES)].astype(f32)
    scaled, inverse = norm_rows(x[...])
    out[...] = grad_first[...] + norm_back(grad[...], scaled, inverse, vec[0:1, :])
    gain = jnp.sum(grad[...] * scaled, axis=0, keepdims=True)
    bias = jnp.sum(grad[...], axis=0, keepdims=True)
    for n in range(lines.shape[0]):
        lanes = slice(n * LANES, (n + 1) * LANES)
        lines[n, 0:1, :] = gain[:, lanes]
        lines[n, 1:2, :] = bias[:, lanes]
        lines[n, 2:4, :] = lines_two[0:2, lanes]
        lines[n, 4:8, :] = jnp.zeros((4, LANES), f32)


def lines_sum_kernel(scal, parts, sums, out):
    out[0:8, :] = jnp.sum(parts[...], axis=0)
    out[8:, :] = sums[...]


def spread(row):
    return jnp.broadcast_to(row, (CHUNKS, LANES))


def power(base, times):
    for _ in range(int(math.log2(times))):
        base = base * base
    return base


def total_of(parts):
    while len(parts) > 1:
        parts = [parts[i] + parts[i + 1] for i in range(0, len(parts), 2)]
    return parts[0]


def one_hot(spots, rows):
    return (spots[...] == lax.broadcasted_iota(jnp.int32, (spots.shape[0], rows), 1)).astype(bf16)


def own_channels(scal, xs, parts):
    place = scal[PLACE]
    for j, x in enumerate(parts):
        for s in range(2):
            xs[s, part(place ^ j, TOKENS), :] = x[:, channel_part(scal, s, place)].astype(f32)


def scan(reverse, xs, a_ref, w_ref, skips, y_ref, end, sh, ih, sq=None, kept=None):
    states = a_ref.shape[0]
    steps = xs.shape[1] // CHUNKS

    def at(step):
        return pl.ds(steps - 1 - step if reverse else step, CHUNKS, stride=steps)

    for s in range(xs.shape[0]):
        cols = pl.ds(s * LANES, LANES)
        rate = [spread(a_ref[n : n + 1, cols]) for n in range(states)]
        ih[0] = jnp.zeros((CHUNKS, LANES), f32)
        zero = ih[0]

        def local(step, carry):
            x = xs[s, at(step), :]
            if sq is not None:
                h, q = carry
                q = tuple(a * (u + v) for a, u, v in zip(rate, q, h))
            else:
                (h,) = carry
            h = tuple(a * v + x for a, v in zip(rate, h))
            return (h, q) if sq is not None else (h,)

        done = lax.fori_loop(0, steps, local, ((zero,) * states,) * (1 if sq is None else 2), unroll=4)
        for n in range(states):
            sh[n] = done[0][n]
            if sq is not None:
                sq[n] = done[1][n]
        jump = power(a_ref[:, cols], steps)
        hold = jnp.zeros((states, LANES), f32)
        hold_q = jnp.zeros((states, LANES), f32)
        for k in range(CHUNKS):
            k = CHUNKS - 1 - k if reverse else k
            ih[:, k, :] = hold
            if sq is not None:
                hold_q = jump * (hold_q + float(steps) * hold) + sq[:, k, :]
            hold = jump * hold + sh[:, k, :]
        if kept is not None:
            kept[0, s] = sh[...]
            kept[1, s] = sq[...]
        end(s, hold, hold_q)
        weight = [spread(w_ref[n : n + 1, cols]) for n in range(states)]
        skip = spread(skips[s][49:50, :])

        def emit(step, h):
            x = xs[s, at(step), :]
            h = tuple(a * v + x for a, v in zip(rate, h))
            y_ref[s, at(step), :] = total_of([w * v for w, v in zip(weight, h)]) + skip * x
            return h

        lax.fori_loop(0, steps, emit, tuple(ih[n] for n in range(states)), unroll=4)


def scan_kernel(scal, x0, x1, x2, x3, ssm0, ssm1, spots, y, to_next, ends, decay, mix, kept, xs, low, sh, sq, ih):
    own_channels(scal, xs, (x0, x1, x2, x3))
    n = decay.shape[0]
    for s, ssm in enumerate((ssm0, ssm1)):
        cols = pl.ds(s * LANES, LANES)
        step = ssm[48:49, :]
        decay[:, cols] = jnp.exp(-step * ssm[0:n, :])
        mix[:, cols] = ssm[32:48, :] * ssm[16:32, :] * step

    def end(s, h, q):
        other = pl.ds((1 - s) * LANES, LANES)
        ends[0:n, other] = h
        ends[n : 2 * n, other] = q

    scan(False, xs, decay, mix, (ssm0, ssm1), y, end, sh, ih, sq, kept)
    for s in range(2):
        low[:, pl.ds((1 - s) * LANES, LANES)] = y[s].astype(bf16)
    to_next[...] = dot(one_hot(spots, low.shape[0]), low[...], 1, 0).astype(bf16)


def carry(reverse, y_ref, a_ref, w_ref, h_ref, out, ih):
    states = a_ref.shape[0]
    steps = y_ref.shape[1] // CHUNKS

    def at(step):
        return pl.ds(steps - 1 - step if reverse else step, CHUNKS, stride=steps)

    for s in range(y_ref.shape[0]):
        cols = pl.ds(s * LANES, LANES)
        rate = [spread(a_ref[n : n + 1, cols]) for n in range(states)]
        jump = power(a_ref[:, cols], steps)
        hold = w_ref[:, cols] * h_ref[0:states, cols]
        for k in range(CHUNKS):
            ih[:, CHUNKS - 1 - k if reverse else k, :] = hold
            hold = jump * hold

        def emit(step, h):
            h = tuple(a * v for a, v in zip(rate, h))
            out[s, at(step), :] = y_ref[s, at(step), :] + total_of(list(h))
            return h

        lax.fori_loop(0, steps, emit, tuple(ih[n] for n in range(states)), unroll=4)


def carry_kernel(scal, y, decay, mix, begin, from_last, spots, context, ih, ys, low):
    carry(False, y, decay, mix, begin, ys, ih)
    for s in range(2):
        low[:, pl.ds(s * LANES, LANES)] = ys[s].astype(bf16)
    context[...] = (dot(one_hot(spots, low.shape[0]), low[...], 1, 0) + wide(from_last)).astype(bf16)


def scan_back_kernel(scal, own, from_next, own_spots, next_spots, ssm0, ssm1, decay, mix, grad, y, ends, sh, ih):
    rows = y.shape[1]
    value = dot(one_hot(own_spots, rows), own[...], 0, 0) + dot(one_hot(next_spots, rows), from_next[...], 0, 0)
    for s in range(2):
        grad[s] = value[:, s * LANES : (s + 1) * LANES]

    def end(s, h, q):
        ends[:, pl.ds((1 - s) * LANES, LANES)] = h

    scan(True, grad, decay, mix, (ssm0, ssm1), y, end, sh, ih)


def carry_back_kernel(scal, y, decay, mix, begin, o0, o1, o2, o3, ih, ys):
    carry(True, y, decay, mix, begin, ys, ih)
    for j, out in enumerate((o0, o1, o2, o3)):
        for s in range(2):
            out[:, pl.ds(s * LANES, LANES)] = ys[s, part(scal[PLACE] ^ j, TOKENS), :].astype(bf16)


def sums_kernel(scal, x0, x1, x2, x3, gs, a_ref, begin, kept, out, xs, ih, iq):
    own_channels(scal, xs, (x0, x1, x2, x3))
    states = a_ref.shape[0]
    steps = xs.shape[1] // CHUNKS
    group = 8
    out[2 * states :, :] = jnp.zeros((out.shape[0] - 2 * states, out.shape[1]), f32)
    for s in range(xs.shape[0]):
        cols = pl.ds(s * LANES, LANES)
        jump = power(a_ref[:, cols], steps)
        hold, hold_q = begin[0:states, cols], begin[states : 2 * states, cols]
        for k in range(CHUNKS):
            ih[:, k, :] = hold
            iq[:, k, :] = hold_q
            hold_q = jump * (hold_q + float(steps) * hold) + kept[1, s, :, k, :]
            hold = jump * hold + kept[0, s, :, k, :]
        for base in range(0, states, group):
            rate = [spread(a_ref[n : n + 1, cols]) for n in range(base, base + group)]

            def gain(step, carried):
                h, q, sw, sq = carried
                at = pl.ds(step, CHUNKS, stride=steps)
                x, g = xs[s, at, :], gs[s, at, :]
                q = tuple(a * (u + v) for a, u, v in zip(rate, q, h))
                h = tuple(a * v + x for a, v in zip(rate, h))
                sw = tuple(u + g * v for u, v in zip(sw, h))
                sq = tuple(u + g * v for u, v in zip(sq, q))
                return h, q, sw, sq

            first = tuple(ih[base + n] for n in range(group)), tuple(iq[base + n] for n in range(group))
            none = tuple(v * 0.0 for v in first[0])
            _, _, sw, sq = lax.fori_loop(0, steps, gain, first + (none, none), unroll=2)
            for n in range(group):
                out[base + n : base + n + 1, cols] = jnp.sum(sw[n], axis=0, keepdims=True)
                out[states + base + n : states + base + n + 1, cols] = jnp.sum(sq[n], axis=0, keepdims=True)
        out[2 * states : 2 * states + 1, cols] = jnp.sum(xs[s] * gs[s], axis=0, keepdims=True)


def qkv_kernel(scal, x0, x1, x2, x3, w00, w01, w10, w11, w, qkv):
    for j, k, ref in ((0, 0, w00), (0, 1, w01), (1, 0, w10), (1, 1, w11)):
        for n in range(2 * TP):
            for m in range(3):
                there = part(2 * n + (scal[ROW] ^ k), 64)
                w[there, pl.ds((2 * m + j) * LANES, LANES)] = ref[n, pl.ds(2 * TOKENS + m * 64, 64), :]
    for j, x in enumerate((x0, x1, x2, x3)):
        qkv[part(scal[PLACE] ^ j, TOKENS), :] = dot(x[...], w[...], 1, 0).astype(bf16)


def masks(size, is_wide, ok_ref, sub):
    rows = lax.broadcasted_iota(jnp.int32, (size, size), 0)
    cols = lax.broadcasted_iota(jnp.int32, (size, size), 1)
    return ok_ref[sub : sub + 1, :] > 0.0, is_wide > 0, cols <= rows


def out_of_order(out_ref, lanes, value, sub, place):
    each = value.shape[0] // TOKENS
    for i in range(each):
        out_ref[part((sub * each + i) ^ place, TOKENS), lanes] = value[i * TOKENS : (i + 1) * TOKENS]


def probabilities(q, ctx_k, k_ref, size, sub, lanes, mask, scale):
    context, earlier, own = mask
    parts = [jnp.where(context, dot(q, ctx_k, 1, 1) * scale, NEG)]
    for other in range(sub):
        keys = k_ref[pl.ds(other * size, size), lanes]
        parts.append(jnp.where(earlier, dot(q, keys, 1, 1) * scale, NEG))
    parts.append(jnp.where(own, dot(q, k_ref[pl.ds(sub * size, size), lanes], 1, 1) * scale, NEG))
    top = functools.reduce(jnp.maximum, [jnp.max(s, axis=1, keepdims=True) for s in parts])
    parts = [jnp.exp(s - top) for s in parts]
    inverse = 1.0 / sum(jnp.sum(s, axis=1, keepdims=True) for s in parts)
    return [s * inverse for s in parts]


def attend_kernel(scal, ok, qkv, c0, c1, c2, c3, w, out_own, out_0, out_1, mixed, ckv, out_w, b0, b1, b2, b3):
    place, core = scal[PLACE], scal[CORE]
    width = qkv.shape[1] // 3
    dim = LANES
    own = core ^ scal[SPAN]
    out_w[part(own, dim), :] = out_own[...]
    out_w[part((1 - own) * 2 + core, 64), :] = out_0[...]
    out_w[part((1 - own) * 2 + 1 - core, 64), :] = out_1[...]
    total = None
    for j, c in enumerate((c0, c1, c2, c3)):
        for s in range(2):
            term = dot(c[:, pl.ds(s * LANES, LANES)], w[channel_part(scal, s, place ^ j), pl.ds(width, 2 * width)], 1, 0)
            total = term if total is None else total + term
    ckv[...] = total.astype(bf16)
    subs = ok.shape[0]
    size = qkv.shape[0] // subs
    scale = dim ** (-0.5)
    for sub in range(subs):
        mask = masks(size, scal[WIDE], ok, sub)
        here = pl.ds(sub * size, size)
        for h in range(width // dim):
            lq, lk, lv = (pl.ds(i * width + h * dim, dim) for i in range(3))
            ck = ckv[pl.ds(sub * CTX, CTX), pl.ds(h * dim, dim)]
            cv = ckv[pl.ds(sub * CTX, CTX), pl.ds(width + h * dim, dim)]
            probs = probabilities(qkv[here, lq], ck, qkv, size, sub, lk, mask, scale)
            value = dot(probs[0].astype(bf16), cv, 1, 0)
            for other in range(sub + 1):
                value += dot(probs[1 + other].astype(bf16), qkv[pl.ds(other * size, size), lv], 1, 0)
            out_of_order(mixed, pl.ds(h * dim, dim), value.astype(bf16), sub, place)
    for j, b in enumerate((b0, b1, b2, b3)):
        b[...] = dot(mixed[pl.ds(j * TOKENS, TOKENS), :], out_w[...], 1, 0).astype(bf16)


def attend_back_kernel(scal, ok, qkv, ckv, g0, g1, g2, g3, out_w, w, out, ctx, x0, x1, x2, x3, gms, acc):
    place = scal[PLACE]
    width = qkv.shape[1] // 3
    dim = LANES
    subs = ok.shape[0]
    size = qkv.shape[0] // subs
    scale = dim ** (-0.5)
    for j, g in enumerate((g0, g1, g2, g3)):
        gms[part(place ^ j, TOKENS), :] = dot(g[...], out_w[...], 1, 1).astype(bf16)
    acc[...] = jnp.zeros_like(acc)
    for sub in range(subs):
        mask = masks(size, scal[WIDE], ok, sub)
        here = pl.ds(sub * size, size)
        cs = pl.ds(sub * CTX, CTX)
        for h in range(width // dim):
            lq, lk, lv = (pl.ds(i * width + h * dim, dim) for i in range(3))
            lh, lhv = pl.ds(h * dim, dim), pl.ds(width + h * dim, dim)
            ck, cv = ckv[cs, lh], ckv[cs, lhv]
            q, gm = qkv[here, lq], gms[here, lh]
            probs = probabilities(q, ck, qkv, size, sub, lk, mask, scale)
            values = [cv] + [qkv[pl.ds(o * size, size), lv] for o in range(sub + 1)]
            keys = [ck] + [qkv[pl.ds(o * size, size), lk] for o in range(sub + 1)]
            grads = [dot(gm, v, 1, 1) for v in values]
            inner = sum(jnp.sum(p * g, axis=1, keepdims=True) for p, g in zip(probs, grads))
            scores = [(p * (g - inner)).astype(bf16) for p, g in zip(probs, grads)]
            grad_q = sum(dot(s, k, 1, 0) for s, k in zip(scores, keys))
            out_of_order(out, lq, (grad_q * scale).astype(bf16), sub, place)
            ctx[cs, lh] = (dot(scores[0], q, 0, 0) * scale).astype(bf16)
            ctx[cs, lhv] = dot(probs[0].astype(bf16), gm, 0, 0).astype(bf16)
            for o in range(sub + 1):
                there = pl.ds(o * size, size)
                acc[there, lh] += dot(scores[1 + o], q, 0, 0) * scale
                acc[there, lhv] += dot(probs[1 + o].astype(bf16), gm, 0, 0)
    for sub in range(subs):
        out_of_order(out, pl.ds(width, 2 * width), acc[pl.ds(sub * size, size), :].astype(bf16), sub, place)
    for j, x in enumerate((x0, x1, x2, x3)):
        for s in range(2):
            rows = channel_part(scal, s, place ^ j)
            x[:, pl.ds(s * LANES, LANES)] = dot(ctx[...], w[rows, pl.ds(width, 2 * width)], 1, 1).astype(bf16)


def lowered_back_kernel(scal, g, w, o0, o1, o2, o3):
    for j, out in enumerate((o0, o1, o2, o3)):
        out[...] = dot(g[pl.ds(j * TOKENS, TOKENS), :], w[...], 1, 1).astype(bf16)


def context_sum_kernel(scal, own, a, b, c, total, turned):
    value = ((wide(own) + wide(a)) + (wide(b) + wide(c))).astype(bf16)
    total[...] = value
    for s in range(2):
        turned[:, pl.ds((1 - s) * LANES, LANES)] = value[:, s * LANES : (s + 1) * LANES]


def attend_weights_kernel(scal, x0, x1, x2, x3, c0, c1, c2, c3, gqkv, gctx, mixed, g0, g1, g2, g3, send, keep, rows, acc, acc_out):
    place, core = scal[PLACE], scal[CORE]
    for j, x in enumerate((x0, x1, x2, x3)):
        rows[pl.ds(j * TOKENS, TOKENS), :] = x[...]
    width = gqkv.shape[1] // 3
    half = rows.shape[1] // 2
    for s in range(2):
        acc[pl.ds(s * half, half), :] = dot(rows[:, pl.ds(s * half, half)], gqkv[...], 0, 0)
    for j, c in enumerate((c0, c1, c2, c3)):
        for s in range(2):
            there = channel_part(scal, s, place ^ j)
            acc[there, pl.ds(width, 2 * width)] += dot(c[:, pl.ds(s * LANES, LANES)], gctx[...], 0, 0)
    size = acc.shape[0]
    for m in range(3):
        keep[pl.ds(m * size, size), :] = acc[:, pl.ds(2 * m * LANES, LANES)].astype(bf16)
        send[pl.ds(m * size, size), :] = acc[:, pl.ds((2 * m + 1) * LANES, LANES)].astype(bf16)
    for j, g in enumerate((g0, g1, g2, g3)):
        rows[pl.ds(j * TOKENS, TOKENS), :] = g[...]
    acc_out[...] = dot(mixed[...], rows[...], 0, 0)
    for s in range(2):
        head = core ^ scal[SPAN] ^ s
        for ref, side in ((keep, core), (send, 1 - core)):
            for i in range(2 * TP):
                there = pl.ds(3 * size + i * LANES + s * 64, 64)
                ref[there, :] = acc_out[part(head * 2 + side, 64), pl.ds(i * LANES, LANES)].astype(bf16)


def units_kernel(scal, c0, c1, c2, c3, u00, u01, u10, u11, own, d00, d01, d10, d11, up_w, down_w, ahead, rows):
    span, core, row = scal[SPAN], scal[CORE], scal[ROW]
    half = up_w.shape[0] // 2
    for j, k, ref in ((0, 0, u00), (0, 1, u01), (1, 0, u10), (1, 1, u11)):
        for n in range(2 * TP):
            for s in range(2):
                there = part((s * 2 + j) * 2 + (row ^ k), LANES)
                up_w[pl.ds(n * LANES, LANES), there] = ref[n, pl.ds(s * TOKENS, TOKENS), :]
    for j in range(2):
        down_w[part(span * 2 + j, UNITS), :] = own[part(core ^ j, UNITS), :]
    for j, k, ref in ((0, 0, d00), (0, 1, d01), (1, 0, d10), (1, 1, d11)):
        down_w[part(((1 - span) * 2 + j) * 2 + (row ^ k), LANES), :] = ref[...]
    for j, c in enumerate((c0, c1, c2, c3)):
        rows[pl.ds(j * TOKENS, TOKENS), :] = c[...]
    for i in range(4):
        tile = pl.ds(i * UNITS, UNITS)
        ahead[:, tile] = dot(rows[...], down_w[tile, :], 1, 1)


def gelu_parts(a):
    c = math.sqrt(2.0 / math.pi)
    t = jnp.tanh(c * (a + 0.044715 * a * a * a))
    half = 0.5 * (1.0 + t)
    return a * half, half + 0.5 * a * (1.0 - t * t) * c * (1.0 + 3 * 0.044715 * a * a)


def hidden_kernel(scal, n0, n1, n2, n3, up_w, ahead, o0, o1, o2, o3, h0, h1, p0, p1, rows, pre):
    for j, n in enumerate((n0, n1, n2, n3)):
        rows[pl.ds(j * TOKENS, TOKENS), :] = n[...]
    for i in range(4):
        s, j = divmod(i, 2)
        tile, lanes = pl.ds(i * UNITS, UNITS), pl.ds(s * UNITS, UNITS)
        act, slope = gelu_parts(dot(rows[...], up_w[:, tile], 1, 0))
        low = (ahead[:, tile] * slope).astype(bf16)
        (h0, h1)[j][:, lanes] = act.astype(bf16)
        (p0, p1)[j][:, lanes] = low
        pre[:, tile] = low
    for j, out in enumerate((o0, o1, o2, o3)):
        out[...] = dot(pre[pl.ds(j * TOKENS, TOKENS), :], up_w[...], 1, 1).astype(bf16)


def result_kernel(scal, h0, h1, down_w, o0, o1, o2, o3):
    for j, out in enumerate((o0, o1, o2, o3)):
        here = pl.ds(j * TOKENS, TOKENS)
        total = None
        for s in range(2):
            for k, h in enumerate((h0, h1)):
                term = dot(h[here, pl.ds(s * UNITS, UNITS)], down_w[pl.ds((2 * s + k) * UNITS, UNITS), :], 1, 0)
                total = term if total is None else total + term
        out[...] = total.astype(bf16)


def units_weights_kernel(scal, rows, cot, h0, h1, p0, p1, d_send, u_send, d_keep, u_keep):
    half = h0.shape[1]
    for h, p, down, up in ((h1, p1, d_send, u_send), (h0, p0, d_keep, u_keep)):
        for i in range(2):
            tile = pl.ds(i * UNITS, UNITS)
            down[tile, :] = dot(h[:, tile], cot[...], 0, 0).astype(bf16)
        for i in range(4):
            s, n = divmod(i, 2)
            there = (pl.ds(n * UNITS, UNITS), pl.ds(s * half, half))
            up[there] = dot(rows[:, pl.ds(i * UNITS, UNITS)], p[...], 0, 0).astype(bf16)


def units_one_kernel(scal, down, down_got, up, up_got, d_send, d_keep, u_send, u_keep):
    row = scal[ROW]
    half = up.shape[0]
    for s in range(2):
        for ref, side in ((d_keep, row), (d_send, 1 - row)):
            there = part(2 * s + side, LANES)
            ref[pl.ds(s * LANES, LANES), :] = (wide(down.at[there, :]) + wide(down_got.at[there, :])).astype(bf16)
        for n in range(2):
            for ref, side in ((u_keep, row), (u_send, 1 - row)):
                there = part(2 * (2 * n + s) + side, LANES)
                ref[:, pl.ds((2 * n + s) * LANES, LANES)] = (wide(up.at[:, there]) + wide(up_got.at[:, there])).astype(bf16)


def units_two_kernel(scal, down, down_got, up, up_got, d_send, d_keep, u_send, u_keep):
    for s, d_ref, u_ref in ((scal[SPAN], d_keep, u_keep), (1 - scal[SPAN], d_send, u_send)):
        there = part(s, LANES)
        d_ref[...] = (wide(down.at[there, :]) + wide(down_got.at[there, :])).astype(bf16)
        there = part(s, UNITS)
        u_ref[...] = (wide(up.at[:, there]) + wide(up_got.at[:, there])).astype(bf16)


def units_three_kernel(scal, up, up_got, x0, x1, x2, x3):
    for j, x in enumerate((x0, x1, x2, x3)):
        there = part(scal[PLACE] ^ j, LANES)
        x[...] = (wide(up.at[there, :]) + wide(up_got.at[there, :])).astype(bf16)


def units_four_kernel(scal, down, down_got, x0, x1, x2, x3, out):
    out[0:LANES, :] = (wide(down) + wide(down_got)).astype(bf16)
    for j, x in enumerate((x0, x1, x2, x3)):
        out[LANES : 2 * LANES, part(scal[PLACE] ^ j, UNITS)] = x[...]


def units_home_kernel(scal, b00, b01, b10, b11, up, down):
    row, core = scal[ROW], scal[CORE]
    for j, k, ref in ((0, 0, b00), (0, 1, b01), (1, 0, b10), (1, 1, b11)):
        quarter = (core ^ j) * 2 + (row ^ k)
        down[part(quarter, LANES), :] = ref[0:LANES, :].astype(f32)
        for rank in range(TP):
            for s in range(2):
                there = (s * TP + rank) * 4 + quarter
                up[:, part(there, LANES)] = ref[LANES : 2 * LANES, pl.ds(rank * UNITS + s * LANES, LANES)].astype(f32)


def heads_one_kernel(scal, own, got, send, keep):
    row = scal[ROW]
    for n in range(own.shape[0] // 64 // 2):
        for ref, side in ((keep, row), (send, 1 - row)):
            size = 64 if n < 3 * 2 * TP else 32
            pairs = 1 if size == 64 else 2
            for i in range(pairs):
                at = part((2 * n + side) if pairs == 1 else (4 * n + 2 * i + side), size)
                there = pl.ds(n * 64 + i * 32, size)
                ref[there, :] = (wide(own.at[at, :]) + wide(got.at[at, :])).astype(bf16)


def heads_two_kernel(scal, own, got, send, keep):
    quarter = TP * 64
    for m in range(3):
        for ref, s in ((keep, scal[SPAN]), (send, 1 - scal[SPAN])):
            at = part(2 * m + s, quarter)
            ref[pl.ds(m * quarter, quarter), :] = (wide(own.at[at, :]) + wide(got.at[at, :])).astype(bf16)
    for i in range(2 * TP):
        for ref, s in ((keep, 0), (send, 1)):
            at = pl.ds(6 * quarter + i * 64 + s * 32, 32)
            ref[pl.ds(3 * quarter + i * 32, 32), :] = (wide(own.at[at, :]) + wide(got.at[at, :])).astype(bf16)


def heads_three_kernel(scal, own, got, low, x0, x1, x2, x3):
    quarter = TP * 64
    at = pl.ds(3 * quarter, low.shape[0])
    low[...] = (wide(own.at[at, :]) + wide(got.at[at, :])).astype(bf16)
    for j, x in enumerate((x0, x1, x2, x3)):
        for m in range(3):
            at = part(m * TP + (scal[PLACE] ^ j), 64)
            x[:, pl.ds(m * LANES, LANES)] = (wide(own.at[at, :]) + wide(got.at[at, :])).astype(bf16)


def heads_four_kernel(scal, low, x0, x1, x2, x3, out):
    width = x0.shape[1]
    for j, x in enumerate((x0, x1, x2, x3)):
        out[:, part(scal[PLACE] ^ j, width)] = x[...]
    for i in range(2 * TP):
        there = (pl.ds(i // TP * 32, 32), pl.ds(TP * width + i % TP * LANES, LANES))
        out[there] = low[pl.ds(i * 32, 32), :]


def heads_home_kernel(scal, b00, b01, b10, b11, gq, gk, gv, go):
    row, core = scal[ROW], scal[CORE]
    width = 3 * LANES
    half = go.shape[1] // 2
    for j, k, ref in ((0, 0, b00), (0, 1, b01), (1, 0, b10), (1, 1, b11)):
        for rank in range(TP):
            for m, out in enumerate((gq, gk, gv)):
                lanes = pl.ds(rank * width + m * LANES, LANES)
                out[part(row ^ k, 64), part((core ^ j) * TP + rank, LANES)] = ref[:, lanes].astype(f32)
        there = part((core ^ j) * 2 + (row ^ k), 32)
        for i in range(2):
            go[there, pl.ds(i * half, half)] = ref[pl.ds(i * 32, 32), pl.ds(TP * width, half)].astype(f32)


def swap(x, axis):
    return lax.ppermute(x, axis, SWAP)


def across(x, d):
    return lax.ppermute(x, "tp", [(i, i ^ d) for i in range(TP)])


def gathered(x):
    return [x] + [across(x, d) for d in range(1, TP)]


def traded(parts):
    return [parts[0]] + [across(parts[d], d) for d in range(1, TP)]


def traded_all(x):
    return lax.all_to_all(x, ("span", "tp"), split_axis=0, concat_axis=0, tiled=True)


def hold_until(x, spent, *others):
    x, *others = lax.optimization_barrier((x,) + others)
    spent.extend(others)
    return x


def by_spans(
    activations,
    cotangent,
    block_sizes,
    context_back,
    first_gain,
    first_bias,
    w_query,
    w_key,
    w_value,
    w_out,
    second_gain,
    second_bias,
    w_up,
    w_down,
    decay_rate,
    input_map,
    output_map,
    step_size,
    skip_gain,
):
    span, place, row, core = (lax.axis_index(a).astype(jnp.int32) for a in ("span", "tp", "y", "core"))
    activations, cotangent, width = activations[0], cotangent[0], block_sizes[0]
    model = activations.shape[1]
    rows = TP * TOKENS
    subs = rows // BLK_A
    ctx_rows = subs * CTX
    mine = 2 * LANES
    half = model // 2
    scal = jnp.stack([span, place, row, core, (width > BLK_A).astype(jnp.int32)])
    tile = lambda n, m, kind=bf16: ((n, m), kind)
    block, piece = tile(TOKENS, model), tile(TOKENS, mine)

    shares, out_part, down_part = call(
        share_kernel,
        [((2 * TP, 448, LANES), bf16), tile(64, model), block],
        *(scal, w_query, w_key, w_value, w_out, w_down, w_up),
        scratch=[pltpu.SemaphoreType.DMA((4 * TP + 2,))],
        loose=(4, 5, 6),
        limit=56,
    )
    row_of = lambda v: v.reshape(1, LANES)
    (pack,) = call(
        pack_kernel,
        [tile(56, LANES, f32)],
        *(scal, decay_rate.T, input_map.T, output_map.T, row_of(step_size), row_of(skip_gain)),
        *(row_of(v) for v in (first_gain, first_bias, second_gain, second_bias)),
        scratch=[pltpu.VMEM((4, 1, LANES), bf16), pltpu.SemaphoreType.DMA((9,))],
        loose=range(1, 10),
        after=(out_part,),
        limit=60,
    )
    pack_far = swap(pack, "span")
    (vec,) = call(lines_kernel, [tile(16, LANES, f32)], scal, pack, pack_far)
    vecs = gathered(vec)
    spent = []

    def starts_of(which):
        begin = which * rows + jnp.arange(subs, dtype=jnp.int32) * BLK_A
        return begin // width * width

    own_spots = ((starts_of(span) - span * rows)[:, None] - context_back[None, :]).reshape(ctx_rows, 1)
    next_spots = ((starts_of(span + 1) - span * rows)[:, None] - context_back[None, :]).reshape(ctx_rows, 1)
    valid = (starts_of(span)[:, None] >= context_back[None, :]).astype(f32)

    shares = traded_all(hold_until(shares, spent, pack_far))

    low, vec = call(norm_one_kernel, [block, tile(8, model, f32)], scal, activations, *vecs)
    lowered = gathered(low)
    shares = [shares, swap(hold_until(shares, spent, low), "y")]
    down_far, out_far = swap(hold_until(down_part, spent, low), "span"), swap(hold_until(out_part, spent, low), "span")
    down_beside = swap(down_far, "y")
    hold, channels = pltpu.VMEM((STATES, CHUNKS, LANES), f32), pltpu.VMEM((2, rows, LANES), f32)
    channel_out, kept = ((2, rows, LANES), f32), ((2, 2, STATES, CHUNKS, LANES), f32)
    low_channels = pltpu.VMEM((rows, mine), bf16)
    local, to_next, ends, decay, mix, kept = call(
        scan_kernel,
        [channel_out, tile(ctx_rows, mine), tile(2 * STATES, mine, f32), tile(STATES, mine, f32), tile(STATES, mine, f32), kept],
        *(scal, *lowered, pack, pack_far, next_spots),
        scratch=[channels, low_channels, hold, hold, hold],
    )
    forward = [(0, 1)]
    begin, from_last = lax.ppermute(ends, "span", forward), lax.ppermute(to_next, "span", forward)
    cot_parts = gathered(hold_until(cotangent, spent, ends))
    (context,) = call(
        carry_kernel,
        [tile(ctx_rows, mine)],
        *(scal, local, decay, mix, begin, from_last, own_spots),
        after=(down_far,),
        scratch=[hold, channels, low_channels],
    )
    shares += [swap(hold_until(w, spent, ends), "core") for w in shares]
    before_qkv = context
    context = gathered(context)
    out_parts = [w_out, out_far, swap(hold_until(out_far, spent, ends), "core")]
    down_parts = [down_far, down_beside]
    qkv_w, qkv = call(qkv_kernel, [tile(model, 3 * mine), tile(rows, 3 * mine)], scal, *lowered, *shares, after=(before_qkv,))

    down_parts += [swap(hold_until(d, spent, qkv), "core") for d in down_parts]

    mixed, ctx_kv, out_w, *branch = call(
        attend_kernel,
        [tile(rows, mine), tile(ctx_rows, 2 * mine), tile(mine, model)] + [block] * TP,
        *(scal, valid, qkv, *context, qkv_w, *out_parts),
        after=tuple(cot_parts[1:]),
    )
    first_sum, low = call(norm_two_kernel, [tile(TOKENS, model, f32), block], scal, activations, *traded(branch), vec)

    square = tile(model, model)
    up_w, down_w, ahead, cot_span = call(
        units_kernel, [square, square, tile(rows, model, f32), tile(rows, model)], scal, *cot_parts, *shares, w_down, *down_parts
    )
    normal = gathered(low)
    side = tile(rows, half)
    *grad_norm, h0, h1, p0, p1, normal_span = call(
        hidden_kernel,
        [block] * TP + [side] * 4 + [tile(rows, model)],
        *(scal, *normal, up_w, ahead),
        scratch=[pltpu.VMEM((rows, model), bf16)],
    )
    grad_norm = traded(grad_norm)
    flat = tile(half, model)
    down_send, up_send, down_keep, up_keep = call(
        units_weights_kernel,
        [flat] * 4,
        *(scal, normal_span, cot_span, h0, h1, p0, p1),
    )
    quarter = tile(half // 2, model)
    d_send, d_keep, u_send, u_keep = call(
        units_one_kernel,
        [quarter, quarter, tile(half, half), tile(half, half)],
        *(scal, down_keep, swap(down_send, "core"), up_keep, swap(up_send, "core")),
    )
    grad_first, low, lines_two = call(
        norm_two_back_kernel,
        [tile(TOKENS, model, f32), block, tile(8, model, f32)],
        *(scal, first_sum, *grad_norm, cotangent, vec),
    )
    branch_back = gathered(low)
    result_parts = call(result_kernel, [block] * TP, scal, h0, h1, down_w, after=(low,))
    d_send, d_keep, u_send, u_keep = call(
        units_two_kernel,
        [block, block, tile(half, mine), tile(half, mine)],
        *(scal, d_keep, swap(d_send, "y"), u_keep, swap(u_send, "y")),
    )

    grad_qkv, grad_ctx, *back = call(
        attend_back_kernel,
        [tile(rows, 3 * mine), tile(ctx_rows, 2 * mine)] + [tile(ctx_rows, mine)] * TP,
        *(scal, valid, qkv, ctx_kv, *branch_back, out_w, qkv_w),
        after=(result_parts[0],),
        scratch=[pltpu.VMEM((rows, mine), bf16), pltpu.VMEM((rows, 2 * mine), f32)],
    )
    back = traded(back)
    grad_context, turned = call(context_sum_kernel, [tile(ctx_rows, mine)] * 2, scal, *back, after=(u_send,))
    from_next = lax.ppermute(turned, "span", [(1, 0)])
    d_send = hold_until(d_send, spent, from_next)
    heads = tile(4 * model, LANES)
    heads_send, heads_keep = call(
        attend_weights_kernel,
        [heads] * 2,
        *(scal, *lowered, *context, grad_qkv, grad_ctx, mixed, *branch_back),
        scratch=[pltpu.VMEM((rows, model), bf16), pltpu.VMEM((model, 3 * mine), f32), pltpu.VMEM((mine, model), f32)],
        after=(turned,),
    )
    heads = tile(2 * model, LANES)
    heads_send, heads_keep = call(
        heads_one_kernel, [heads] * 2, scal, heads_keep, swap(heads_send, "core")
    )
    grad_lowered = traded(call(lowered_back_kernel, [block] * TP, scal, grad_qkv, qkv_w, after=(turned,)))

    u_parts = call(units_three_kernel, [piece] * TP, scal, u_keep, swap(hold_until(u_send, spent, grad_ctx), "span"))

    grad_states, grad_local, grad_ends = call(
        scan_back_kernel,
        [channel_out, channel_out, tile(STATES, mine, f32)],
        *(scal, grad_context, from_next, own_spots, next_spots, pack, pack_far, decay, mix),
        scratch=[hold, hold],
        after=(heads_send,),
    )
    grad_begin = lax.ppermute(grad_ends, "span", [(1, 0)])
    heads = tile(model, LANES)
    heads_send, heads_keep = call(heads_two_kernel, [heads] * 2, scal, heads_keep, swap(hold_until(heads_send, spent, from_next), "y"), after=(grad_begin,))
    (sums,) = call(
        sums_kernel,
        [tile(40, mine, f32)],
        *(scal, *lowered, grad_states, decay, begin, kept),
        scratch=[channels, hold, hold],
        after=(grad_ends,),
    )
    grad_conv = call(
        carry_back_kernel,
        [piece] * TP,
        *(scal, grad_local, decay, mix, grad_begin),
        scratch=[hold, channels],
        after=(sums, *grad_lowered[1:],),
    )
    grad_conv = traded(grad_conv)
    grad_inputs, lines = call(
        last_kernel,
        [tile(TOKENS, model, f32), ((2 * TP, 8, LANES), f32)],
        *(scal, activations, vec, grad_first, *grad_lowered, *grad_conv, lines_two),
        scratch=[pltpu.VMEM((TOKENS, model), f32)],
        after=(u_parts[0], heads_send,),
    )
    (u_all,) = call(units_four_kernel, [tile(2 * LANES, model)], scal, d_keep, swap(d_send, "span"), *traded([hold_until(u, spent, grad_begin) for u in u_parts]))
    out_low, *q_parts = call(
        heads_three_kernel,
        [tile(2 * LANES, LANES)] + [tile(64, 3 * LANES)] * TP,
        *(scal, heads_keep, swap(heads_send, "span")),
    )
    u_beside = swap(u_all, "y")
    result_parts = [hold_until(r, spent, lines) for r in result_parts]
    result_parts = traded(result_parts)
    result = first_sum + sum(x.astype(f32) for x in result_parts)
    (q_all,) = call(heads_four_kernel, [tile(64, 2 * model)], scal, out_low, *traded(q_parts))
    q_beside = swap(q_all, "y")
    grad_up, grad_down = call(
        units_home_kernel,
        [tile(LANES, 4 * model, f32), tile(half, model, f32)],
        *(scal, u_all, u_beside, swap(u_all, "core"), swap(u_beside, "core")),
        after=(q_all,),
    )
    home = tile(LANES, model, f32)
    grad_query, grad_key, grad_value, grad_out = call(
        heads_home_kernel, [home] * 4, scal, q_all, q_beside, swap(q_all, "core"), swap(q_beside, "core"), after=tuple(spent)
    )

    lines = traded_all(lines)
    sums = sums[:, :LANES] + swap(sums[:, LANES:], "span")
    (small,) = call(lines_sum_kernel, [tile(48, LANES, f32)], scal, lines, sums, after=(out_low,))
    small = small + swap(small, "y")
    small = small + swap(small, "core")
    lines, sums = small[:8], small[8:]
    grad_mix, grad_skip = sums[:STATES].T, sums[2 * STATES]
    step = step_size[:, None]
    grad_speed = -(output_map * input_map * step) * sums[STATES : 2 * STATES].T
    grad_step = jnp.sum(grad_mix * output_map * input_map + grad_speed * decay_rate, axis=1)
    return (
        result[None],
        grad_inputs[None],
        lines[0],
        lines[1],
        grad_query,
        grad_key,
        grad_value,
        grad_out,
        lines[2],
        lines[3],
        grad_up,
        grad_down,
        grad_speed * step,
        grad_mix * output_map * step,
        grad_mix * input_map * step,
        grad_step,
        grad_skip,
    )


def from_behind(x, axis, by):
    peers = lax.axis_size(axis)
    pairs = [(i, i + by) for i in range(peers) if 0 <= i + by < peers]
    return lax.ppermute(x, axis, pairs)


def smooth_gate(values):
    return jax.nn.gelu(values, approximate=True)


def ssm_kernel(decay_rate, input_map, output_map, step_size, length):
    offsets = jnp.arange(length).astype(jnp.float32)
    weight = output_map * input_map * step_size[:, None]
    decay_speed = step_size[:, None] * decay_rate
    total_sum = jnp.zeros((decay_rate.shape[0], length), jnp.float32)
    for state_index in range(decay_rate.shape[1]):
        total_sum = total_sum + weight[:, state_index : state_index + 1] * jnp.exp(
            -decay_speed[:, state_index : state_index + 1] * offsets[None, :]
        )
    return total_sum


def phase_table(row_count, col_count, period):
    first_ids = jnp.arange(row_count, dtype=jnp.int32)[:, None]
    second_ids = jnp.arange(col_count, dtype=jnp.int32)[None, :]
    angles = (first_ids * second_ids % period).astype(jnp.float32) * (2.0 * math.pi / period)
    return (jnp.cos(angles), jnp.sin(angles))


def exact_einsum(form, left_side, right_side):
    return jnp.einsum(form, left_side, right_side, precision=lax.Precision.HIGHEST)


def spectrum(signal, low_len, high_len):
    row_count = signal.shape[0]
    total_len = low_len * high_len
    grid_rows = signal.reshape(row_count, high_len, low_len)
    cos_high, sin_high = phase_table(high_len, high_len, high_len)
    real_part = exact_einsum("rmn,mk->rkn", grid_rows, cos_high)
    imag_part = -exact_einsum("rmn,mk->rkn", grid_rows, sin_high)
    cos_twist, sin_twist = phase_table(high_len, low_len, total_len)
    real_part, imag_part = (
        real_part * cos_twist + imag_part * sin_twist,
        imag_part * cos_twist - real_part * sin_twist,
    )
    cos_low, sin_low = phase_table(low_len, low_len, low_len)
    out_real = exact_einsum("rkn,nj->rkj", real_part, cos_low) + exact_einsum(
        "rkn,nj->rkj", imag_part, sin_low
    )
    out_imag = exact_einsum("rkn,nj->rkj", imag_part, cos_low) - exact_einsum(
        "rkn,nj->rkj", real_part, sin_low
    )
    return (out_real, out_imag)


def signal_of(real_part, imag_part, low_len, high_len, keep_len):
    row_count = real_part.shape[0]
    total_len = low_len * high_len
    cos_low, sin_low = phase_table(low_len, low_len, low_len)
    mid_real = exact_einsum("rkj,nj->rkn", real_part, cos_low) - exact_einsum(
        "rkj,nj->rkn", imag_part, sin_low
    )
    mid_imag = exact_einsum("rkj,nj->rkn", real_part, sin_low) + exact_einsum(
        "rkj,nj->rkn", imag_part, cos_low
    )
    cos_twist, sin_twist = phase_table(high_len, low_len, total_len)
    turn_real = mid_real * cos_twist - mid_imag * sin_twist
    turn_imag = mid_real * sin_twist + mid_imag * cos_twist
    cos_high, sin_high = phase_table(high_len, high_len, high_len)
    grid_rows = exact_einsum("rkn,km->rmn", turn_real, cos_high) - exact_einsum(
        "rkn,km->rmn", turn_imag, sin_high
    )
    return grid_rows.reshape(row_count, total_len)[:, :keep_len] / total_len


def padded(values):
    return jnp.concatenate([values, jnp.zeros_like(values)], axis=-1)


def norm_parts(values):
    center = values - jnp.mean(values, axis=-1, keepdims=True)
    inverse_dev = lax.rsqrt(jnp.mean(center * center, axis=-1, keepdims=True) + 1e-05)
    return (center * inverse_dev, inverse_dev)


def plain_norm_back(grad_values, scaled, inverse_dev, gain_vector):
    weighted = grad_values * gain_vector.astype(jnp.float32)
    return inverse_dev * (
        weighted
        - jnp.mean(weighted, axis=-1, keepdims=True)
        - scaled * jnp.mean(weighted * scaled, axis=-1, keepdims=True)
    )


def matmul(left_side, right_side):
    return jnp.einsum("...i,ij->...j", left_side, right_side, preferred_element_type=jnp.float32)


def matmul_t(left_side, right_side):
    return jnp.einsum("...j,ij->...i", left_side, right_side, preferred_element_type=jnp.float32)


def outer_sum(left_side, right_side):
    return jnp.einsum(
        "ri,rj->ij",
        left_side.reshape(-1, left_side.shape[-1]),
        right_side.reshape(-1, right_side.shape[-1]),
        preferred_element_type=jnp.float32,
    )


def take_rows(rows_table, row_ids):
    return jnp.take(rows_table, row_ids, axis=0)


def plain(
    activations,
    cotangent,
    block_sizes,
    context_back,
    first_gain,
    first_bias,
    w_query,
    w_key,
    w_value,
    w_out,
    second_gain,
    second_bias,
    w_up,
    w_down,
    decay_rate,
    input_map,
    output_map,
    step_size,
    skip_gain,
):
    seq_ways = lax.axis_size("seq")
    place = lax.axis_index("seq")
    seq_count, tokens, model_width = activations.shape
    channels = decay_rate.shape[0]
    length = tokens * seq_ways
    sub_len = min(BLK_A, tokens)
    sub_count = tokens // sub_len
    shift_count = max(BLK_B // tokens - 1, 0)
    head_dim = model_width // HEADS
    score_scale = head_dim ** (-0.5)
    per_dev = sub_count * CTX
    low_len = 2 * seq_ways
    (
        gain_one,
        bias_one,
        query_full,
        key_full,
        value_full,
        out_full,
        gain_two,
        bias_two,
        up_full,
        down_full,
    ) = (
        lax.all_gather(first_gain, "seq", axis=0, tiled=True),
        lax.all_gather(first_bias, "seq", axis=0, tiled=True),
        lax.all_gather(w_query, "seq", axis=0, tiled=True),
        lax.all_gather(w_key, "seq", axis=0, tiled=True),
        lax.all_gather(w_value, "seq", axis=0, tiled=True),
        lax.all_gather(w_out, "seq", axis=0, tiled=True),
        lax.all_gather(second_gain, "seq", axis=0, tiled=True),
        lax.all_gather(second_bias, "seq", axis=0, tiled=True),
        lax.all_gather(w_up, "seq", axis=0, tiled=True),
        lax.all_gather(w_down, "seq", axis=0, tiled=True),
    )
    scaled_one, inverse_one = norm_parts(activations)
    lowered = (scaled_one * gain_one.astype(jnp.float32) + bias_one.astype(jnp.float32)).astype(
        jnp.bfloat16
    )
    by_channel = lax.all_to_all(
        jnp.swapaxes(lowered, 1, 2), "seq", split_axis=1, concat_axis=2, tiled=True
    )
    channel_in = by_channel.astype(jnp.float32)
    kernel, kernel_pull = jax.vjp(
        lambda a, b, c, e: ssm_kernel(a, b, c, e, length),
        decay_rate,
        input_map,
        output_map,
        step_size,
    )
    input_real, input_imag = spectrum(padded(channel_in.reshape(-1, length)), low_len, tokens)
    input_real = input_real.reshape(seq_count, channels, tokens, low_len)
    input_imag = input_imag.reshape(seq_count, channels, tokens, low_len)
    kernel_real, kernel_imag = spectrum(padded(kernel), low_len, tokens)
    conv_real = input_real * kernel_real - input_imag * kernel_imag
    conv_imag = input_real * kernel_imag + input_imag * kernel_real
    convolved = signal_of(
        conv_real.reshape(-1, tokens, low_len),
        conv_imag.reshape(-1, tokens, low_len),
        low_len,
        tokens,
        length,
    )
    states = convolved.reshape(seq_count, channels, length) + skip_gain[None, :, None] * channel_in
    targets = (
        jnp.arange(seq_ways, dtype=jnp.int32)[:, None] * tokens
        + jnp.arange(sub_count, dtype=jnp.int32)[None, :] * sub_len
    )
    sizes_three = block_sizes[:, None, None]
    block_start = targets[None] // sizes_three * sizes_three
    positions = block_start[..., None] - context_back
    valid_all = positions >= 0
    picks = jnp.maximum(positions, 0).reshape(seq_count, -1)
    position_major = jnp.swapaxes(states, 1, 2)
    picked = jax.vmap(take_rows)(position_major, picks)
    picked = jnp.where(valid_all.reshape(seq_count, -1, 1), picked, 0.0).astype(jnp.bfloat16)
    picked = jnp.swapaxes(picked, 1, 2)
    arrived = lax.all_to_all(
        picked.reshape(seq_count, channels, seq_ways, per_dev),
        "seq",
        split_axis=2,
        concat_axis=1,
        tiled=True,
    )
    context = jnp.swapaxes(arrived.reshape(seq_count, model_width, per_dev), 1, 2)
    own_valid = lax.dynamic_index_in_dim(valid_all, place, axis=1, keepdims=False).reshape(
        seq_count, per_dev
    )
    queries = matmul(lowered, query_full).astype(jnp.bfloat16)
    keys_own = matmul(lowered, key_full).astype(jnp.bfloat16)
    values_own = matmul(lowered, value_full).astype(jnp.bfloat16)
    ctx_keys = matmul(context, key_full).astype(jnp.bfloat16)
    ctx_values = matmul(context, value_full).astype(jnp.bfloat16)
    key_parts = [ctx_keys]
    value_parts = [ctx_values]
    key_places = []
    token_ids = jnp.arange(tokens, dtype=jnp.int32)
    for distance in range(shift_count, 0, -1):
        far_keys, far_values = from_behind((keys_own, values_own), "seq", distance)
        key_parts.append(far_keys)
        value_parts.append(far_values)
        key_places.append((place - distance) * tokens + token_ids)
    key_parts.append(keys_own)
    value_parts.append(values_own)
    key_places.append(place * tokens + token_ids)
    all_keys = jnp.concatenate(key_parts, axis=1)
    all_values = jnp.concatenate(value_parts, axis=1)
    key_pos = jnp.concatenate(key_places)
    query_pos = place * tokens + token_ids
    same_block = key_pos[None, None, :] // sizes_three == query_pos[None, :, None] // sizes_three
    causal = key_pos[None, None, :] <= query_pos[None, :, None]
    ctx_allowed = (
        (token_ids // sub_len)[:, None] == (jnp.arange(per_dev, dtype=jnp.int32) // CTX)[None, :]
    )[None] & own_valid[:, None, :]
    allowed = jnp.concatenate([ctx_allowed, same_block & causal], axis=2)

    def split_heads(values):
        return values.reshape(values.shape[0], values.shape[1], HEADS, head_dim)

    def scores_of():
        raw_scores = (
            jnp.einsum(
                "sqhd,skhd->shqk",
                split_heads(queries),
                split_heads(all_keys),
                preferred_element_type=jnp.float32,
            )
            * score_scale
        )
        return jnp.where(allowed[:, None], raw_scores, -1e30)

    scores = scores_of()
    row_top = jnp.max(scores, axis=-1, keepdims=True)
    log_total = row_top + jnp.log(jnp.sum(jnp.exp(scores - row_top), axis=-1, keepdims=True))
    probs_low = jnp.exp(scores - log_total).astype(jnp.bfloat16)
    attended = jnp.einsum(
        "shqk,skhd->sqhd", probs_low, split_heads(all_values), preferred_element_type=jnp.float32
    )
    mixed_out = attended.reshape(seq_count, tokens, model_width).astype(jnp.bfloat16)
    first_sum = activations + matmul(mixed_out, out_full)
    scaled_two, inverse_two = norm_parts(first_sum)
    normal_two = (scaled_two * gain_two.astype(jnp.float32) + bias_two.astype(jnp.float32)).astype(
        jnp.bfloat16
    )
    pre_gate = matmul(normal_two, up_full)
    hidden, gate_pull = jax.vjp(smooth_gate, pre_gate)
    hidden_low = hidden.astype(jnp.bfloat16)
    result = first_sum + matmul(hidden_low, down_full)
    grad_down = outer_sum(hidden_low, cotangent)
    grad_hidden = matmul_t(cotangent, down_full)
    grad_pre = gate_pull(grad_hidden)[0].astype(jnp.bfloat16)
    grad_up = outer_sum(normal_two, grad_pre)
    grad_norm_two = matmul_t(grad_pre, up_full)
    grad_gain_two = jnp.sum(grad_norm_two * scaled_two, axis=(0, 1))
    grad_bias_two = jnp.sum(grad_norm_two, axis=(0, 1))
    grad_first = cotangent.astype(jnp.float32) + plain_norm_back(
        grad_norm_two, scaled_two, inverse_two, gain_two
    )
    grad_branch = grad_first.astype(jnp.bfloat16)
    grad_out = outer_sum(mixed_out, grad_branch)
    grad_mixed = split_heads(matmul_t(grad_branch, out_full).astype(jnp.bfloat16))
    scores = scores_of()
    probabilities = jnp.exp(scores - log_total)
    probs_low = probabilities.astype(jnp.bfloat16)
    grad_probs = jnp.einsum(
        "sqhd,skhd->shqk", grad_mixed, split_heads(all_values), preferred_element_type=jnp.float32
    )
    grad_all_values = jnp.einsum(
        "shqk,sqhd->skhd", probs_low, grad_mixed, preferred_element_type=jnp.float32
    )
    grad_scores = (
        probabilities * (grad_probs - jnp.sum(probabilities * grad_probs, axis=-1, keepdims=True))
    ).astype(jnp.bfloat16)
    grad_queries = (
        jnp.einsum(
            "shqk,skhd->sqhd",
            grad_scores,
            split_heads(all_keys),
            preferred_element_type=jnp.float32,
        )
        * score_scale
    )
    grad_queries = grad_queries.reshape(seq_count, tokens, model_width).astype(jnp.bfloat16)
    grad_all_keys = (
        jnp.einsum(
            "shqk,sqhd->skhd", grad_scores, split_heads(queries), preferred_element_type=jnp.float32
        )
        * score_scale
    )
    grad_all_keys = grad_all_keys.reshape(seq_count, -1, model_width)
    grad_all_values = grad_all_values.reshape(seq_count, -1, model_width)
    grad_ctx_keys = grad_all_keys[:, :per_dev]
    grad_ctx_values = grad_all_values[:, :per_dev]
    grad_keys = grad_all_keys[:, -tokens:]
    grad_values = grad_all_values[:, -tokens:]
    for distance in range(shift_count, 0, -1):
        begin = per_dev + (shift_count - distance) * tokens
        back_keys, back_values = (
            from_behind(
                grad_all_keys[:, begin : begin + tokens].astype(jnp.bfloat16), "seq", -distance
            ).astype(jnp.float32),
            from_behind(
                grad_all_values[:, begin : begin + tokens].astype(jnp.bfloat16), "seq", -distance
            ).astype(jnp.float32),
        )
        grad_keys = grad_keys + back_keys
        grad_values = grad_values + back_values
    grad_keys_low = grad_keys.astype(jnp.bfloat16)
    grad_values_low = grad_values.astype(jnp.bfloat16)
    context_wide = context.astype(jnp.float32)
    grad_query_w = outer_sum(lowered, grad_queries)
    grad_key_w = outer_sum(lowered, grad_keys_low) + outer_sum(context_wide, grad_ctx_keys)
    grad_value_w = outer_sum(lowered, grad_values_low) + outer_sum(context_wide, grad_ctx_values)
    grad_normal_one = (
        matmul_t(grad_queries, query_full)
        + matmul_t(grad_keys_low, key_full)
        + matmul_t(grad_values_low, value_full)
    )
    grad_context = matmul_t(grad_ctx_keys, key_full) + matmul_t(grad_ctx_values, value_full)
    sent_back = jnp.swapaxes(grad_context, 1, 2).reshape(seq_count, model_width, 1, per_dev)
    returned = lax.all_to_all(
        sent_back.astype(jnp.bfloat16), "seq", split_axis=1, concat_axis=2, tiled=True
    ).astype(sent_back.dtype)
    returned = jnp.where(
        valid_all.reshape(seq_count, 1, -1), returned.reshape(seq_count, channels, -1), 0.0
    )
    segment_ids = (jnp.arange(seq_count, dtype=jnp.int32)[:, None] * length + picks).reshape(-1)
    flat_rows = jnp.swapaxes(returned, 1, 2).reshape(-1, channels)
    grad_states = jax.ops.segment_sum(flat_rows, segment_ids, num_segments=seq_count * length)
    grad_states = jnp.swapaxes(grad_states.reshape(seq_count, length, channels), 1, 2)
    grad_real, grad_imag = spectrum(padded(grad_states.reshape(-1, length)), low_len, tokens)
    grad_real = grad_real.reshape(seq_count, channels, tokens, low_len)
    grad_imag = grad_imag.reshape(seq_count, channels, tokens, low_len)
    back_real = grad_real * kernel_real + grad_imag * kernel_imag
    back_imag = grad_imag * kernel_real - grad_real * kernel_imag
    grad_conv = signal_of(
        back_real.reshape(-1, tokens, low_len),
        back_imag.reshape(-1, tokens, low_len),
        low_len,
        tokens,
        length,
    )
    grad_conv = grad_conv.reshape(seq_count, channels, length)
    corr_real = jnp.sum(grad_real * input_real + grad_imag * input_imag, axis=0)
    corr_imag = jnp.sum(grad_imag * input_real - grad_real * input_imag, axis=0)
    grad_kernel = signal_of(corr_real, corr_imag, low_len, tokens, length)
    grad_rate, grad_in_map, grad_out_map, grad_step = kernel_pull(grad_kernel)
    grad_skip = jnp.sum(grad_states * channel_in, axis=(0, 2))
    grad_channel = grad_conv + skip_gain[None, :, None] * grad_states
    back_tokens = lax.all_to_all(
        grad_channel.astype(jnp.bfloat16), "seq", split_axis=2, concat_axis=1, tiled=True
    ).astype(grad_channel.dtype)
    grad_normal_one = grad_normal_one + jnp.swapaxes(back_tokens, 1, 2)
    grad_gain_one = jnp.sum(grad_normal_one * scaled_one, axis=(0, 1))
    grad_bias_one = jnp.sum(grad_normal_one, axis=(0, 1))
    grad_inputs = grad_first + plain_norm_back(grad_normal_one, scaled_one, inverse_one, gain_one)
    shares = (
        lax.psum_scatter(
            grad_gain_one.astype(jnp.bfloat16), "seq", scatter_dimension=0, tiled=True
        ).astype(jnp.float32),
        lax.psum_scatter(
            grad_bias_one.astype(jnp.bfloat16), "seq", scatter_dimension=0, tiled=True
        ).astype(jnp.float32),
        lax.psum_scatter(
            grad_query_w.astype(jnp.bfloat16), "seq", scatter_dimension=0, tiled=True
        ).astype(jnp.float32),
        lax.psum_scatter(
            grad_key_w.astype(jnp.bfloat16), "seq", scatter_dimension=0, tiled=True
        ).astype(jnp.float32),
        lax.psum_scatter(
            grad_value_w.astype(jnp.bfloat16), "seq", scatter_dimension=0, tiled=True
        ).astype(jnp.float32),
        lax.psum_scatter(
            grad_out.astype(jnp.bfloat16), "seq", scatter_dimension=0, tiled=True
        ).astype(jnp.float32),
        lax.psum_scatter(
            grad_gain_two.astype(jnp.bfloat16), "seq", scatter_dimension=0, tiled=True
        ).astype(jnp.float32),
        lax.psum_scatter(
            grad_bias_two.astype(jnp.bfloat16), "seq", scatter_dimension=0, tiled=True
        ).astype(jnp.float32),
        lax.psum_scatter(
            grad_up.astype(jnp.bfloat16), "seq", scatter_dimension=0, tiled=True
        ).astype(jnp.float32),
        lax.psum_scatter(
            grad_down.astype(jnp.bfloat16), "seq", scatter_dimension=0, tiled=True
        ).astype(jnp.float32),
    )
    summed = (
        lax.psum(shares[0].astype(jnp.bfloat16), "dp").astype(jnp.float32),
        lax.psum(shares[1].astype(jnp.bfloat16), "dp").astype(jnp.float32),
        lax.psum(shares[2].astype(jnp.bfloat16), "dp").astype(jnp.float32),
        lax.psum(shares[3].astype(jnp.bfloat16), "dp").astype(jnp.float32),
        lax.psum(shares[4].astype(jnp.bfloat16), "dp").astype(jnp.float32),
        lax.psum(shares[5].astype(jnp.bfloat16), "dp").astype(jnp.float32),
        lax.psum(shares[6].astype(jnp.bfloat16), "dp").astype(jnp.float32),
        lax.psum(shares[7].astype(jnp.bfloat16), "dp").astype(jnp.float32),
        lax.psum(shares[8].astype(jnp.bfloat16), "dp").astype(jnp.float32),
        lax.psum(shares[9].astype(jnp.bfloat16), "dp").astype(jnp.float32),
        lax.psum(grad_rate.astype(jnp.bfloat16), "dp").astype(jnp.float32),
        lax.psum(grad_in_map.astype(jnp.bfloat16), "dp").astype(jnp.float32),
        lax.psum(grad_out_map.astype(jnp.bfloat16), "dp").astype(jnp.float32),
        lax.psum(grad_step.astype(jnp.bfloat16), "dp").astype(jnp.float32),
        lax.psum(grad_skip.astype(jnp.bfloat16), "dp").astype(jnp.float32),
    )
    summed = tuple(summed)
    return (
        result,
        grad_inputs,
        summed[0],
        summed[1],
        summed[2],
        summed[3],
        summed[4],
        summed[5],
        summed[6],
        summed[7],
        summed[8],
        summed[9],
        summed[10],
        summed[11],
        summed[12],
        summed[13],
        summed[14],
    )


def solution(mesh):
    dp_ways, seq_ways = mesh.shape["dp"], mesh.shape["seq"]
    lone, data, flat, cut = P(), P("dp", "seq", None), P("seq"), P("seq", None)
    in_specs = (data, data, P("dp"), lone, flat, flat, cut, cut, cut, cut, flat, flat, cut, cut, cut, cut, cut, flat, flat)
    out_specs = (data, data, flat, flat, cut, cut, cut, cut, flat, flat, cut, cut, cut, cut, cut, flat, flat)

    def run(activations, *others):
        seqs, length, model = activations.shape
        tokens = length // seq_ways
        if (seqs, dp_ways, seq_ways, tokens, model) != (4, 4, 2 * TP, TOKENS, HEADS * LANES):
            return jax.shard_map(plain, mesh=mesh, in_specs=in_specs, out_specs=out_specs, check_vma=False)(activations, *others)
        fine = Mesh(mesh.devices.reshape(2, 2, 2, TP), ("y", "core", "span", "tp"))
        names = {"dp": ("y", "core"), "seq": ("span", "tp")}
        split = lambda specs: tuple(P(*(names.get(a) for a in spec)) for spec in specs)
        whole = jax.shard_map(by_spans, mesh=fine, in_specs=split(in_specs), out_specs=split(out_specs), check_vma=False)
        return whole(activations, *others)

    return run
```

```python
import functools
import math

import jax
import jax.numpy as jnp
from jax import lax
from jax.experimental import pallas as pl
from jax.experimental.pallas import tpu as pltpu
from jax.sharding import Mesh
from jax.sharding import PartitionSpec as P

HEADS = 8
CTX = 128
BLK_A = 256
BLK_B = 512
TP = 4
TOKENS = 128
LANES = 128
UNITS = 256
STATES = 16
CHUNKS = 8
NEG = -1e30
f32 = jnp.float32
bf16 = jnp.bfloat16
LIMIT = 24
SWAP = [(0, 1), (1, 0)]
PER_US = 16000000000
MICROSECONDS = dict(
    norm_one_kernel=0.85,
    scan_kernel=4.6,
    carry_kernel=2.0,
    qkv_kernel=2.3,
    attend_kernel=4.0,
    norm_two_kernel=1.0,
    units_kernel=3.0,
    hidden_kernel=5.4,
    units_weights_kernel=3.0,
    units_one_kernel=1.1,
    norm_two_back_kernel=1.2,
    attend_back_kernel=4.8,
    attend_weights_kernel=2.4,
    context_sum_kernel=0.65,
    heads_one_kernel=0.8,
    units_two_kernel=0.8,
    result_kernel=1.8,
    scan_back_kernel=4.0,
    units_three_kernel=0.7,
    carry_back_kernel=1.9,
    heads_two_kernel=0.9,
    sums_kernel=0.9,
    units_four_kernel=0.6,
    last_kernel=2.1,
    heads_three_kernel=0.6,
    heads_four_kernel=0.6,
    units_home_kernel=3.0,
    heads_home_kernel=2.1,
    pack_kernel=0.7,
    lines_kernel=0.5,
    lowered_back_kernel=1.7,
    share_kernel=2.5,
    lines_sum_kernel=0.5,
)


SPAN, PLACE, ROW, CORE, WIDE = range(5)


def call(kernel, outs, *args, scratch=(), loose=(), after=(), limit=LIMIT):
    count = len(args)
    vmem, free = pl.BlockSpec(memory_space=pltpu.VMEM), pl.BlockSpec(memory_space=pl.ANY)
    specs = [pl.BlockSpec(memory_space=pltpu.SMEM)] + [free if i in loose else vmem for i in range(1, count)] + [free] * len(after)

    def inner(*refs):
        kernel(*refs[:count], *refs[count + len(after) :])

    return pl.pallas_call(
        inner,
        out_shape=[jax.ShapeDtypeStruct(shape, kind) for shape, kind in outs],
        in_specs=specs,
        out_specs=[vmem] * len(outs),
        scratch_shapes=list(scratch),
        compiler_params=pltpu.CompilerParams(vmem_limit_bytes=limit * 1024 * 1024),
        cost_estimate=pl.CostEstimate(flops=int(MICROSECONDS[kernel.__name__] * PER_US), bytes_accessed=0, transcendentals=0),
    )(*args, *after)


def part(index, size):
    return pl.ds(pl.multiple_of(index * size, size), size)


def channel_part(scal, s, rank):
    return part((s ^ scal[SPAN]) * TP + rank, LANES)


def dot(a, b, ca, cb):
    return lax.dot_general(a, b, (((ca,), (cb,)), ((), ())), preferred_element_type=f32)


def wide(ref):
    return ref[...].astype(f32)


def send_all(copies, sems):
    copies = [pltpu.make_async_copy(a, b, sems.at[i]) for i, (a, b) in enumerate(copies)]
    for copy in copies:
        copy.start()
    for copy in copies:
        copy.wait()


def share_kernel(scal, wq, wk, wv, out, down, up, send, out_send, down_send, sems):
    core, row = scal[CORE], scal[ROW]
    copies = [(out.at[part(core, 64), :], out_send), (down.at[part(core * 2 + row, LANES), :], down_send)]
    for to in range(2 * TP):
        for s in range(2):
            there = ((s * TP + to % TP) * 2 + core) * 2 + row
            copies.append((up.at[:, part(there, LANES)], send.at[to, pl.ds(s * TOKENS, TOKENS), :]))
    copies = [pltpu.make_async_copy(a, b, sems.at[i]) for i, (a, b) in enumerate(copies)]
    for copy in copies:
        copy.start()
    for rank in range(TP):
        for m, w in enumerate((wq, wk, wv)):
            value = w[part(row, 64), part(core * TP + rank, LANES)]
            for s in range(2):
                send[s * TP + rank, pl.ds(2 * TOKENS + m * 64, 64), :] = value
    for copy in copies:
        copy.wait()


def pack_kernel(scal, rate, inward, outward, step, skip, g1, b1, g2, b2, out, vecs, sems):
    places = [pl.ds(i * STATES, STATES) for i in range(3)] + [pl.ds(3 * STATES + i, 1) for i in range(2)]
    copies = [(ref, out.at[at, :]) for ref, at in zip((rate, inward, outward, step, skip), places)]
    copies += [(ref, vecs.at[i]) for i, ref in enumerate((g1, b1, g2, b2))]
    copies = [pltpu.make_async_copy(a, b, sems.at[i]) for i, (a, b) in enumerate(copies)]
    for copy in copies:
        copy.start()
    for copy in copies:
        copy.wait()
    for i in range(4):
        out[3 * STATES + 2 + i : 3 * STATES + 3 + i, :] = vecs[i].astype(f32)
    out[3 * STATES + 6 :, :] = jnp.zeros((out.shape[0] - 3 * STATES - 6, LANES), f32)


def lines_kernel(scal, own, far, vec):
    for ref, s in ((own, scal[SPAN]), (far, 1 - scal[SPAN])):
        vec[part(s, 8), :] = jnp.concatenate([ref[50:54, :], jnp.zeros((4, LANES), f32)], axis=0)


def norm_rows(x):
    center = x - jnp.mean(x, axis=1, keepdims=True)
    inverse = lax.rsqrt(jnp.mean(center * center, axis=1, keepdims=True) + 1e-05)
    return center * inverse, inverse


def gather_lines(scal, vecs, lines):
    for j, vec in enumerate(vecs):
        for s in range(2):
            lines[:, part(s * TP + (scal[PLACE] ^ j), LANES)] = vec[s * 8 : s * 8 + 8, :]


def norm_one_kernel(scal, x, v0, v1, v2, v3, low, lines):
    gather_lines(scal, (v0, v1, v2, v3), lines)
    scaled, _ = norm_rows(x[...])
    low[...] = (scaled * lines[0:1, :] + lines[1:2, :]).astype(bf16)


def sum_of(own, a, b, c):
    return (wide(own) + wide(a)) + (wide(b) + wide(c))


def norm_two_kernel(scal, x, own, a, b, c, vec, total, low):
    first = x[...] + sum_of(own, a, b, c)
    total[...] = first
    scaled, _ = norm_rows(first)
    low[...] = (scaled * vec[2:3, :] + vec[3:4, :]).astype(bf16)


def norm_back(grad, scaled, inverse, gain):
    e = grad * gain
    return inverse * (e - jnp.mean(e, axis=1, keepdims=True) - scaled * jnp.mean(e * scaled, axis=1, keepdims=True))


def norm_two_back_kernel(scal, total, own, a, b, c, cot, vec, grad_first, low, lines):
    grad = sum_of(own, a, b, c)
    scaled, inverse = norm_rows(total[...])
    value = cot[...].astype(f32) + norm_back(grad, scaled, inverse, vec[2:3, :])
    grad_first[...] = value
    low[...] = value.astype(bf16)
    lines[0:1, :] = jnp.sum(grad * scaled, axis=0, keepdims=True)
    lines[1:2, :] = jnp.sum(grad, axis=0, keepdims=True)
    lines[2:8, :] = jnp.zeros((6, lines.shape[1]), f32)


def last_kernel(scal, x, vec, grad_first, own, a, b, c, p0, p1, p2, p3, lines_two, out, lines, grad):
    grad[...] = sum_of(own, a, b, c)
    for j, p in enumerate((p0, p1, p2, p3)):
        for s in range(2):
            lanes = channel_part(scal, s, scal[PLACE] ^ j)
            grad[:, lanes] = grad[:, lanes] + p[:, pl.ds(s * LANES, LANES)].astype(f32)
    scaled, inverse = norm_rows(x[...])
    out[...] = grad_first[...] + norm_back(grad[...], scaled, inverse, vec[0:1, :])
    gain = jnp.sum(grad[...] * scaled, axis=0, keepdims=True)
    bias = jnp.sum(grad[...], axis=0, keepdims=True)
    for n in range(lines.shape[0]):
        lanes = slice(n * LANES, (n + 1) * LANES)
        lines[n, 0:1, :] = gain[:, lanes]
        lines[n, 1:2, :] = bias[:, lanes]
        lines[n, 2:4, :] = lines_two[0:2, lanes]
        lines[n, 4:8, :] = jnp.zeros((4, LANES), f32)


def lines_sum_kernel(scal, parts, sums, out):
    out[0:8, :] = jnp.sum(parts[...], axis=0)
    out[8:, :] = sums[...]


def spread(row):
    return jnp.broadcast_to(row, (CHUNKS, LANES))


def power(base, times):
    for _ in range(int(math.log2(times))):
        base = base * base
    return base


def total_of(parts):
    while len(parts) > 1:
        parts = [parts[i] + parts[i + 1] for i in range(0, len(parts), 2)]
    return parts[0]


def one_hot(spots, rows):
    return (spots[...] == lax.broadcasted_iota(jnp.int32, (spots.shape[0], rows), 1)).astype(bf16)


def own_channels(scal, xs, parts):
    place = scal[PLACE]
    for j, x in enumerate(parts):
        for s in range(2):
            xs[s, part(place ^ j, TOKENS), :] = x[:, channel_part(scal, s, place)].astype(f32)


def scan(reverse, xs, a_ref, w_ref, skips, y_ref, end, sh, ih, sq=None, kept=None):
    states = a_ref.shape[0]
    steps = xs.shape[1] // CHUNKS

    def at(step):
        return pl.ds(steps - 1 - step if reverse else step, CHUNKS, stride=steps)

    for s in range(xs.shape[0]):
        cols = pl.ds(s * LANES, LANES)
        rate = [spread(a_ref[n : n + 1, cols]) for n in range(states)]
        ih[0] = jnp.zeros((CHUNKS, LANES), f32)
        zero = ih[0]

        def local(step, carry):
            x = xs[s, at(step), :]
            if sq is not None:
                h, q = carry
                q = tuple(a * (u + v) for a, u, v in zip(rate, q, h))
            else:
                (h,) = carry
            h = tuple(a * v + x for a, v in zip(rate, h))
            return (h, q) if sq is not None else (h,)

        done = lax.fori_loop(0, steps, local, ((zero,) * states,) * (1 if sq is None else 2), unroll=4)
        for n in range(states):
            sh[n] = done[0][n]
            if sq is not None:
                sq[n] = done[1][n]
        jump = power(a_ref[:, cols], steps)
        hold = jnp.zeros((states, LANES), f32)
        hold_q = jnp.zeros((states, LANES), f32)
        for k in range(CHUNKS):
            k = CHUNKS - 1 - k if reverse else k
            ih[:, k, :] = hold
            if sq is not None:
                hold_q = jump * (hold_q + float(steps) * hold) + sq[:, k, :]
            hold = jump * hold + sh[:, k, :]
        if kept is not None:
            kept[0, s] = sh[...]
            kept[1, s] = sq[...]
        end(s, hold, hold_q)
        weight = [spread(w_ref[n : n + 1, cols]) for n in range(states)]
        skip = spread(skips[s][49:50, :])

        def emit(step, h):
            x = xs[s, at(step), :]
            h = tuple(a * v + x for a, v in zip(rate, h))
            y_ref[s, at(step), :] = total_of([w * v for w, v in zip(weight, h)]) + skip * x
            return h

        lax.fori_loop(0, steps, emit, tuple(ih[n] for n in range(states)), unroll=4)


def scan_kernel(scal, x0, x1, x2, x3, ssm0, ssm1, spots, y, to_next, ends, decay, mix, kept, xs, low, sh, sq, ih):
    own_channels(scal, xs, (x0, x1, x2, x3))
    n = decay.shape[0]
    for s, ssm in enumerate((ssm0, ssm1)):
        cols = pl.ds(s * LANES, LANES)
        step = ssm[48:49, :]
        decay[:, cols] = jnp.exp(-step * ssm[0:n, :])
        mix[:, cols] = ssm[32:48, :] * ssm[16:32, :] * step

    def end(s, h, q):
        other = pl.ds((1 - s) * LANES, LANES)
        ends[0:n, other] = h
        ends[n : 2 * n, other] = q

    scan(False, xs, decay, mix, (ssm0, ssm1), y, end, sh, ih, sq, kept)
    for s in range(2):
        low[:, pl.ds((1 - s) * LANES, LANES)] = y[s].astype(bf16)
    to_next[...] = dot(one_hot(spots, low.shape[0]), low[...], 1, 0).astype(bf16)


def carry(reverse, y_ref, a_ref, w_ref, h_ref, out, ih):
    states = a_ref.shape[0]
    steps = y_ref.shape[1] // CHUNKS

    def at(step):
        return pl.ds(steps - 1 - step if reverse else step, CHUNKS, stride=steps)

    for s in range(y_ref.shape[0]):
        cols = pl.ds(s * LANES, LANES)
        rate = [spread(a_ref[n : n + 1, cols]) for n in range(states)]
        jump = power(a_ref[:, cols], steps)
        hold = w_ref[:, cols] * h_ref[0:states, cols]
        for k in range(CHUNKS):
            ih[:, CHUNKS - 1 - k if reverse else k, :] = hold
            hold = jump * hold

        def emit(step, h):
            h = tuple(a * v for a, v in zip(rate, h))
            out[s, at(step), :] = y_ref[s, at(step), :] + total_of(list(h))
            return h

        lax.fori_loop(0, steps, emit, tuple(ih[n] for n in range(states)), unroll=4)


def carry_kernel(scal, y, decay, mix, begin, from_last, spots, context, ih, ys, low):
    carry(False, y, decay, mix, begin, ys, ih)
    for s in range(2):
        low[:, pl.ds(s * LANES, LANES)] = ys[s].astype(bf16)
    context[...] = (dot(one_hot(spots, low.shape[0]), low[...], 1, 0) + wide(from_last)).astype(bf16)


def scan_back_kernel(scal, own, from_next, own_spots, next_spots, ssm0, ssm1, decay, mix, grad, y, ends, sh, ih):
    rows = y.shape[1]
    value = dot(one_hot(own_spots, rows), own[...], 0, 0) + dot(one_hot(next_spots, rows), from_next[...], 0, 0)
    for s in range(2):
        grad[s] = value[:, s * LANES : (s + 1) * LANES]

    def end(s, h, q):
        ends[:, pl.ds((1 - s) * LANES, LANES)] = h

    scan(True, grad, decay, mix, (ssm0, ssm1), y, end, sh, ih)


def carry_back_kernel(scal, y, decay, mix, begin, o0, o1, o2, o3, ih, ys):
    carry(True, y, decay, mix, begin, ys, ih)
    for j, out in enumerate((o0, o1, o2, o3)):
        for s in range(2):
            out[:, pl.ds(s * LANES, LANES)] = ys[s, part(scal[PLACE] ^ j, TOKENS), :].astype(bf16)


def sums_kernel(scal, x0, x1, x2, x3, gs, a_ref, begin, kept, out, xs, ih, iq):
    own_channels(scal, xs, (x0, x1, x2, x3))
    states = a_ref.shape[0]
    steps = xs.shape[1] // CHUNKS
    group = 8
    out[2 * states :, :] = jnp.zeros((out.shape[0] - 2 * states, out.shape[1]), f32)
    for s in range(xs.shape[0]):
        cols = pl.ds(s * LANES, LANES)
        jump = power(a_ref[:, cols], steps)
        hold, hold_q = begin[0:states, cols], begin[states : 2 * states, cols]
        for k in range(CHUNKS):
            ih[:, k, :] = hold
            iq[:, k, :] = hold_q
            hold_q = jump * (hold_q + float(steps) * hold) + kept[1, s, :, k, :]
            hold = jump * hold + kept[0, s, :, k, :]
        for base in range(0, states, group):
            rate = [spread(a_ref[n : n + 1, cols]) for n in range(base, base + group)]

            def gain(step, carried):
                h, q, sw, sq = carried
                at = pl.ds(step, CHUNKS, stride=steps)
                x, g = xs[s, at, :], gs[s, at, :]
                q = tuple(a * (u + v) for a, u, v in zip(rate, q, h))
                h = tuple(a * v + x for a, v in zip(rate, h))
                sw = tuple(u + g * v for u, v in zip(sw, h))
                sq = tuple(u + g * v for u, v in zip(sq, q))
                return h, q, sw, sq

            first = tuple(ih[base + n] for n in range(group)), tuple(iq[base + n] for n in range(group))
            none = tuple(v * 0.0 for v in first[0])
            _, _, sw, sq = lax.fori_loop(0, steps, gain, first + (none, none), unroll=2)
            for n in range(group):
                out[base + n : base + n + 1, cols] = jnp.sum(sw[n], axis=0, keepdims=True)
                out[states + base + n : states + base + n + 1, cols] = jnp.sum(sq[n], axis=0, keepdims=True)
        out[2 * states : 2 * states + 1, cols] = jnp.sum(xs[s] * gs[s], axis=0, keepdims=True)


def qkv_kernel(scal, x0, x1, x2, x3, w00, w01, w10, w11, w, qkv):
    for j, k, ref in ((0, 0, w00), (0, 1, w01), (1, 0, w10), (1, 1, w11)):
        for n in range(2 * TP):
            for m in range(3):
                there = part(2 * n + (scal[ROW] ^ k), 64)
                w[there, pl.ds((2 * m + j) * LANES, LANES)] = ref[n, pl.ds(2 * TOKENS + m * 64, 64), :]
    for j, x in enumerate((x0, x1, x2, x3)):
        qkv[part(scal[PLACE] ^ j, TOKENS), :] = dot(x[...], w[...], 1, 0).astype(bf16)


def masks(size, is_wide, ok_ref, sub):
    rows = lax.broadcasted_iota(jnp.int32, (size, size), 0)
    cols = lax.broadcasted_iota(jnp.int32, (size, size), 1)
    return ok_ref[sub : sub + 1, :] > 0.0, is_wide > 0, cols <= rows


def out_of_order(out_ref, lanes, value, sub, place):
    each = value.shape[0] // TOKENS
    for i in range(each):
        out_ref[part((sub * each + i) ^ place, TOKENS), lanes] = value[i * TOKENS : (i + 1) * TOKENS]


def probabilities(q, ctx_k, k_ref, size, sub, lanes, mask, scale):
    context, earlier, own = mask
    parts = [jnp.where(context, dot(q, ctx_k, 1, 1) * scale, NEG)]
    for other in range(sub):
        keys = k_ref[pl.ds(other * size, size), lanes]
        parts.append(jnp.where(earlier, dot(q, keys, 1, 1) * scale, NEG))
    parts.append(jnp.where(own, dot(q, k_ref[pl.ds(sub * size, size), lanes], 1, 1) * scale, NEG))
    top = functools.reduce(jnp.maximum, [jnp.max(s, axis=1, keepdims=True) for s in parts])
    parts = [jnp.exp(s - top) for s in parts]
    inverse = 1.0 / sum(jnp.sum(s, axis=1, keepdims=True) for s in parts)
    return [s * inverse for s in parts]


def attend_kernel(scal, ok, qkv, c0, c1, c2, c3, w, out_own, out_0, out_1, mixed, ckv, out_w, b0, b1, b2, b3):
    place, core = scal[PLACE], scal[CORE]
    width = qkv.shape[1] // 3
    dim = LANES
    own = core ^ scal[SPAN]
    out_w[part(own, dim), :] = out_own[...]
    out_w[part((1 - own) * 2 + core, 64), :] = out_0[...]
    out_w[part((1 - own) * 2 + 1 - core, 64), :] = out_1[...]
    total = None
    for j, c in enumerate((c0, c1, c2, c3)):
        for s in range(2):
            term = dot(c[:, pl.ds(s * LANES, LANES)], w[channel_part(scal, s, place ^ j), pl.ds(width, 2 * width)], 1, 0)
            total = term if total is None else total + term
    ckv[...] = total.astype(bf16)
    subs = ok.shape[0]
    size = qkv.shape[0] // subs
    scale = dim ** (-0.5)
    for sub in range(subs):
        mask = masks(size, scal[WIDE], ok, sub)
        here = pl.ds(sub * size, size)
        for h in range(width // dim):
            lq, lk, lv = (pl.ds(i * width + h * dim, dim) for i in range(3))
            ck = ckv[pl.ds(sub * CTX, CTX), pl.ds(h * dim, dim)]
            cv = ckv[pl.ds(sub * CTX, CTX), pl.ds(width + h * dim, dim)]
            probs = probabilities(qkv[here, lq], ck, qkv, size, sub, lk, mask, scale)
            value = dot(probs[0].astype(bf16), cv, 1, 0)
            for other in range(sub + 1):
                value += dot(probs[1 + other].astype(bf16), qkv[pl.ds(other * size, size), lv], 1, 0)
            out_of_order(mixed, pl.ds(h * dim, dim), value.astype(bf16), sub, place)
    for j, b in enumerate((b0, b1, b2, b3)):
        b[...] = dot(mixed[pl.ds(j * TOKENS, TOKENS), :], out_w[...], 1, 0).astype(bf16)


def attend_back_kernel(scal, ok, qkv, ckv, g0, g1, g2, g3, out_w, w, out, ctx, x0, x1, x2, x3, gms, acc):
    place = scal[PLACE]
    width = qkv.shape[1] // 3
    dim = LANES
    subs = ok.shape[0]
    size = qkv.shape[0] // subs
    scale = dim ** (-0.5)
    for j, g in enumerate((g0, g1, g2, g3)):
        gms[part(place ^ j, TOKENS), :] = dot(g[...], out_w[...], 1, 1).astype(bf16)
    acc[...] = jnp.zeros_like(acc)
    for sub in range(subs):
        mask = masks(size, scal[WIDE], ok, sub)
        here = pl.ds(sub * size, size)
        cs = pl.ds(sub * CTX, CTX)
        for h in range(width // dim):
            lq, lk, lv = (pl.ds(i * width + h * dim, dim) for i in range(3))
            lh, lhv = pl.ds(h * dim, dim), pl.ds(width + h * dim, dim)
            ck, cv = ckv[cs, lh], ckv[cs, lhv]
            q, gm = qkv[here, lq], gms[here, lh]
            probs = probabilities(q, ck, qkv, size, sub, lk, mask, scale)
            values = [cv] + [qkv[pl.ds(o * size, size), lv] for o in range(sub + 1)]
            keys = [ck] + [qkv[pl.ds(o * size, size), lk] for o in range(sub + 1)]
            grads = [dot(gm, v, 1, 1) for v in values]
            inner = sum(jnp.sum(p * g, axis=1, keepdims=True) for p, g in zip(probs, grads))
            scores = [(p * (g - inner)).astype(bf16) for p, g in zip(probs, grads)]
            grad_q = sum(dot(s, k, 1, 0) for s, k in zip(scores, keys))
            out_of_order(out, lq, (grad_q * scale).astype(bf16), sub, place)
            ctx[cs, lh] = (dot(scores[0], q, 0, 0) * scale).astype(bf16)
            ctx[cs, lhv] = dot(probs[0].astype(bf16), gm, 0, 0).astype(bf16)
            for o in range(sub + 1):
                there = pl.ds(o * size, size)
                acc[there, lh] += dot(scores[1 + o], q, 0, 0) * scale
                acc[there, lhv] += dot(probs[1 + o].astype(bf16), gm, 0, 0)
    for sub in range(subs):
        out_of_order(out, pl.ds(width, 2 * width), acc[pl.ds(sub * size, size), :].astype(bf16), sub, place)
    for j, x in enumerate((x0, x1, x2, x3)):
        for s in range(2):
            rows = channel_part(scal, s, place ^ j)
            x[:, pl.ds(s * LANES, LANES)] = dot(ctx[...], w[rows, pl.ds(width, 2 * width)], 1, 1).astype(bf16)


def lowered_back_kernel(scal, g, w, o0, o1, o2, o3):
    for j, out in enumerate((o0, o1, o2, o3)):
        out[...] = dot(g[pl.ds(j * TOKENS, TOKENS), :], w[...], 1, 1).astype(bf16)


def context_sum_kernel(scal, own, a, b, c, total, turned):
    value = ((wide(own) + wide(a)) + (wide(b) + wide(c))).astype(bf16)
    total[...] = value
    for s in range(2):
        turned[:, pl.ds((1 - s) * LANES, LANES)] = value[:, s * LANES : (s + 1) * LANES]


def attend_weights_kernel(scal, x0, x1, x2, x3, c0, c1, c2, c3, gqkv, gctx, mixed, g0, g1, g2, g3, send, keep, rows, acc, acc_out):
    place, core = scal[PLACE], scal[CORE]
    for j, x in enumerate((x0, x1, x2, x3)):
        rows[pl.ds(j * TOKENS, TOKENS), :] = x[...]
    width = gqkv.shape[1] // 3
    half = rows.shape[1] // 2
    for s in range(2):
        acc[pl.ds(s * half, half), :] = dot(rows[:, pl.ds(s * half, half)], gqkv[...], 0, 0)
    for j, c in enumerate((c0, c1, c2, c3)):
        for s in range(2):
            there = channel_part(scal, s, place ^ j)
            acc[there, pl.ds(width, 2 * width)] += dot(c[:, pl.ds(s * LANES, LANES)], gctx[...], 0, 0)
    size = acc.shape[0]
    for m in range(3):
        keep[pl.ds(m * size, size), :] = acc[:, pl.ds(2 * m * LANES, LANES)].astype(bf16)
        send[pl.ds(m * size, size), :] = acc[:, pl.ds((2 * m + 1) * LANES, LANES)].astype(bf16)
    for j, g in enumerate((g0, g1, g2, g3)):
        rows[pl.ds(j * TOKENS, TOKENS), :] = g[...]
    acc_out[...] = dot(mixed[...], rows[...], 0, 0)
    for s in range(2):
        head = core ^ scal[SPAN] ^ s
        for ref, side in ((keep, core), (send, 1 - core)):
            for i in range(2 * TP):
                there = pl.ds(3 * size + i * LANES + s * 64, 64)
                ref[there, :] = acc_out[part(head * 2 + side, 64), pl.ds(i * LANES, LANES)].astype(bf16)


def units_kernel(scal, c0, c1, c2, c3, u00, u01, u10, u11, own, d00, d01, d10, d11, up_w, down_w, ahead, rows):
    span, core, row = scal[SPAN], scal[CORE], scal[ROW]
    half = up_w.shape[0] // 2
    for j, k, ref in ((0, 0, u00), (0, 1, u01), (1, 0, u10), (1, 1, u11)):
        for n in range(2 * TP):
            for s in range(2):
                there = part((s * 2 + j) * 2 + (row ^ k), LANES)
                up_w[pl.ds(n * LANES, LANES), there] = ref[n, pl.ds(s * TOKENS, TOKENS), :]
    for j in range(2):
        down_w[part(span * 2 + j, UNITS), :] = own[part(core ^ j, UNITS), :]
    for j, k, ref in ((0, 0, d00), (0, 1, d01), (1, 0, d10), (1, 1, d11)):
        down_w[part(((1 - span) * 2 + j) * 2 + (row ^ k), LANES), :] = ref[...]
    for j, c in enumerate((c0, c1, c2, c3)):
        rows[pl.ds(j * TOKENS, TOKENS), :] = c[...]
    for i in range(4):
        tile = pl.ds(i * UNITS, UNITS)
        ahead[:, tile] = dot(rows[...], down_w[tile, :], 1, 1)


def gelu_parts(a):
    c = math.sqrt(2.0 / math.pi)
    t = jnp.tanh(c * (a + 0.044715 * a * a * a))
    half = 0.5 * (1.0 + t)
    return a * half, half + 0.5 * a * (1.0 - t * t) * c * (1.0 + 3 * 0.044715 * a * a)


def hidden_kernel(scal, n0, n1, n2, n3, up_w, ahead, o0, o1, o2, o3, h0, h1, p0, p1, rows, pre):
    for j, n in enumerate((n0, n1, n2, n3)):
        rows[pl.ds(j * TOKENS, TOKENS), :] = n[...]
    for i in range(4):
        s, j = divmod(i, 2)
        tile, lanes = pl.ds(i * UNITS, UNITS), pl.ds(s * UNITS, UNITS)
        act, slope = gelu_parts(dot(rows[...], up_w[:, tile], 1, 0))
        low = (ahead[:, tile] * slope).astype(bf16)
        (h0, h1)[j][:, lanes] = act.astype(bf16)
        (p0, p1)[j][:, lanes] = low
        pre[:, tile] = low
    for j, out in enumerate((o0, o1, o2, o3)):
        out[...] = dot(pre[pl.ds(j * TOKENS, TOKENS), :], up_w[...], 1, 1).astype(bf16)


def result_kernel(scal, h0, h1, down_w, o0, o1, o2, o3):
    for j, out in enumerate((o0, o1, o2, o3)):
        here = pl.ds(j * TOKENS, TOKENS)
        total = None
        for s in range(2):
            for k, h in enumerate((h0, h1)):
                term = dot(h[here, pl.ds(s * UNITS, UNITS)], down_w[pl.ds((2 * s + k) * UNITS, UNITS), :], 1, 0)
                total = term if total is None else total + term
        out[...] = total.astype(bf16)


def units_weights_kernel(scal, rows, cot, h0, h1, p0, p1, d_send, u_send, d_keep, u_keep):
    half = h0.shape[1]
    for h, p, down, up in ((h1, p1, d_send, u_send), (h0, p0, d_keep, u_keep)):
        for i in range(2):
            tile = pl.ds(i * UNITS, UNITS)
            down[tile, :] = dot(h[:, tile], cot[...], 0, 0).astype(bf16)
        for i in range(4):
            s, n = divmod(i, 2)
            there = (pl.ds(n * UNITS, UNITS), pl.ds(s * half, half))
            up[there] = dot(rows[:, pl.ds(i * UNITS, UNITS)], p[...], 0, 0).astype(bf16)


def units_one_kernel(scal, down, down_got, up, up_got, d_send, d_keep, u_send, u_keep):
    row = scal[ROW]
    half = up.shape[0]
    for s in range(2):
        for ref, side in ((d_keep, row), (d_send, 1 - row)):
            there = part(2 * s + side, LANES)
            ref[pl.ds(s * LANES, LANES), :] = (wide(down.at[there, :]) + wide(down_got.at[there, :])).astype(bf16)
        for n in range(2):
            for ref, side in ((u_keep, row), (u_send, 1 - row)):
                there = part(2 * (2 * n + s) + side, LANES)
                ref[:, pl.ds((2 * n + s) * LANES, LANES)] = (wide(up.at[:, there]) + wide(up_got.at[:, there])).astype(bf16)


def units_two_kernel(scal, down, down_got, up, up_got, d_send, d_keep, u_send, u_keep):
    for s, d_ref, u_ref in ((scal[SPAN], d_keep, u_keep), (1 - scal[SPAN], d_send, u_send)):
        there = part(s, LANES)
        d_ref[...] = (wide(down.at[there, :]) + wide(down_got.at[there, :])).astype(bf16)
        there = part(s, UNITS)
        u_ref[...] = (wide(up.at[:, there]) + wide(up_got.at[:, there])).astype(bf16)


def units_three_kernel(scal, up, up_got, x0, x1, x2, x3):
    for j, x in enumerate((x0, x1, x2, x3)):
        there = part(scal[PLACE] ^ j, LANES)
        x[...] = (wide(up.at[there, :]) + wide(up_got.at[there, :])).astype(bf16)


def units_four_kernel(scal, down, down_got, x0, x1, x2, x3, out):
    out[0:LANES, :] = (wide(down) + wide(down_got)).astype(bf16)
    for j, x in enumerate((x0, x1, x2, x3)):
        out[LANES : 2 * LANES, part(scal[PLACE] ^ j, UNITS)] = x[...]


def units_home_kernel(scal, b00, b01, b10, b11, up, down):
    row, core = scal[ROW], scal[CORE]
    for j, k, ref in ((0, 0, b00), (0, 1, b01), (1, 0, b10), (1, 1, b11)):
        quarter = (core ^ j) * 2 + (row ^ k)
        down[part(quarter, LANES), :] = ref[0:LANES, :].astype(f32)
        for rank in range(TP):
            for s in range(2):
                there = (s * TP + rank) * 4 + quarter
                up[:, part(there, LANES)] = ref[LANES : 2 * LANES, pl.ds(rank * UNITS + s * LANES, LANES)].astype(f32)


def heads_one_kernel(scal, own, got, send, keep):
    row = scal[ROW]
    for n in range(own.shape[0] // 64 // 2):
        for ref, side in ((keep, row), (send, 1 - row)):
            size = 64 if n < 3 * 2 * TP else 32
            pairs = 1 if size == 64 else 2
            for i in range(pairs):
                at = part((2 * n + side) if pairs == 1 else (4 * n + 2 * i + side), size)
                there = pl.ds(n * 64 + i * 32, size)
                ref[there, :] = (wide(own.at[at, :]) + wide(got.at[at, :])).astype(bf16)


def heads_two_kernel(scal, own, got, send, keep):
    quarter = TP * 64
    for m in range(3):
        for ref, s in ((keep, scal[SPAN]), (send, 1 - scal[SPAN])):
            at = part(2 * m + s, quarter)
            ref[pl.ds(m * quarter, quarter), :] = (wide(own.at[at, :]) + wide(got.at[at, :])).astype(bf16)
    for i in range(2 * TP):
        for ref, s in ((keep, 0), (send, 1)):
            at = pl.ds(6 * quarter + i * 64 + s * 32, 32)
            ref[pl.ds(3 * quarter + i * 32, 32), :] = (wide(own.at[at, :]) + wide(got.at[at, :])).astype(bf16)


def heads_three_kernel(scal, own, got, low, x0, x1, x2, x3):
    quarter = TP * 64
    at = pl.ds(3 * quarter, low.shape[0])
    low[...] = (wide(own.at[at, :]) + wide(got.at[at, :])).astype(bf16)
    for j, x in enumerate((x0, x1, x2, x3)):
        for m in range(3):
            at = part(m * TP + (scal[PLACE] ^ j), 64)
            x[:, pl.ds(m * LANES, LANES)] = (wide(own.at[at, :]) + wide(got.at[at, :])).astype(bf16)


def heads_four_kernel(scal, low, x0, x1, x2, x3, out):
    width = x0.shape[1]
    for j, x in enumerate((x0, x1, x2, x3)):
        out[:, part(scal[PLACE] ^ j, width)] = x[...]
    for i in range(2 * TP):
        there = (pl.ds(i // TP * 32, 32), pl.ds(TP * width + i % TP * LANES, LANES))
        out[there] = low[pl.ds(i * 32, 32), :]


def heads_home_kernel(scal, b00, b01, b10, b11, gq, gk, gv, go):
    row, core = scal[ROW], scal[CORE]
    width = 3 * LANES
    half = go.shape[1] // 2
    for j, k, ref in ((0, 0, b00), (0, 1, b01), (1, 0, b10), (1, 1, b11)):
        for rank in range(TP):
            for m, out in enumerate((gq, gk, gv)):
                lanes = pl.ds(rank * width + m * LANES, LANES)
                out[part(row ^ k, 64), part((core ^ j) * TP + rank, LANES)] = ref[:, lanes].astype(f32)
        there = part((core ^ j) * 2 + (row ^ k), 32)
        for i in range(2):
            go[there, pl.ds(i * half, half)] = ref[pl.ds(i * 32, 32), pl.ds(TP * width, half)].astype(f32)


def swap(x, axis):
    return lax.ppermute(x, axis, SWAP)


def across(x, d):
    return lax.ppermute(x, "tp", [(i, i ^ d) for i in range(TP)])


def gathered(x):
    return [x] + [across(x, d) for d in range(1, TP)]


def traded(parts):
    return [parts[0]] + [across(parts[d], d) for d in range(1, TP)]


def traded_all(x):
    return lax.all_to_all(x, ("span", "tp"), split_axis=0, concat_axis=0, tiled=True)


def hold_until(x, spent, *others):
    x, *others = lax.optimization_barrier((x,) + others)
    spent.extend(others)
    return x


def by_spans(
    activations,
    cotangent,
    block_sizes,
    context_back,
    first_gain,
    first_bias,
    w_query,
    w_key,
    w_value,
    w_out,
    second_gain,
    second_bias,
    w_up,
    w_down,
    decay_rate,
    input_map,
    output_map,
    step_size,
    skip_gain,
):
    span, place, row, core = (lax.axis_index(a).astype(jnp.int32) for a in ("span", "tp", "y", "core"))
    activations, cotangent, width = activations[0], cotangent[0], block_sizes[0]
    model = activations.shape[1]
    rows = TP * TOKENS
    subs = rows // BLK_A
    ctx_rows = subs * CTX
    mine = 2 * LANES
    half = model // 2
    scal = jnp.stack([span, place, row, core, (width > BLK_A).astype(jnp.int32)])
    tile = lambda n, m, kind=bf16: ((n, m), kind)
    block, piece = tile(TOKENS, model), tile(TOKENS, mine)

    shares, out_part, down_part = call(
        share_kernel,
        [((2 * TP, 448, LANES), bf16), tile(64, model), block],
        *(scal, w_query, w_key, w_value, w_out, w_down, w_up),
        scratch=[pltpu.SemaphoreType.DMA((4 * TP + 2,))],
        loose=(4, 5, 6),
        limit=56,
    )
    row_of = lambda v: v.reshape(1, LANES)
    (pack,) = call(
        pack_kernel,
        [tile(56, LANES, f32)],
        *(scal, decay_rate.T, input_map.T, output_map.T, row_of(step_size), row_of(skip_gain)),
        *(row_of(v) for v in (first_gain, first_bias, second_gain, second_bias)),
        scratch=[pltpu.VMEM((4, 1, LANES), bf16), pltpu.SemaphoreType.DMA((9,))],
        loose=range(1, 10),
        after=(out_part,),
        limit=60,
    )
    pack_far = swap(pack, "span")
    (vec,) = call(lines_kernel, [tile(16, LANES, f32)], scal, pack, pack_far)
    vecs = gathered(vec)
    spent = []

    def starts_of(which):
        begin = which * rows + jnp.arange(subs, dtype=jnp.int32) * BLK_A
        return begin // width * width

    own_spots = ((starts_of(span) - span * rows)[:, None] - context_back[None, :]).reshape(ctx_rows, 1)
    next_spots = ((starts_of(span + 1) - span * rows)[:, None] - context_back[None, :]).reshape(ctx_rows, 1)
    valid = (starts_of(span)[:, None] >= context_back[None, :]).astype(f32)

    shares = traded_all(hold_until(shares, spent, pack_far))

    low, vec = call(norm_one_kernel, [block, tile(8, model, f32)], scal, activations, *vecs)
    lowered = gathered(low)
    shares = [shares, swap(hold_until(shares, spent, low), "y")]
    down_far, out_far = swap(hold_until(down_part, spent, low), "span"), swap(hold_until(out_part, spent, low), "span")
    down_beside = swap(down_far, "y")
    hold, channels = pltpu.VMEM((STATES, CHUNKS, LANES), f32), pltpu.VMEM((2, rows, LANES), f32)
    channel_out, kept = ((2, rows, LANES), f32), ((2, 2, STATES, CHUNKS, LANES), f32)
    low_channels = pltpu.VMEM((rows, mine), bf16)
    local, to_next, ends, decay, mix, kept = call(
        scan_kernel,
        [channel_out, tile(ctx_rows, mine), tile(2 * STATES, mine, f32), tile(STATES, mine, f32), tile(STATES, mine, f32), kept],
        *(scal, *lowered, pack, pack_far, next_spots),
        scratch=[channels, low_channels, hold, hold, hold],
    )
    forward = [(0, 1)]
    begin, from_last = lax.ppermute(ends, "span", forward), lax.ppermute(to_next, "span", forward)
    cot_parts = gathered(hold_until(cotangent, spent, ends))
    (context,) = call(
        carry_kernel,
        [tile(ctx_rows, mine)],
        *(scal, local, decay, mix, begin, from_last, own_spots),
        after=(down_far,),
        scratch=[hold, channels, low_channels],
    )
    shares += [swap(hold_until(w, spent, ends), "core") for w in shares]
    before_qkv = context
    context = gathered(context)
    out_parts = [w_out, out_far, swap(hold_until(out_far, spent, ends), "core")]
    down_parts = [down_far, down_beside]
    qkv_w, qkv = call(qkv_kernel, [tile(model, 3 * mine), tile(rows, 3 * mine)], scal, *lowered, *shares, after=(before_qkv,))

    down_parts += [swap(hold_until(d, spent, qkv), "core") for d in down_parts]

    mixed, ctx_kv, out_w, *branch = call(
        attend_kernel,
        [tile(rows, mine), tile(ctx_rows, 2 * mine), tile(mine, model)] + [block] * TP,
        *(scal, valid, qkv, *context, qkv_w, *out_parts),
        after=tuple(cot_parts[1:]),
    )
    first_sum, low = call(norm_two_kernel, [tile(TOKENS, model, f32), block], scal, activations, *traded(branch), vec)

    square = tile(model, model)
    up_w, down_w, ahead, cot_span = call(
        units_kernel, [square, square, tile(rows, model, f32), tile(rows, model)], scal, *cot_parts, *shares, w_down, *down_parts
    )
    normal = gathered(low)
    side = tile(rows, half)
    *grad_norm, h0, h1, p0, p1, normal_span = call(
        hidden_kernel,
        [block] * TP + [side] * 4 + [tile(rows, model)],
        *(scal, *normal, up_w, ahead),
        scratch=[pltpu.VMEM((rows, model), bf16)],
    )
    grad_norm = traded(grad_norm)
    flat = tile(half, model)
    down_send, up_send, down_keep, up_keep = call(
        units_weights_kernel,
        [flat] * 4,
        *(scal, normal_span, cot_span, h0, h1, p0, p1),
    )
    quarter = tile(half // 2, model)
    d_send, d_keep, u_send, u_keep = call(
        units_one_kernel,
        [quarter, quarter, tile(half, half), tile(half, half)],
        *(scal, down_keep, swap(down_send, "core"), up_keep, swap(up_send, "core")),
    )
    grad_first, low, lines_two = call(
        norm_two_back_kernel,
        [tile(TOKENS, model, f32), block, tile(8, model, f32)],
        *(scal, first_sum, *grad_norm, cotangent, vec),
    )
    branch_back = gathered(low)
    result_parts = call(result_kernel, [block] * TP, scal, h0, h1, down_w, after=(low,))
    d_send, d_keep, u_send, u_keep = call(
        units_two_kernel,
        [block, block, tile(half, mine), tile(half, mine)],
        *(scal, d_keep, swap(d_send, "y"), u_keep, swap(u_send, "y")),
    )

    grad_qkv, grad_ctx, *back = call(
        attend_back_kernel,
        [tile(rows, 3 * mine), tile(ctx_rows, 2 * mine)] + [tile(ctx_rows, mine)] * TP,
        *(scal, valid, qkv, ctx_kv, *branch_back, out_w, qkv_w),
        after=(result_parts[0],),
        scratch=[pltpu.VMEM((rows, mine), bf16), pltpu.VMEM((rows, 2 * mine), f32)],
    )
    back = traded(back)
    grad_context, turned = call(context_sum_kernel, [tile(ctx_rows, mine)] * 2, scal, *back, after=(u_send,))
    from_next = lax.ppermute(turned, "span", [(1, 0)])
    d_send = hold_until(d_send, spent, from_next)
    heads = tile(4 * model, LANES)
    heads_send, heads_keep = call(
        attend_weights_kernel,
        [heads] * 2,
        *(scal, *lowered, *context, grad_qkv, grad_ctx, mixed, *branch_back),
        scratch=[pltpu.VMEM((rows, model), bf16), pltpu.VMEM((model, 3 * mine), f32), pltpu.VMEM((mine, model), f32)],
        after=(turned,),
    )
    heads = tile(2 * model, LANES)
    heads_send, heads_keep = call(
        heads_one_kernel, [heads] * 2, scal, heads_keep, swap(heads_send, "core")
    )
    grad_lowered = traded(call(lowered_back_kernel, [block] * TP, scal, grad_qkv, qkv_w, after=(turned,)))

    u_parts = call(units_three_kernel, [piece] * TP, scal, u_keep, swap(hold_until(u_send, spent, grad_ctx), "span"))

    grad_states, grad_local, grad_ends = call(
        scan_back_kernel,
        [channel_out, channel_out, tile(STATES, mine, f32)],
        *(scal, grad_context, from_next, own_spots, next_spots, pack, pack_far, decay, mix),
        scratch=[hold, hold],
        after=(heads_send,),
    )
    grad_begin = lax.ppermute(grad_ends, "span", [(1, 0)])
    heads = tile(model, LANES)
    heads_send, heads_keep = call(heads_two_kernel, [heads] * 2, scal, heads_keep, swap(hold_until(heads_send, spent, from_next), "y"), after=(grad_begin,))
    (sums,) = call(
        sums_kernel,
        [tile(40, mine, f32)],
        *(scal, *lowered, grad_states, decay, begin, kept),
        scratch=[channels, hold, hold],
        after=(grad_ends,),
    )
    grad_conv = call(
        carry_back_kernel,
        [piece] * TP,
        *(scal, grad_local, decay, mix, grad_begin),
        scratch=[hold, channels],
        after=(sums, *grad_lowered[1:],),
    )
    grad_conv = traded(grad_conv)
    grad_inputs, lines = call(
        last_kernel,
        [tile(TOKENS, model, f32), ((2 * TP, 8, LANES), f32)],
        *(scal, activations, vec, grad_first, *grad_lowered, *grad_conv, lines_two),
        scratch=[pltpu.VMEM((TOKENS, model), f32)],
        after=(u_parts[0], heads_send,),
    )
    (u_all,) = call(units_four_kernel, [tile(2 * LANES, model)], scal, d_keep, swap(d_send, "span"), *traded([hold_until(u, spent, grad_begin) for u in u_parts]))
    out_low, *q_parts = call(
        heads_three_kernel,
        [tile(2 * LANES, LANES)] + [tile(64, 3 * LANES)] * TP,
        *(scal, heads_keep, swap(heads_send, "span")),
    )
    u_beside = swap(u_all, "y")
    result_parts = [hold_until(r, spent, lines) for r in result_parts]
    result_parts = traded(result_parts)
    result = first_sum + sum(x.astype(f32) for x in result_parts)
    (q_all,) = call(heads_four_kernel, [tile(64, 2 * model)], scal, out_low, *traded(q_parts))
    q_beside = swap(q_all, "y")
    grad_up, grad_down = call(
        units_home_kernel,
        [tile(LANES, 4 * model, f32), tile(half, model, f32)],
        *(scal, u_all, u_beside, swap(u_all, "core"), swap(u_beside, "core")),
        after=(q_all,),
    )
    home = tile(LANES, model, f32)
    grad_query, grad_key, grad_value, grad_out = call(
        heads_home_kernel, [home] * 4, scal, q_all, q_beside, swap(q_all, "core"), swap(q_beside, "core"), after=tuple(spent)
    )

    lines = traded_all(lines)
    sums = sums[:, :LANES] + swap(sums[:, LANES:], "span")
    (small,) = call(lines_sum_kernel, [tile(48, LANES, f32)], scal, lines, sums, after=(out_low,))
    small = small + swap(small, "y")
    small = small + swap(small, "core")
    lines, sums = small[:8], small[8:]
    grad_mix, grad_skip = sums[:STATES].T, sums[2 * STATES]
    step = step_size[:, None]
    grad_speed = -(output_map * input_map * step) * sums[STATES : 2 * STATES].T
    grad_step = jnp.sum(grad_mix * output_map * input_map + grad_speed * decay_rate, axis=1)
    return (
        result[None],
        grad_inputs[None],
        lines[0],
        lines[1],
        grad_query,
        grad_key,
        grad_value,
        grad_out,
        lines[2],
        lines[3],
        grad_up,
        grad_down,
        grad_speed * step,
        grad_mix * output_map * step,
        grad_mix * input_map * step,
        grad_step,
        grad_skip,
    )


def from_behind(x, axis, by):
    peers = lax.axis_size(axis)
    pairs = [(i, i + by) for i in range(peers) if 0 <= i + by < peers]
    return lax.ppermute(x, axis, pairs)


def smooth_gate(values):
    return jax.nn.gelu(values, approximate=True)


def ssm_kernel(decay_rate, input_map, output_map, step_size, length):
    offsets = jnp.arange(length).astype(jnp.float32)
    weight = output_map * input_map * step_size[:, None]
    decay_speed = step_size[:, None] * decay_rate
    total_sum = jnp.zeros((decay_rate.shape[0], length), jnp.float32)
    for state_index in range(decay_rate.shape[1]):
        total_sum = total_sum + weight[:, state_index : state_index + 1] * jnp.exp(
            -decay_speed[:, state_index : state_index + 1] * offsets[None, :]
        )
    return total_sum


def phase_table(row_count, col_count, period):
    first_ids = jnp.arange(row_count, dtype=jnp.int32)[:, None]
    second_ids = jnp.arange(col_count, dtype=jnp.int32)[None, :]
    angles = (first_ids * second_ids % period).astype(jnp.float32) * (2.0 * math.pi / period)
    return (jnp.cos(angles), jnp.sin(angles))


def exact_einsum(form, left_side, right_side):
    return jnp.einsum(form, left_side, right_side, precision=lax.Precision.HIGHEST)


def spectrum(signal, low_len, high_len):
    row_count = signal.shape[0]
    total_len = low_len * high_len
    grid_rows = signal.reshape(row_count, high_len, low_len)
    cos_high, sin_high = phase_table(high_len, high_len, high_len)
    real_part = exact_einsum("rmn,mk->rkn", grid_rows, cos_high)
    imag_part = -exact_einsum("rmn,mk->rkn", grid_rows, sin_high)
    cos_twist, sin_twist = phase_table(high_len, low_len, total_len)
    real_part, imag_part = (
        real_part * cos_twist + imag_part * sin_twist,
        imag_part * cos_twist - real_part * sin_twist,
    )
    cos_low, sin_low = phase_table(low_len, low_len, low_len)
    out_real = exact_einsum("rkn,nj->rkj", real_part, cos_low) + exact_einsum(
        "rkn,nj->rkj", imag_part, sin_low
    )
    out_imag = exact_einsum("rkn,nj->rkj", imag_part, cos_low) - exact_einsum(
        "rkn,nj->rkj", real_part, sin_low
    )
    return (out_real, out_imag)


def signal_of(real_part, imag_part, low_len, high_len, keep_len):
    row_count = real_part.shape[0]
    total_len = low_len * high_len
    cos_low, sin_low = phase_table(low_len, low_len, low_len)
    mid_real = exact_einsum("rkj,nj->rkn", real_part, cos_low) - exact_einsum(
        "rkj,nj->rkn", imag_part, sin_low
    )
    mid_imag = exact_einsum("rkj,nj->rkn", real_part, sin_low) + exact_einsum(
        "rkj,nj->rkn", imag_part, cos_low
    )
    cos_twist, sin_twist = phase_table(high_len, low_len, total_len)
    turn_real = mid_real * cos_twist - mid_imag * sin_twist
    turn_imag = mid_real * sin_twist + mid_imag * cos_twist
    cos_high, sin_high = phase_table(high_len, high_len, high_len)
    grid_rows = exact_einsum("rkn,km->rmn", turn_real, cos_high) - exact_einsum(
        "rkn,km->rmn", turn_imag, sin_high
    )
    return grid_rows.reshape(row_count, total_len)[:, :keep_len] / total_len


def padded(values):
    return jnp.concatenate([values, jnp.zeros_like(values)], axis=-1)


def norm_parts(values):
    center = values - jnp.mean(values, axis=-1, keepdims=True)
    inverse_dev = lax.rsqrt(jnp.mean(center * center, axis=-1, keepdims=True) + 1e-05)
    return (center * inverse_dev, inverse_dev)


def plain_norm_back(grad_values, scaled, inverse_dev, gain_vector):
    weighted = grad_values * gain_vector.astype(jnp.float32)
    return inverse_dev * (
        weighted
        - jnp.mean(weighted, axis=-1, keepdims=True)
        - scaled * jnp.mean(weighted * scaled, axis=-1, keepdims=True)
    )


def matmul(left_side, right_side):
    return jnp.einsum("...i,ij->...j", left_side, right_side, preferred_element_type=jnp.float32)


def matmul_t(left_side, right_side):
    return jnp.einsum("...j,ij->...i", left_side, right_side, preferred_element_type=jnp.float32)


def outer_sum(left_side, right_side):
    return jnp.einsum(
        "ri,rj->ij",
        left_side.reshape(-1, left_side.shape[-1]),
        right_side.reshape(-1, right_side.shape[-1]),
        preferred_element_type=jnp.float32,
    )


def take_rows(rows_table, row_ids):
    return jnp.take(rows_table, row_ids, axis=0)


def plain(
    activations,
    cotangent,
    block_sizes,
    context_back,
    first_gain,
    first_bias,
    w_query,
    w_key,
    w_value,
    w_out,
    second_gain,
    second_bias,
    w_up,
    w_down,
    decay_rate,
    input_map,
    output_map,
    step_size,
    skip_gain,
):
    seq_ways = lax.axis_size("seq")
    place = lax.axis_index("seq")
    seq_count, tokens, model_width = activations.shape
    channels = decay_rate.shape[0]
    length = tokens * seq_ways
    sub_len = min(BLK_A, tokens)
    sub_count = tokens // sub_len
    shift_count = max(BLK_B // tokens - 1, 0)
    head_dim = model_width // HEADS
    score_scale = head_dim ** (-0.5)
    per_dev = sub_count * CTX
    low_len = 2 * seq_ways
    (
        gain_one,
        bias_one,
        query_full,
        key_full,
        value_full,
        out_full,
        gain_two,
        bias_two,
        up_full,
        down_full,
    ) = (
        lax.all_gather(first_gain, "seq", axis=0, tiled=True),
        lax.all_gather(first_bias, "seq", axis=0, tiled=True),
        lax.all_gather(w_query, "seq", axis=0, tiled=True),
        lax.all_gather(w_key, "seq", axis=0, tiled=True),
        lax.all_gather(w_value, "seq", axis=0, tiled=True),
        lax.all_gather(w_out, "seq", axis=0, tiled=True),
        lax.all_gather(second_gain, "seq", axis=0, tiled=True),
        lax.all_gather(second_bias, "seq", axis=0, tiled=True),
        lax.all_gather(w_up, "seq", axis=0, tiled=True),
        lax.all_gather(w_down, "seq", axis=0, tiled=True),
    )
    scaled_one, inverse_one = norm_parts(activations)
    lowered = (scaled_one * gain_one.astype(jnp.float32) + bias_one.astype(jnp.float32)).astype(
        jnp.bfloat16
    )
    by_channel = lax.all_to_all(
        jnp.swapaxes(lowered, 1, 2), "seq", split_axis=1, concat_axis=2, tiled=True
    )
    channel_in = by_channel.astype(jnp.float32)
    kernel, kernel_pull = jax.vjp(
        lambda a, b, c, e: ssm_kernel(a, b, c, e, length),
        decay_rate,
        input_map,
        output_map,
        step_size,
    )
    input_real, input_imag = spectrum(padded(channel_in.reshape(-1, length)), low_len, tokens)
    input_real = input_real.reshape(seq_count, channels, tokens, low_len)
    input_imag = input_imag.reshape(seq_count, channels, tokens, low_len)
    kernel_real, kernel_imag = spectrum(padded(kernel), low_len, tokens)
    conv_real = input_real * kernel_real - input_imag * kernel_imag
    conv_imag = input_real * kernel_imag + input_imag * kernel_real
    convolved = signal_of(
        conv_real.reshape(-1, tokens, low_len),
        conv_imag.reshape(-1, tokens, low_len),
        low_len,
        tokens,
        length,
    )
    states = convolved.reshape(seq_count, channels, length) + skip_gain[None, :, None] * channel_in
    targets = (
        jnp.arange(seq_ways, dtype=jnp.int32)[:, None] * tokens
        + jnp.arange(sub_count, dtype=jnp.int32)[None, :] * sub_len
    )
    sizes_three = block_sizes[:, None, None]
    block_start = targets[None] // sizes_three * sizes_three
    positions = block_start[..., None] - context_back
    valid_all = positions >= 0
    picks = jnp.maximum(positions, 0).reshape(seq_count, -1)
    position_major = jnp.swapaxes(states, 1, 2)
    picked = jax.vmap(take_rows)(position_major, picks)
    picked = jnp.where(valid_all.reshape(seq_count, -1, 1), picked, 0.0).astype(jnp.bfloat16)
    picked = jnp.swapaxes(picked, 1, 2)
    arrived = lax.all_to_all(
        picked.reshape(seq_count, channels, seq_ways, per_dev),
        "seq",
        split_axis=2,
        concat_axis=1,
        tiled=True,
    )
    context = jnp.swapaxes(arrived.reshape(seq_count, model_width, per_dev), 1, 2)
    own_valid = lax.dynamic_index_in_dim(valid_all, place, axis=1, keepdims=False).reshape(
        seq_count, per_dev
    )
    queries = matmul(lowered, query_full).astype(jnp.bfloat16)
    keys_own = matmul(lowered, key_full).astype(jnp.bfloat16)
    values_own = matmul(lowered, value_full).astype(jnp.bfloat16)
    ctx_keys = matmul(context, key_full).astype(jnp.bfloat16)
    ctx_values = matmul(context, value_full).astype(jnp.bfloat16)
    key_parts = [ctx_keys]
    value_parts = [ctx_values]
    key_places = []
    token_ids = jnp.arange(tokens, dtype=jnp.int32)
    for distance in range(shift_count, 0, -1):
        far_keys, far_values = from_behind((keys_own, values_own), "seq", distance)
        key_parts.append(far_keys)
        value_parts.append(far_values)
        key_places.append((place - distance) * tokens + token_ids)
    key_parts.append(keys_own)
    value_parts.append(values_own)
    key_places.append(place * tokens + token_ids)
    all_keys = jnp.concatenate(key_parts, axis=1)
    all_values = jnp.concatenate(value_parts, axis=1)
    key_pos = jnp.concatenate(key_places)
    query_pos = place * tokens + token_ids
    same_block = key_pos[None, None, :] // sizes_three == query_pos[None, :, None] // sizes_three
    causal = key_pos[None, None, :] <= query_pos[None, :, None]
    ctx_allowed = (
        (token_ids // sub_len)[:, None] == (jnp.arange(per_dev, dtype=jnp.int32) // CTX)[None, :]
    )[None] & own_valid[:, None, :]
    allowed = jnp.concatenate([ctx_allowed, same_block & causal], axis=2)

    def split_heads(values):
        return values.reshape(values.shape[0], values.shape[1], HEADS, head_dim)

    def scores_of():
        raw_scores = (
            jnp.einsum(
                "sqhd,skhd->shqk",
                split_heads(queries),
                split_heads(all_keys),
                preferred_element_type=jnp.float32,
            )
            * score_scale
        )
        return jnp.where(allowed[:, None], raw_scores, -1e30)

    scores = scores_of()
    row_top = jnp.max(scores, axis=-1, keepdims=True)
    log_total = row_top + jnp.log(jnp.sum(jnp.exp(scores - row_top), axis=-1, keepdims=True))
    probs_low = jnp.exp(scores - log_total).astype(jnp.bfloat16)
    attended = jnp.einsum(
        "shqk,skhd->sqhd", probs_low, split_heads(all_values), preferred_element_type=jnp.float32
    )
    mixed_out = attended.reshape(seq_count, tokens, model_width).astype(jnp.bfloat16)
    first_sum = activations + matmul(mixed_out, out_full)
    scaled_two, inverse_two = norm_parts(first_sum)
    normal_two = (scaled_two * gain_two.astype(jnp.float32) + bias_two.astype(jnp.float32)).astype(
        jnp.bfloat16
    )
    pre_gate = matmul(normal_two, up_full)
    hidden, gate_pull = jax.vjp(smooth_gate, pre_gate)
    hidden_low = hidden.astype(jnp.bfloat16)
    result = first_sum + matmul(hidden_low, down_full)
    grad_down = outer_sum(hidden_low, cotangent)
    grad_hidden = matmul_t(cotangent, down_full)
    grad_pre = gate_pull(grad_hidden)[0].astype(jnp.bfloat16)
    grad_up = outer_sum(normal_two, grad_pre)
    grad_norm_two = matmul_t(grad_pre, up_full)
    grad_gain_two = jnp.sum(grad_norm_two * scaled_two, axis=(0, 1))
    grad_bias_two = jnp.sum(grad_norm_two, axis=(0, 1))
    grad_first = cotangent.astype(jnp.float32) + plain_norm_back(
        grad_norm_two, scaled_two, inverse_two, gain_two
    )
    grad_branch = grad_first.astype(jnp.bfloat16)
    grad_out = outer_sum(mixed_out, grad_branch)
    grad_mixed = split_heads(matmul_t(grad_branch, out_full).astype(jnp.bfloat16))
    scores = scores_of()
    probabilities = jnp.exp(scores - log_total)
    probs_low = probabilities.astype(jnp.bfloat16)
    grad_probs = jnp.einsum(
        "sqhd,skhd->shqk", grad_mixed, split_heads(all_values), preferred_element_type=jnp.float32
    )
    grad_all_values = jnp.einsum(
        "shqk,sqhd->skhd", probs_low, grad_mixed, preferred_element_type=jnp.float32
    )
    grad_scores = (
        probabilities * (grad_probs - jnp.sum(probabilities * grad_probs, axis=-1, keepdims=True))
    ).astype(jnp.bfloat16)
    grad_queries = (
        jnp.einsum(
            "shqk,skhd->sqhd",
            grad_scores,
            split_heads(all_keys),
            preferred_element_type=jnp.float32,
        )
        * score_scale
    )
    grad_queries = grad_queries.reshape(seq_count, tokens, model_width).astype(jnp.bfloat16)
    grad_all_keys = (
        jnp.einsum(
            "shqk,sqhd->skhd", grad_scores, split_heads(queries), preferred_element_type=jnp.float32
        )
        * score_scale
    )
    grad_all_keys = grad_all_keys.reshape(seq_count, -1, model_width)
    grad_all_values = grad_all_values.reshape(seq_count, -1, model_width)
    grad_ctx_keys = grad_all_keys[:, :per_dev]
    grad_ctx_values = grad_all_values[:, :per_dev]
    grad_keys = grad_all_keys[:, -tokens:]
    grad_values = grad_all_values[:, -tokens:]
    for distance in range(shift_count, 0, -1):
        begin = per_dev + (shift_count - distance) * tokens
        back_keys, back_values = (
            from_behind(
                grad_all_keys[:, begin : begin + tokens].astype(jnp.bfloat16), "seq", -distance
            ).astype(jnp.float32),
            from_behind(
                grad_all_values[:, begin : begin + tokens].astype(jnp.bfloat16), "seq", -distance
            ).astype(jnp.float32),
        )
        grad_keys = grad_keys + back_keys
        grad_values = grad_values + back_values
    grad_keys_low = grad_keys.astype(jnp.bfloat16)
    grad_values_low = grad_values.astype(jnp.bfloat16)
    context_wide = context.astype(jnp.float32)
    grad_query_w = outer_sum(lowered, grad_queries)
    grad_key_w = outer_sum(lowered, grad_keys_low) + outer_sum(context_wide, grad_ctx_keys)
    grad_value_w = outer_sum(lowered, grad_values_low) + outer_sum(context_wide, grad_ctx_values)
    grad_normal_one = (
        matmul_t(grad_queries, query_full)
        + matmul_t(grad_keys_low, key_full)
        + matmul_t(grad_values_low, value_full)
    )
    grad_context = matmul_t(grad_ctx_keys, key_full) + matmul_t(grad_ctx_values, value_full)
    sent_back = jnp.swapaxes(grad_context, 1, 2).reshape(seq_count, model_width, 1, per_dev)
    returned = lax.all_to_all(
        sent_back.astype(jnp.bfloat16), "seq", split_axis=1, concat_axis=2, tiled=True
    ).astype(sent_back.dtype)
    returned = jnp.where(
        valid_all.reshape(seq_count, 1, -1), returned.reshape(seq_count, channels, -1), 0.0
    )
    segment_ids = (jnp.arange(seq_count, dtype=jnp.int32)[:, None] * length + picks).reshape(-1)
    flat_rows = jnp.swapaxes(returned, 1, 2).reshape(-1, channels)
    grad_states = jax.ops.segment_sum(flat_rows, segment_ids, num_segments=seq_count * length)
    grad_states = jnp.swapaxes(grad_states.reshape(seq_count, length, channels), 1, 2)
    grad_real, grad_imag = spectrum(padded(grad_states.reshape(-1, length)), low_len, tokens)
    grad_real = grad_real.reshape(seq_count, channels, tokens, low_len)
    grad_imag = grad_imag.reshape(seq_count, channels, tokens, low_len)
    back_real = grad_real * kernel_real + grad_imag * kernel_imag
    back_imag = grad_imag * kernel_real - grad_real * kernel_imag
    grad_conv = signal_of(
        back_real.reshape(-1, tokens, low_len),
        back_imag.reshape(-1, tokens, low_len),
        low_len,
        tokens,
        length,
    )
    grad_conv = grad_conv.reshape(seq_count, channels, length)
    corr_real = jnp.sum(grad_real * input_real + grad_imag * input_imag, axis=0)
    corr_imag = jnp.sum(grad_imag * input_real - grad_real * input_imag, axis=0)
    grad_kernel = signal_of(corr_real, corr_imag, low_len, tokens, length)
    grad_rate, grad_in_map, grad_out_map, grad_step = kernel_pull(grad_kernel)
    grad_skip = jnp.sum(grad_states * channel_in, axis=(0, 2))
    grad_channel = grad_conv + skip_gain[None, :, None] * grad_states
    back_tokens = lax.all_to_all(
        grad_channel.astype(jnp.bfloat16), "seq", split_axis=2, concat_axis=1, tiled=True
    ).astype(grad_channel.dtype)
    grad_normal_one = grad_normal_one + jnp.swapaxes(back_tokens, 1, 2)
    grad_gain_one = jnp.sum(grad_normal_one * scaled_one, axis=(0, 1))
    grad_bias_one = jnp.sum(grad_normal_one, axis=(0, 1))
    grad_inputs = grad_first + plain_norm_back(grad_normal_one, scaled_one, inverse_one, gain_one)
    shares = (
        lax.psum_scatter(
            grad_gain_one.astype(jnp.bfloat16), "seq", scatter_dimension=0, tiled=True
        ).astype(jnp.float32),
        lax.psum_scatter(
            grad_bias_one.astype(jnp.bfloat16), "seq", scatter_dimension=0, tiled=True
        ).astype(jnp.float32),
        lax.psum_scatter(
            grad_query_w.astype(jnp.bfloat16), "seq", scatter_dimension=0, tiled=True
        ).astype(jnp.float32),
        lax.psum_scatter(
            grad_key_w.astype(jnp.bfloat16), "seq", scatter_dimension=0, tiled=True
        ).astype(jnp.float32),
        lax.psum_scatter(
            grad_value_w.astype(jnp.bfloat16), "seq", scatter_dimension=0, tiled=True
        ).astype(jnp.float32),
        lax.psum_scatter(
            grad_out.astype(jnp.bfloat16), "seq", scatter_dimension=0, tiled=True
        ).astype(jnp.float32),
        lax.psum_scatter(
            grad_gain_two.astype(jnp.bfloat16), "seq", scatter_dimension=0, tiled=True
        ).astype(jnp.float32),
        lax.psum_scatter(
            grad_bias_two.astype(jnp.bfloat16), "seq", scatter_dimension=0, tiled=True
        ).astype(jnp.float32),
        lax.psum_scatter(
            grad_up.astype(jnp.bfloat16), "seq", scatter_dimension=0, tiled=True
        ).astype(jnp.float32),
        lax.psum_scatter(
            grad_down.astype(jnp.bfloat16), "seq", scatter_dimension=0, tiled=True
        ).astype(jnp.float32),
    )
    summed = (
        lax.psum(shares[0].astype(jnp.bfloat16), "dp").astype(jnp.float32),
        lax.psum(shares[1].astype(jnp.bfloat16), "dp").astype(jnp.float32),
        lax.psum(shares[2].astype(jnp.bfloat16), "dp").astype(jnp.float32),
        lax.psum(shares[3].astype(jnp.bfloat16), "dp").astype(jnp.float32),
        lax.psum(shares[4].astype(jnp.bfloat16), "dp").astype(jnp.float32),
        lax.psum(shares[5].astype(jnp.bfloat16), "dp").astype(jnp.float32),
        lax.psum(shares[6].astype(jnp.bfloat16), "dp").astype(jnp.float32),
        lax.psum(shares[7].astype(jnp.bfloat16), "dp").astype(jnp.float32),
        lax.psum(shares[8].astype(jnp.bfloat16), "dp").astype(jnp.float32),
        lax.psum(shares[9].astype(jnp.bfloat16), "dp").astype(jnp.float32),
        lax.psum(grad_rate.astype(jnp.bfloat16), "dp").astype(jnp.float32),
        lax.psum(grad_in_map.astype(jnp.bfloat16), "dp").astype(jnp.float32),
        lax.psum(grad_out_map.astype(jnp.bfloat16), "dp").astype(jnp.float32),
        lax.psum(grad_step.astype(jnp.bfloat16), "dp").astype(jnp.float32),
        lax.psum(grad_skip.astype(jnp.bfloat16), "dp").astype(jnp.float32),
    )
    summed = tuple(summed)
    return (
        result,
        grad_inputs,
        summed[0],
        summed[1],
        summed[2],
        summed[3],
        summed[4],
        summed[5],
        summed[6],
        summed[7],
        summed[8],
        summed[9],
        summed[10],
        summed[11],
        summed[12],
        summed[13],
        summed[14],
    )


def solution(mesh):
    dp_ways, seq_ways = mesh.shape["dp"], mesh.shape["seq"]
    lone, data, flat, cut = P(), P("dp", "seq", None), P("seq"), P("seq", None)
    in_specs = (data, data, P("dp"), lone, flat, flat, cut, cut, cut, cut, flat, flat, cut, cut, cut, cut, cut, flat, flat)
    out_specs = (data, data, flat, flat, cut, cut, cut, cut, flat, flat, cut, cut, cut, cut, cut, flat, flat)

    def run(activations, *others):
        seqs, length, model = activations.shape
        tokens = length // seq_ways
        if (seqs, dp_ways, seq_ways, tokens, model) != (4, 4, 2 * TP, TOKENS, HEADS * LANES):
            return jax.shard_map(plain, mesh=mesh, in_specs=in_specs, out_specs=out_specs, check_vma=False)(activations, *others)
        fine = Mesh(mesh.devices.reshape(2, 2, 2, TP), ("y", "core", "span", "tp"))
        names = {"dp": ("y", "core"), "seq": ("span", "tp")}
        split = lambda specs: tuple(P(*(names.get(a) for a in spec)) for spec in specs)
        whole = jax.shard_map(by_spans, mesh=fine, in_specs=split(in_specs), out_specs=split(out_specs), check_vma=False)
        return whole(activations, *others)

    return run
```

```python
import functools
import math

import jax
import jax.numpy as jnp
from jax import lax
from jax.experimental import pallas as pl
from jax.experimental.pallas import tpu as pltpu
from jax.sharding import Mesh
from jax.sharding import PartitionSpec as P

HEADS = 8
CTX = 128
BLK_A = 256
BLK_B = 512
TP = 4
TOKENS = 128
LANES = 128
UNITS = 256
STATES = 16
CHUNKS = 8
NEG = -1e30
f32 = jnp.float32
bf16 = jnp.bfloat16
LIMIT = 24
SWAP = [(0, 1), (1, 0)]
PER_US = 16000000000
MICROSECONDS = dict(
    norm_one_kernel=0.85,
    scan_kernel=4.6,
    carry_kernel=2.0,
    qkv_kernel=2.3,
    attend_kernel=4.0,
    norm_two_kernel=1.0,
    units_kernel=3.0,
    hidden_kernel=5.4,
    units_weights_kernel=3.0,
    units_one_kernel=1.1,
    norm_two_back_kernel=1.2,
    attend_back_kernel=4.8,
    attend_weights_kernel=2.4,
    context_sum_kernel=0.65,
    heads_one_kernel=0.8,
    units_two_kernel=0.8,
    result_kernel=1.8,
    scan_back_kernel=4.0,
    units_three_kernel=0.7,
    carry_back_kernel=1.9,
    heads_two_kernel=0.9,
    sums_kernel=0.9,
    units_four_kernel=0.6,
    last_kernel=2.1,
    heads_three_kernel=0.6,
    heads_four_kernel=0.6,
    units_home_kernel=3.0,
    heads_home_kernel=2.1,
    pack_kernel=0.7,
    lines_kernel=0.5,
    lowered_back_kernel=1.7,
    share_kernel=2.5,
    lines_sum_kernel=0.5,
)


SPAN, PLACE, ROW, CORE, WIDE = range(5)


def call(kernel, outs, *args, scratch=(), loose=(), after=(), limit=LIMIT):
    count = len(args)
    vmem, free = pl.BlockSpec(memory_space=pltpu.VMEM), pl.BlockSpec(memory_space=pl.ANY)
    specs = [pl.BlockSpec(memory_space=pltpu.SMEM)] + [free if i in loose else vmem for i in range(1, count)] + [free] * len(after)

    def inner(*refs):
        kernel(*refs[:count], *refs[count + len(after) :])

    return pl.pallas_call(
        inner,
        out_shape=[jax.ShapeDtypeStruct(shape, kind) for shape, kind in outs],
        in_specs=specs,
        out_specs=[vmem] * len(outs),
        scratch_shapes=list(scratch),
        compiler_params=pltpu.CompilerParams(vmem_limit_bytes=limit * 1024 * 1024),
        cost_estimate=pl.CostEstimate(flops=int(MICROSECONDS[kernel.__name__] * PER_US), bytes_accessed=0, transcendentals=0),
    )(*args, *after)


def part(index, size):
    return pl.ds(pl.multiple_of(index * size, size), size)


def channel_part(scal, s, rank):
    return part((s ^ scal[SPAN]) * TP + rank, LANES)


def dot(a, b, ca, cb):
    return lax.dot_general(a, b, (((ca,), (cb,)), ((), ())), preferred_element_type=f32)


def wide(ref):
    return ref[...].astype(f32)


def send_all(copies, sems):
    copies = [pltpu.make_async_copy(a, b, sems.at[i]) for i, (a, b) in enumerate(copies)]
    for copy in copies:
        copy.start()
    for copy in copies:
        copy.wait()


def share_kernel(scal, wq, wk, wv, out, down, up, send, out_send, down_send, sems):
    core, row = scal[CORE], scal[ROW]
    copies = [(out.at[part(core, 64), :], out_send), (down.at[part(core * 2 + row, LANES), :], down_send)]
    for to in range(2 * TP):
        for s in range(2):
            there = ((s * TP + to % TP) * 2 + core) * 2 + row
            copies.append((up.at[:, part(there, LANES)], send.at[to, pl.ds(s * TOKENS, TOKENS), :]))
    copies = [pltpu.make_async_copy(a, b, sems.at[i]) for i, (a, b) in enumerate(copies)]
    for copy in copies:
        copy.start()
    for rank in range(TP):
        for m, w in enumerate((wq, wk, wv)):
            value = w[part(row, 64), part(core * TP + rank, LANES)]
            for s in range(2):
                send[s * TP + rank, pl.ds(2 * TOKENS + m * 64, 64), :] = value
    for copy in copies:
        copy.wait()


def pack_kernel(scal, rate, inward, outward, step, skip, g1, b1, g2, b2, out, vecs, sems):
    places = [pl.ds(i * STATES, STATES) for i in range(3)] + [pl.ds(3 * STATES + i, 1) for i in range(2)]
    copies = [(ref, out.at[at, :]) for ref, at in zip((rate, inward, outward, step, skip), places)]
    copies += [(ref, vecs.at[i]) for i, ref in enumerate((g1, b1, g2, b2))]
    copies = [pltpu.make_async_copy(a, b, sems.at[i]) for i, (a, b) in enumerate(copies)]
    for copy in copies:
        copy.start()
    for copy in copies:
        copy.wait()
    for i in range(4):
        out[3 * STATES + 2 + i : 3 * STATES + 3 + i, :] = vecs[i].astype(f32)
    out[3 * STATES + 6 :, :] = jnp.zeros((out.shape[0] - 3 * STATES - 6, LANES), f32)


def lines_kernel(scal, own, far, vec):
    for ref, s in ((own, scal[SPAN]), (far, 1 - scal[SPAN])):
        vec[part(s, 8), :] = jnp.concatenate([ref[50:54, :], jnp.zeros((4, LANES), f32)], axis=0)


def norm_rows(x):
    center = x - jnp.mean(x, axis=1, keepdims=True)
    inverse = lax.rsqrt(jnp.mean(center * center, axis=1, keepdims=True) + 1e-05)
    return center * inverse, inverse


def gather_lines(scal, vecs, lines):
    for j, vec in enumerate(vecs):
        for s in range(2):
            lines[:, part(s * TP + (scal[PLACE] ^ j), LANES)] = vec[s * 8 : s * 8 + 8, :]


def norm_one_kernel(scal, x, v0, v1, v2, v3, low, lines):
    gather_lines(scal, (v0, v1, v2, v3), lines)
    scaled, _ = norm_rows(x[...])
    low[...] = (scaled * lines[0:1, :] + lines[1:2, :]).astype(bf16)


def sum_of(own, a, b, c):
    return (wide(own) + wide(a)) + (wide(b) + wide(c))


def norm_two_kernel(scal, x, own, a, b, c, vec, total, low):
    first = x[...] + sum_of(own, a, b, c)
    total[...] = first
    scaled, _ = norm_rows(first)
    low[...] = (scaled * vec[2:3, :] + vec[3:4, :]).astype(bf16)


def norm_back(grad, scaled, inverse, gain):
    e = grad * gain
    return inverse * (e - jnp.mean(e, axis=1, keepdims=True) - scaled * jnp.mean(e * scaled, axis=1, keepdims=True))


def norm_two_back_kernel(scal, total, own, a, b, c, cot, vec, grad_first, low, lines):
    grad = sum_of(own, a, b, c)
    scaled, inverse = norm_rows(total[...])
    value = cot[...].astype(f32) + norm_back(grad, scaled, inverse, vec[2:3, :])
    grad_first[...] = value
    low[...] = value.astype(bf16)
    lines[0:1, :] = jnp.sum(grad * scaled, axis=0, keepdims=True)
    lines[1:2, :] = jnp.sum(grad, axis=0, keepdims=True)
    lines[2:8, :] = jnp.zeros((6, lines.shape[1]), f32)


def last_kernel(scal, x, vec, grad_first, own, a, b, c, p0, p1, p2, p3, lines_two, out, lines, grad):
    grad[...] = sum_of(own, a, b, c)
    for j, p in enumerate((p0, p1, p2, p3)):
        for s in range(2):
            lanes = channel_part(scal, s, scal[PLACE] ^ j)
            grad[:, lanes] = grad[:, lanes] + p[:, pl.ds(s * LANES, LANES)].astype(f32)
    scaled, inverse = norm_rows(x[...])
    out[...] = grad_first[...] + norm_back(grad[...], scaled, inverse, vec[0:1, :])
    gain = jnp.sum(grad[...] * scaled, axis=0, keepdims=True)
    bias = jnp.sum(grad[...], axis=0, keepdims=True)
    for n in range(lines.shape[0]):
        lanes = slice(n * LANES, (n + 1) * LANES)
        lines[n, 0:1, :] = gain[:, lanes]
        lines[n, 1:2, :] = bias[:, lanes]
        lines[n, 2:4, :] = lines_two[0:2, lanes]
        lines[n, 4:8, :] = jnp.zeros((4, LANES), f32)


def lines_sum_kernel(scal, parts, sums, out):
    out[0:8, :] = jnp.sum(parts[...], axis=0)
    out[8:, :] = sums[...]


def spread(row):
    return jnp.broadcast_to(row, (CHUNKS, LANES))


def power(base, times):
    for _ in range(int(math.log2(times))):
        base = base * base
    return base


def total_of(parts):
    while len(parts) > 1:
        parts = [parts[i] + parts[i + 1] for i in range(0, len(parts), 2)]
    return parts[0]


def one_hot(spots, rows):
    return (spots[...] == lax.broadcasted_iota(jnp.int32, (spots.shape[0], rows), 1)).astype(bf16)


def own_channels(scal, xs, parts):
    place = scal[PLACE]
    for j, x in enumerate(parts):
        for s in range(2):
            xs[s, part(place ^ j, TOKENS), :] = x[:, channel_part(scal, s, place)].astype(f32)


def scan(reverse, xs, a_ref, w_ref, skips, y_ref, end, sh, ih, sq=None, kept=None):
    states = a_ref.shape[0]
    steps = xs.shape[1] // CHUNKS

    def at(step):
        return pl.ds(steps - 1 - step if reverse else step, CHUNKS, stride=steps)

    for s in range(xs.shape[0]):
        cols = pl.ds(s * LANES, LANES)
        rate = [spread(a_ref[n : n + 1, cols]) for n in range(states)]
        ih[0] = jnp.zeros((CHUNKS, LANES), f32)
        zero = ih[0]

        def local(step, carry):
            x = xs[s, at(step), :]
            if sq is not None:
                h, q = carry
                q = tuple(a * (u + v) for a, u, v in zip(rate, q, h))
            else:
                (h,) = carry
            h = tuple(a * v + x for a, v in zip(rate, h))
            return (h, q) if sq is not None else (h,)

        done = lax.fori_loop(0, steps, local, ((zero,) * states,) * (1 if sq is None else 2), unroll=4)
        for n in range(states):
            sh[n] = done[0][n]
            if sq is not None:
                sq[n] = done[1][n]
        jump = power(a_ref[:, cols], steps)
        hold = jnp.zeros((states, LANES), f32)
        hold_q = jnp.zeros((states, LANES), f32)
        for k in range(CHUNKS):
            k = CHUNKS - 1 - k if reverse else k
            ih[:, k, :] = hold
            if sq is not None:
                hold_q = jump * (hold_q + float(steps) * hold) + sq[:, k, :]
            hold = jump * hold + sh[:, k, :]
        if kept is not None:
            kept[0, s] = sh[...]
            kept[1, s] = sq[...]
        end(s, hold, hold_q)
        weight = [spread(w_ref[n : n + 1, cols]) for n in range(states)]
        skip = spread(skips[s][49:50, :])

        def emit(step, h):
            x = xs[s, at(step), :]
            h = tuple(a * v + x for a, v in zip(rate, h))
            y_ref[s, at(step), :] = total_of([w * v for w, v in zip(weight, h)]) + skip * x
            return h

        lax.fori_loop(0, steps, emit, tuple(ih[n] for n in range(states)), unroll=4)


def scan_kernel(scal, x0, x1, x2, x3, ssm0, ssm1, spots, y, to_next, ends, decay, mix, kept, xs, low, sh, sq, ih):
    own_channels(scal, xs, (x0, x1, x2, x3))
    n = decay.shape[0]
    for s, ssm in enumerate((ssm0, ssm1)):
        cols = pl.ds(s * LANES, LANES)
        step = ssm[48:49, :]
        decay[:, cols] = jnp.exp(-step * ssm[0:n, :])
        mix[:, cols] = ssm[32:48, :] * ssm[16:32, :] * step

    def end(s, h, q):
        other = pl.ds((1 - s) * LANES, LANES)
        ends[0:n, other] = h
        ends[n : 2 * n, other] = q

    scan(False, xs, decay, mix, (ssm0, ssm1), y, end, sh, ih, sq, kept)
    for s in range(2):
        low[:, pl.ds((1 - s) * LANES, LANES)] = y[s].astype(bf16)
    to_next[...] = dot(one_hot(spots, low.shape[0]), low[...], 1, 0).astype(bf16)


def carry(reverse, y_ref, a_ref, w_ref, h_ref, out, ih):
    states = a_ref.shape[0]
    steps = y_ref.shape[1] // CHUNKS

    def at(step):
        return pl.ds(steps - 1 - step if reverse else step, CHUNKS, stride=steps)

    for s in range(y_ref.shape[0]):
        cols = pl.ds(s * LANES, LANES)
        rate = [spread(a_ref[n : n + 1, cols]) for n in range(states)]
        jump = power(a_ref[:, cols], steps)
        hold = w_ref[:, cols] * h_ref[0:states, cols]
        for k in range(CHUNKS):
            ih[:, CHUNKS - 1 - k if reverse else k, :] = hold
            hold = jump * hold

        def emit(step, h):
            h = tuple(a * v for a, v in zip(rate, h))
            out[s, at(step), :] = y_ref[s, at(step), :] + total_of(list(h))
            return h

        lax.fori_loop(0, steps, emit, tuple(ih[n] for n in range(states)), unroll=4)


def carry_kernel(scal, y, decay, mix, begin, from_last, spots, context, ih, ys, low):
    carry(False, y, decay, mix, begin, ys, ih)
    for s in range(2):
        low[:, pl.ds(s * LANES, LANES)] = ys[s].astype(bf16)
    context[...] = (dot(one_hot(spots, low.shape[0]), low[...], 1, 0) + wide(from_last)).astype(bf16)


def scan_back_kernel(scal, own, from_next, own_spots, next_spots, ssm0, ssm1, decay, mix, grad, y, ends, sh, ih):
    rows = y.shape[1]
    value = dot(one_hot(own_spots, rows), own[...], 0, 0) + dot(one_hot(next_spots, rows), from_next[...], 0, 0)
    for s in range(2):
        grad[s] = value[:, s * LANES : (s + 1) * LANES]

    def end(s, h, q):
        ends[:, pl.ds((1 - s) * LANES, LANES)] = h

    scan(True, grad, decay, mix, (ssm0, ssm1), y, end, sh, ih)


def carry_back_kernel(scal, y, decay, mix, begin, o0, o1, o2, o3, ih, ys):
    carry(True, y, decay, mix, begin, ys, ih)
    for j, out in enumerate((o0, o1, o2, o3)):
        for s in range(2):
            out[:, pl.ds(s * LANES, LANES)] = ys[s, part(scal[PLACE] ^ j, TOKENS), :].astype(bf16)


def sums_kernel(scal, x0, x1, x2, x3, gs, a_ref, begin, kept, out, xs, ih, iq):
    own_channels(scal, xs, (x0, x1, x2, x3))
    states = a_ref.shape[0]
    steps = xs.shape[1] // CHUNKS
    group = 8
    out[2 * states :, :] = jnp.zeros((out.shape[0] - 2 * states, out.shape[1]), f32)
    for s in range(xs.shape[0]):
        cols = pl.ds(s * LANES, LANES)
        jump = power(a_ref[:, cols], steps)
        hold, hold_q = begin[0:states, cols], begin[states : 2 * states, cols]
        for k in range(CHUNKS):
            ih[:, k, :] = hold
            iq[:, k, :] = hold_q
            hold_q = jump * (hold_q + float(steps) * hold) + kept[1, s, :, k, :]
            hold = jump * hold + kept[0, s, :, k, :]
        for base in range(0, states, group):
            rate = [spread(a_ref[n : n + 1, cols]) for n in range(base, base + group)]

            def gain(step, carried):
                h, q, sw, sq = carried
                at = pl.ds(step, CHUNKS, stride=steps)
                x, g = xs[s, at, :], gs[s, at, :]
                q = tuple(a * (u + v) for a, u, v in zip(rate, q, h))
                h = tuple(a * v + x for a, v in zip(rate, h))
                sw = tuple(u + g * v for u, v in zip(sw, h))
                sq = tuple(u + g * v for u, v in zip(sq, q))
                return h, q, sw, sq

            first = tuple(ih[base + n] for n in range(group)), tuple(iq[base + n] for n in range(group))
            none = tuple(v * 0.0 for v in first[0])
            _, _, sw, sq = lax.fori_loop(0, steps, gain, first + (none, none), unroll=2)
            for n in range(group):
                out[base + n : base + n + 1, cols] = jnp.sum(sw[n], axis=0, keepdims=True)
                out[states + base + n : states + base + n + 1, cols] = jnp.sum(sq[n], axis=0, keepdims=True)
        out[2 * states : 2 * states + 1, cols] = jnp.sum(xs[s] * gs[s], axis=0, keepdims=True)


def qkv_kernel(scal, x0, x1, x2, x3, w00, w01, w10, w11, w, qkv):
    for j, k, ref in ((0, 0, w00), (0, 1, w01), (1, 0, w10), (1, 1, w11)):
        for n in range(2 * TP):
            for m in range(3):
                there = part(2 * n + (scal[ROW] ^ k), 64)
                w[there, pl.ds((2 * m + j) * LANES, LANES)] = ref[n, pl.ds(2 * TOKENS + m * 64, 64), :]
    for j, x in enumerate((x0, x1, x2, x3)):
        qkv[part(scal[PLACE] ^ j, TOKENS), :] = dot(x[...], w[...], 1, 0).astype(bf16)


def masks(size, is_wide, ok_ref, sub):
    rows = lax.broadcasted_iota(jnp.int32, (size, size), 0)
    cols = lax.broadcasted_iota(jnp.int32, (size, size), 1)
    return ok_ref[sub : sub + 1, :] > 0.0, is_wide > 0, cols <= rows


def out_of_order(out_ref, lanes, value, sub, place):
    each = value.shape[0] // TOKENS
    for i in range(each):
        out_ref[part((sub * each + i) ^ place, TOKENS), lanes] = value[i * TOKENS : (i + 1) * TOKENS]


def probabilities(q, ctx_k, k_ref, size, sub, lanes, mask, scale):
    context, earlier, own = mask
    parts = [jnp.where(context, dot(q, ctx_k, 1, 1) * scale, NEG)]
    for other in range(sub):
        keys = k_ref[pl.ds(other * size, size), lanes]
        parts.append(jnp.where(earlier, dot(q, keys, 1, 1) * scale, NEG))
    parts.append(jnp.where(own, dot(q, k_ref[pl.ds(sub * size, size), lanes], 1, 1) * scale, NEG))
    top = functools.reduce(jnp.maximum, [jnp.max(s, axis=1, keepdims=True) for s in parts])
    parts = [jnp.exp(s - top) for s in parts]
    inverse = 1.0 / sum(jnp.sum(s, axis=1, keepdims=True) for s in parts)
    return [s * inverse for s in parts]


def attend_kernel(scal, ok, qkv, c0, c1, c2, c3, w, out_own, out_0, out_1, mixed, ckv, out_w, b0, b1, b2, b3):
    place, core = scal[PLACE], scal[CORE]
    width = qkv.shape[1] // 3
    dim = LANES
    own = core ^ scal[SPAN]
    out_w[part(own, dim), :] = out_own[...]
    out_w[part((1 - own) * 2 + core, 64), :] = out_0[...]
    out_w[part((1 - own) * 2 + 1 - core, 64), :] = out_1[...]
    total = None
    for j, c in enumerate((c0, c1, c2, c3)):
        for s in range(2):
            term = dot(c[:, pl.ds(s * LANES, LANES)], w[channel_part(scal, s, place ^ j), pl.ds(width, 2 * width)], 1, 0)
            total = term if total is None else total + term
    ckv[...] = total.astype(bf16)
    subs = ok.shape[0]
    size = qkv.shape[0] // subs
    scale = dim ** (-0.5)
    for sub in range(subs):
        mask = masks(size, scal[WIDE], ok, sub)
        here = pl.ds(sub * size, size)
        for h in range(width // dim):
            lq, lk, lv = (pl.ds(i * width + h * dim, dim) for i in range(3))
            ck = ckv[pl.ds(sub * CTX, CTX), pl.ds(h * dim, dim)]
            cv = ckv[pl.ds(sub * CTX, CTX), pl.ds(width + h * dim, dim)]
            probs = probabilities(qkv[here, lq], ck, qkv, size, sub, lk, mask, scale)
            value = dot(probs[0].astype(bf16), cv, 1, 0)
            for other in range(sub + 1):
                value += dot(probs[1 + other].astype(bf16), qkv[pl.ds(other * size, size), lv], 1, 0)
            out_of_order(mixed, pl.ds(h * dim, dim), value.astype(bf16), sub, place)
    for j, b in enumerate((b0, b1, b2, b3)):
        b[...] = dot(mixed[pl.ds(j * TOKENS, TOKENS), :], out_w[...], 1, 0).astype(bf16)


def attend_back_kernel(scal, ok, qkv, ckv, g0, g1, g2, g3, out_w, w, out, ctx, x0, x1, x2, x3, gms, acc):
    place = scal[PLACE]
    width = qkv.shape[1] // 3
    dim = LANES
    subs = ok.shape[0]
    size = qkv.shape[0] // subs
    scale = dim ** (-0.5)
    for j, g in enumerate((g0, g1, g2, g3)):
        gms[part(place ^ j, TOKENS), :] = dot(g[...], out_w[...], 1, 1).astype(bf16)
    acc[...] = jnp.zeros_like(acc)
    for sub in range(subs):
        mask = masks(size, scal[WIDE], ok, sub)
        here = pl.ds(sub * size, size)
        cs = pl.ds(sub * CTX, CTX)
        for h in range(width // dim):
            lq, lk, lv = (pl.ds(i * width + h * dim, dim) for i in range(3))
            lh, lhv = pl.ds(h * dim, dim), pl.ds(width + h * dim, dim)
            ck, cv = ckv[cs, lh], ckv[cs, lhv]
            q, gm = qkv[here, lq], gms[here, lh]
            probs = probabilities(q, ck, qkv, size, sub, lk, mask, scale)
            values = [cv] + [qkv[pl.ds(o * size, size), lv] for o in range(sub + 1)]
            keys = [ck] + [qkv[pl.ds(o * size, size), lk] for o in range(sub + 1)]
            grads = [dot(gm, v, 1, 1) for v in values]
            inner = sum(jnp.sum(p * g, axis=1, keepdims=True) for p, g in zip(probs, grads))
            scores = [(p * (g - inner)).astype(bf16) for p, g in zip(probs, grads)]
            grad_q = sum(dot(s, k, 1, 0) for s, k in zip(scores, keys))
            out_of_order(out, lq, (grad_q * scale).astype(bf16), sub, place)
            ctx[cs, lh] = (dot(scores[0], q, 0, 0) * scale).astype(bf16)
            ctx[cs, lhv] = dot(probs[0].astype(bf16), gm, 0, 0).astype(bf16)
            for o in range(sub + 1):
                there = pl.ds(o * size, size)
                acc[there, lh] += dot(scores[1 + o], q, 0, 0) * scale
                acc[there, lhv] += dot(probs[1 + o].astype(bf16), gm, 0, 0)
    for sub in range(subs):
        out_of_order(out, pl.ds(width, 2 * width), acc[pl.ds(sub * size, size), :].astype(bf16), sub, place)
    for j, x in enumerate((x0, x1, x2, x3)):
        for s in range(2):
            rows = channel_part(scal, s, place ^ j)
            x[:, pl.ds(s * LANES, LANES)] = dot(ctx[...], w[rows, pl.ds(width, 2 * width)], 1, 1).astype(bf16)


def lowered_back_kernel(scal, g, w, o0, o1, o2, o3):
    for j, out in enumerate((o0, o1, o2, o3)):
        out[...] = dot(g[pl.ds(j * TOKENS, TOKENS), :], w[...], 1, 1).astype(bf16)


def context_sum_kernel(scal, own, a, b, c, total, turned):
    value = ((wide(own) + wide(a)) + (wide(b) + wide(c))).astype(bf16)
    total[...] = value
    for s in range(2):
        turned[:, pl.ds((1 - s) * LANES, LANES)] = value[:, s * LANES : (s + 1) * LANES]


def attend_weights_kernel(scal, x0, x1, x2, x3, c0, c1, c2, c3, gqkv, gctx, mixed, g0, g1, g2, g3, send, keep, rows, acc, acc_out):
    place, core = scal[PLACE], scal[CORE]
    for j, x in enumerate((x0, x1, x2, x3)):
        rows[pl.ds(j * TOKENS, TOKENS), :] = x[...]
    width = gqkv.shape[1] // 3
    half = rows.shape[1] // 2
    for s in range(2):
        acc[pl.ds(s * half, half), :] = dot(rows[:, pl.ds(s * half, half)], gqkv[...], 0, 0)
    for j, c in enumerate((c0, c1, c2, c3)):
        for s in range(2):
            there = channel_part(scal, s, place ^ j)
            acc[there, pl.ds(width, 2 * width)] += dot(c[:, pl.ds(s * LANES, LANES)], gctx[...], 0, 0)
    size = acc.shape[0]
    for m in range(3):
        keep[pl.ds(m * size, size), :] = acc[:, pl.ds(2 * m * LANES, LANES)].astype(bf16)
        send[pl.ds(m * size, size), :] = acc[:, pl.ds((2 * m + 1) * LANES, LANES)].astype(bf16)
    for j, g in enumerate((g0, g1, g2, g3)):
        rows[pl.ds(j * TOKENS, TOKENS), :] = g[...]
    acc_out[...] = dot(mixed[...], rows[...], 0, 0)
    for s in range(2):
        head = core ^ scal[SPAN] ^ s
        for ref, side in ((keep, core), (send, 1 - core)):
            for i in range(2 * TP):
                there = pl.ds(3 * size + i * LANES + s * 64, 64)
                ref[there, :] = acc_out[part(head * 2 + side, 64), pl.ds(i * LANES, LANES)].astype(bf16)


def units_kernel(scal, c0, c1, c2, c3, u00, u01, u10, u11, own, d00, d01, d10, d11, up_w, down_w, ahead, rows):
    span, core, row = scal[SPAN], scal[CORE], scal[ROW]
    half = up_w.shape[0] // 2
    for j, k, ref in ((0, 0, u00), (0, 1, u01), (1, 0, u10), (1, 1, u11)):
        for n in range(2 * TP):
            for s in range(2):
                there = part((s * 2 + j) * 2 + (row ^ k), LANES)
                up_w[pl.ds(n * LANES, LANES), there] = ref[n, pl.ds(s * TOKENS, TOKENS), :]
    for j in range(2):
        down_w[part(span * 2 + j, UNITS), :] = own[part(core ^ j, UNITS), :]
    for j, k, ref in ((0, 0, d00), (0, 1, d01), (1, 0, d10), (1, 1, d11)):
        down_w[part(((1 - span) * 2 + j) * 2 + (row ^ k), LANES), :] = ref[...]
    for j, c in enumerate((c0, c1, c2, c3)):
        rows[pl.ds(j * TOKENS, TOKENS), :] = c[...]
    for i in range(4):
        tile = pl.ds(i * UNITS, UNITS)
        ahead[:, tile] = dot(rows[...], down_w[tile, :], 1, 1)


def gelu_parts(a):
    c = math.sqrt(2.0 / math.pi)
    t = jnp.tanh(c * (a + 0.044715 * a * a * a))
    half = 0.5 * (1.0 + t)
    return a * half, half + 0.5 * a * (1.0 - t * t) * c * (1.0 + 3 * 0.044715 * a * a)


def hidden_kernel(scal, n0, n1, n2, n3, up_w, ahead, o0, o1, o2, o3, h0, h1, p0, p1, rows, pre):
    for j, n in enumerate((n0, n1, n2, n3)):
        rows[pl.ds(j * TOKENS, TOKENS), :] = n[...]
    for i in range(4):
        s, j = divmod(i, 2)
        tile, lanes = pl.ds(i * UNITS, UNITS), pl.ds(s * UNITS, UNITS)
        act, slope = gelu_parts(dot(rows[...], up_w[:, tile], 1, 0))
        low = (ahead[:, tile] * slope).astype(bf16)
        (h0, h1)[j][:, lanes] = act.astype(bf16)
        (p0, p1)[j][:, lanes] = low
        pre[:, tile] = low
    for j, out in enumerate((o0, o1, o2, o3)):
        out[...] = dot(pre[pl.ds(j * TOKENS, TOKENS), :], up_w[...], 1, 1).astype(bf16)


def result_kernel(scal, h0, h1, down_w, o0, o1, o2, o3):
    for j, out in enumerate((o0, o1, o2, o3)):
        here = pl.ds(j * TOKENS, TOKENS)
        total = None
        for s in range(2):
            for k, h in enumerate((h0, h1)):
                term = dot(h[here, pl.ds(s * UNITS, UNITS)], down_w[pl.ds((2 * s + k) * UNITS, UNITS), :], 1, 0)
                total = term if total is None else total + term
        out[...] = total.astype(bf16)


def units_weights_kernel(scal, rows, cot, h0, h1, p0, p1, d_send, u_send, d_keep, u_keep):
    half = h0.shape[1]
    for h, p, down, up in ((h1, p1, d_send, u_send), (h0, p0, d_keep, u_keep)):
        for i in range(2):
            tile = pl.ds(i * UNITS, UNITS)
            down[tile, :] = dot(h[:, tile], cot[...], 0, 0).astype(bf16)
        for i in range(4):
            s, n = divmod(i, 2)
            there = (pl.ds(n * UNITS, UNITS), pl.ds(s * half, half))
            up[there] = dot(rows[:, pl.ds(i * UNITS, UNITS)], p[...], 0, 0).astype(bf16)


def units_one_kernel(scal, down, down_got, up, up_got, d_send, d_keep, u_send, u_keep):
    row = scal[ROW]
    half = up.shape[0]
    for s in range(2):
        for ref, side in ((d_keep, row), (d_send, 1 - row)):
            there = part(2 * s + side, LANES)
            ref[pl.ds(s * LANES, LANES), :] = (wide(down.at[there, :]) + wide(down_got.at[there, :])).astype(bf16)
        for n in range(2):
            for ref, side in ((u_keep, row), (u_send, 1 - row)):
                there = part(2 * (2 * n + s) + side, LANES)
                ref[:, pl.ds((2 * n + s) * LANES, LANES)] = (wide(up.at[:, there]) + wide(up_got.at[:, there])).astype(bf16)


def units_two_kernel(scal, down, down_got, up, up_got, d_send, d_keep, u_send, u_keep):
    for s, d_ref, u_ref in ((scal[SPAN], d_keep, u_keep), (1 - scal[SPAN], d_send, u_send)):
        there = part(s, LANES)
        d_ref[...] = (wide(down.at[there, :]) + wide(down_got.at[there, :])).astype(bf16)
        there = part(s, UNITS)
        u_ref[...] = (wide(up.at[:, there]) + wide(up_got.at[:, there])).astype(bf16)


def units_three_kernel(scal, up, up_got, x0, x1, x2, x3):
    for j, x in enumerate((x0, x1, x2, x3)):
        there = part(scal[PLACE] ^ j, LANES)
        x[...] = (wide(up.at[there, :]) + wide(up_got.at[there, :])).astype(bf16)


def units_four_kernel(scal, down, down_got, x0, x1, x2, x3, out):
    out[0:LANES, :] = (wide(down) + wide(down_got)).astype(bf16)
    for j, x in enumerate((x0, x1, x2, x3)):
        out[LANES : 2 * LANES, part(scal[PLACE] ^ j, UNITS)] = x[...]


def units_home_kernel(scal, b00, b01, b10, b11, up, down):
    row, core = scal[ROW], scal[CORE]
    for j, k, ref in ((0, 0, b00), (0, 1, b01), (1, 0, b10), (1, 1, b11)):
        quarter = (core ^ j) * 2 + (row ^ k)
        down[part(quarter, LANES), :] = ref[0:LANES, :].astype(f32)
        for rank in range(TP):
            for s in range(2):
                there = (s * TP + rank) * 4 + quarter
                up[:, part(there, LANES)] = ref[LANES : 2 * LANES, pl.ds(rank * UNITS + s * LANES, LANES)].astype(f32)


def heads_one_kernel(scal, own, got, send, keep):
    row = scal[ROW]
    for n in range(own.shape[0] // 64 // 2):
        for ref, side in ((keep, row), (send, 1 - row)):
            size = 64 if n < 3 * 2 * TP else 32
            pairs = 1 if size == 64 else 2
            for i in range(pairs):
                at = part((2 * n + side) if pairs == 1 else (4 * n + 2 * i + side), size)
                there = pl.ds(n * 64 + i * 32, size)
                ref[there, :] = (wide(own.at[at, :]) + wide(got.at[at, :])).astype(bf16)


def heads_two_kernel(scal, own, got, send, keep):
    quarter = TP * 64
    for m in range(3):
        for ref, s in ((keep, scal[SPAN]), (send, 1 - scal[SPAN])):
            at = part(2 * m + s, quarter)
            ref[pl.ds(m * quarter, quarter), :] = (wide(own.at[at, :]) + wide(got.at[at, :])).astype(bf16)
    for i in range(2 * TP):
        for ref, s in ((keep, 0), (send, 1)):
            at = pl.ds(6 * quarter + i * 64 + s * 32, 32)
            ref[pl.ds(3 * quarter + i * 32, 32), :] = (wide(own.at[at, :]) + wide(got.at[at, :])).astype(bf16)


def heads_three_kernel(scal, own, got, low, x0, x1, x2, x3):
    quarter = TP * 64
    at = pl.ds(3 * quarter, low.shape[0])
    low[...] = (wide(own.at[at, :]) + wide(got.at[at, :])).astype(bf16)
    for j, x in enumerate((x0, x1, x2, x3)):
        for m in range(3):
            at = part(m * TP + (scal[PLACE] ^ j), 64)
            x[:, pl.ds(m * LANES, LANES)] = (wide(own.at[at, :]) + wide(got.at[at, :])).astype(bf16)


def heads_four_kernel(scal, low, x0, x1, x2, x3, out):
    width = x0.shape[1]
    for j, x in enumerate((x0, x1, x2, x3)):
        out[:, part(scal[PLACE] ^ j, width)] = x[...]
    for i in range(2 * TP):
        there = (pl.ds(i // TP * 32, 32), pl.ds(TP * width + i % TP * LANES, LANES))
        out[there] = low[pl.ds(i * 32, 32), :]


def heads_home_kernel(scal, b00, b01, b10, b11, gq, gk, gv, go):
    row, core = scal[ROW], scal[CORE]
    width = 3 * LANES
    half = go.shape[1] // 2
    for j, k, ref in ((0, 0, b00), (0, 1, b01), (1, 0, b10), (1, 1, b11)):
        for rank in range(TP):
            for m, out in enumerate((gq, gk, gv)):
                lanes = pl.ds(rank * width + m * LANES, LANES)
                out[part(row ^ k, 64), part((core ^ j) * TP + rank, LANES)] = ref[:, lanes].astype(f32)
        there = part((core ^ j) * 2 + (row ^ k), 32)
        for i in range(2):
            go[there, pl.ds(i * half, half)] = ref[pl.ds(i * 32, 32), pl.ds(TP * width, half)].astype(f32)


def swap(x, axis):
    return lax.ppermute(x, axis, SWAP)


def across(x, d):
    return lax.ppermute(x, "tp", [(i, i ^ d) for i in range(TP)])


def gathered(x):
    return [x] + [across(x, d) for d in range(1, TP)]


def traded(parts):
    return [parts[0]] + [across(parts[d], d) for d in range(1, TP)]


def traded_all(x):
    return lax.all_to_all(x, ("span", "tp"), split_axis=0, concat_axis=0, tiled=True)


def hold_until(x, spent, *others):
    x, *others = lax.optimization_barrier((x,) + others)
    spent.extend(others)
    return x


def by_spans(
    activations,
    cotangent,
    block_sizes,
    context_back,
    first_gain,
    first_bias,
    w_query,
    w_key,
    w_value,
    w_out,
    second_gain,
    second_bias,
    w_up,
    w_down,
    decay_rate,
    input_map,
    output_map,
    step_size,
    skip_gain,
):
    span, place, row, core = (lax.axis_index(a).astype(jnp.int32) for a in ("span", "tp", "y", "core"))
    activations, cotangent, width = activations[0], cotangent[0], block_sizes[0]
    model = activations.shape[1]
    rows = TP * TOKENS
    subs = rows // BLK_A
    ctx_rows = subs * CTX
    mine = 2 * LANES
    half = model // 2
    scal = jnp.stack([span, place, row, core, (width > BLK_A).astype(jnp.int32)])
    tile = lambda n, m, kind=bf16: ((n, m), kind)
    block, piece = tile(TOKENS, model), tile(TOKENS, mine)

    shares, out_part, down_part = call(
        share_kernel,
        [((2 * TP, 448, LANES), bf16), tile(64, model), block],
        *(scal, w_query, w_key, w_value, w_out, w_down, w_up),
        scratch=[pltpu.SemaphoreType.DMA((4 * TP + 2,))],
        loose=(4, 5, 6),
        limit=56,
    )
    row_of = lambda v: v.reshape(1, LANES)
    (pack,) = call(
        pack_kernel,
        [tile(56, LANES, f32)],
        *(scal, decay_rate.T, input_map.T, output_map.T, row_of(step_size), row_of(skip_gain)),
        *(row_of(v) for v in (first_gain, first_bias, second_gain, second_bias)),
        scratch=[pltpu.VMEM((4, 1, LANES), bf16), pltpu.SemaphoreType.DMA((9,))],
        loose=range(1, 10),
        after=(out_part,),
        limit=60,
    )
    pack_far = swap(pack, "span")
    (vec,) = call(lines_kernel, [tile(16, LANES, f32)], scal, pack, pack_far)
    vecs = gathered(vec)
    spent = []

    def starts_of(which):
        begin = which * rows + jnp.arange(subs, dtype=jnp.int32) * BLK_A
        return begin // width * width

    own_spots = ((starts_of(span) - span * rows)[:, None] - context_back[None, :]).reshape(ctx_rows, 1)
    next_spots = ((starts_of(span + 1) - span * rows)[:, None] - context_back[None, :]).reshape(ctx_rows, 1)
    valid = (starts_of(span)[:, None] >= context_back[None, :]).astype(f32)

    shares = traded_all(hold_until(shares, spent, pack_far))

    low, vec = call(norm_one_kernel, [block, tile(8, model, f32)], scal, activations, *vecs)
    lowered = gathered(low)
    shares = [shares, swap(hold_until(shares, spent, low), "y")]
    down_far, out_far = swap(hold_until(down_part, spent, low), "span"), swap(hold_until(out_part, spent, low), "span")
    down_beside = swap(down_far, "y")
    hold, channels = pltpu.VMEM((STATES, CHUNKS, LANES), f32), pltpu.VMEM((2, rows, LANES), f32)
    channel_out, kept = ((2, rows, LANES), f32), ((2, 2, STATES, CHUNKS, LANES), f32)
    low_channels = pltpu.VMEM((rows, mine), bf16)
    local, to_next, ends, decay, mix, kept = call(
        scan_kernel,
        [channel_out, tile(ctx_rows, mine), tile(2 * STATES, mine, f32), tile(STATES, mine, f32), tile(STATES, mine, f32), kept],
        *(scal, *lowered, pack, pack_far, next_spots),
        scratch=[channels, low_channels, hold, hold, hold],
    )
    forward = [(0, 1)]
    begin, from_last = lax.ppermute(ends, "span", forward), lax.ppermute(to_next, "span", forward)
    cot_parts = gathered(hold_until(cotangent, spent, ends))
    (context,) = call(
        carry_kernel,
        [tile(ctx_rows, mine)],
        *(scal, local, decay, mix, begin, from_last, own_spots),
        after=(down_far,),
        scratch=[hold, channels, low_channels],
    )
    shares += [swap(hold_until(w, spent, ends), "core") for w in shares]
    before_qkv = context
    context = gathered(context)
    out_parts = [w_out, out_far, swap(hold_until(out_far, spent, ends), "core")]
    down_parts = [down_far, down_beside]
    qkv_w, qkv = call(qkv_kernel, [tile(model, 3 * mine), tile(rows, 3 * mine)], scal, *lowered, *shares, after=(before_qkv,))

    down_parts += [swap(hold_until(d, spent, qkv), "core") for d in down_parts]

    mixed, ctx_kv, out_w, *branch = call(
        attend_kernel,
        [tile(rows, mine), tile(ctx_rows, 2 * mine), tile(mine, model)] + [block] * TP,
        *(scal, valid, qkv, *context, qkv_w, *out_parts),
        after=tuple(cot_parts[1:]),
    )
    first_sum, low = call(norm_two_kernel, [tile(TOKENS, model, f32), block], scal, activations, *traded(branch), vec)

    square = tile(model, model)
    up_w, down_w, ahead, cot_span = call(
        units_kernel, [square, square, tile(rows, model, f32), tile(rows, model)], scal, *cot_parts, *shares, w_down, *down_parts
    )
    normal = gathered(low)
    side = tile(rows, half)
    *grad_norm, h0, h1, p0, p1, normal_span = call(
        hidden_kernel,
        [block] * TP + [side] * 4 + [tile(rows, model)],
        *(scal, *normal, up_w, ahead),
        scratch=[pltpu.VMEM((rows, model), bf16)],
    )
    grad_norm = traded(grad_norm)
    flat = tile(half, model)
    down_send, up_send, down_keep, up_keep = call(
        units_weights_kernel,
        [flat] * 4,
        *(scal, normal_span, cot_span, h0, h1, p0, p1),
    )
    quarter = tile(half // 2, model)
    d_send, d_keep, u_send, u_keep = call(
        units_one_kernel,
        [quarter, quarter, tile(half, half), tile(half, half)],
        *(scal, down_keep, swap(down_send, "core"), up_keep, swap(up_send, "core")),
    )
    grad_first, low, lines_two = call(
        norm_two_back_kernel,
        [tile(TOKENS, model, f32), block, tile(8, model, f32)],
        *(scal, first_sum, *grad_norm, cotangent, vec),
    )
    branch_back = gathered(low)
    result_parts = call(result_kernel, [block] * TP, scal, h0, h1, down_w, after=(low,))
    d_send, d_keep, u_send, u_keep = call(
        units_two_kernel,
        [block, block, tile(half, mine), tile(half, mine)],
        *(scal, d_keep, swap(d_send, "y"), u_keep, swap(u_send, "y")),
    )

    grad_qkv, grad_ctx, *back = call(
        attend_back_kernel,
        [tile(rows, 3 * mine), tile(ctx_rows, 2 * mine)] + [tile(ctx_rows, mine)] * TP,
        *(scal, valid, qkv, ctx_kv, *branch_back, out_w, qkv_w),
        after=(result_parts[0],),
        scratch=[pltpu.VMEM((rows, mine), bf16), pltpu.VMEM((rows, 2 * mine), f32)],
    )
    back = traded(back)
    grad_context, turned = call(context_sum_kernel, [tile(ctx_rows, mine)] * 2, scal, *back, after=(u_send,))
    from_next = lax.ppermute(turned, "span", [(1, 0)])
    d_send = hold_until(d_send, spent, from_next)
    heads = tile(4 * model, LANES)
    heads_send, heads_keep = call(
        attend_weights_kernel,
        [heads] * 2,
        *(scal, *lowered, *context, grad_qkv, grad_ctx, mixed, *branch_back),
        scratch=[pltpu.VMEM((rows, model), bf16), pltpu.VMEM((model, 3 * mine), f32), pltpu.VMEM((mine, model), f32)],
        after=(turned,),
    )
    heads = tile(2 * model, LANES)
    heads_send, heads_keep = call(
        heads_one_kernel, [heads] * 2, scal, heads_keep, swap(heads_send, "core")
    )
    grad_lowered = traded(call(lowered_back_kernel, [block] * TP, scal, grad_qkv, qkv_w, after=(turned,)))

    u_parts = call(units_three_kernel, [piece] * TP, scal, u_keep, swap(hold_until(u_send, spent, grad_ctx), "span"))

    grad_states, grad_local, grad_ends = call(
        scan_back_kernel,
        [channel_out, channel_out, tile(STATES, mine, f32)],
        *(scal, grad_context, from_next, own_spots, next_spots, pack, pack_far, decay, mix),
        scratch=[hold, hold],
        after=(heads_send,),
    )
    grad_begin = lax.ppermute(grad_ends, "span", [(1, 0)])
    heads = tile(model, LANES)
    heads_send, heads_keep = call(heads_two_kernel, [heads] * 2, scal, heads_keep, swap(hold_until(heads_send, spent, from_next), "y"), after=(grad_begin,))
    (sums,) = call(
        sums_kernel,
        [tile(40, mine, f32)],
        *(scal, *lowered, grad_states, decay, begin, kept),
        scratch=[channels, hold, hold],
        after=(grad_ends,),
    )
    grad_conv = call(
        carry_back_kernel,
        [piece] * TP,
        *(scal, grad_local, decay, mix, grad_begin),
        scratch=[hold, channels],
        after=(sums, *grad_lowered[1:],),
    )
    grad_conv = traded(grad_conv)
    grad_inputs, lines = call(
        last_kernel,
        [tile(TOKENS, model, f32), ((2 * TP, 8, LANES), f32)],
        *(scal, activations, vec, grad_first, *grad_lowered, *grad_conv, lines_two),
        scratch=[pltpu.VMEM((TOKENS, model), f32)],
        after=(heads_send,),
    )
    (u_all,) = call(units_four_kernel, [tile(2 * LANES, model)], scal, d_keep, swap(d_send, "span"), *traded([hold_until(u, spent, grad_begin) for u in u_parts]))
    out_low, *q_parts = call(
        heads_three_kernel,
        [tile(2 * LANES, LANES)] + [tile(64, 3 * LANES)] * TP,
        *(scal, heads_keep, swap(heads_send, "span")),
    )
    u_beside = swap(u_all, "y")
    result_parts = [hold_until(r, spent, lines) for r in result_parts]
    result_parts = traded(result_parts)
    result = first_sum + sum(x.astype(f32) for x in result_parts)
    (q_all,) = call(heads_four_kernel, [tile(64, 2 * model)], scal, out_low, *traded(q_parts))
    q_beside = swap(q_all, "y")
    grad_up, grad_down = call(
        units_home_kernel,
        [tile(LANES, 4 * model, f32), tile(half, model, f32)],
        *(scal, u_all, u_beside, swap(u_all, "core"), swap(u_beside, "core")),
        after=(q_all,),
    )
    home = tile(LANES, model, f32)
    grad_query, grad_key, grad_value, grad_out = call(
        heads_home_kernel, [home] * 4, scal, q_all, q_beside, swap(q_all, "core"), swap(q_beside, "core"), after=tuple(spent)
    )

    lines = traded_all(lines)
    sums = sums[:, :LANES] + swap(sums[:, LANES:], "span")
    (small,) = call(lines_sum_kernel, [tile(48, LANES, f32)], scal, lines, sums, after=(out_low,))
    small = small + swap(small, "y")
    small = small + swap(small, "core")
    lines, sums = small[:8], small[8:]
    grad_mix, grad_skip = sums[:STATES].T, sums[2 * STATES]
    step = step_size[:, None]
    grad_speed = -(output_map * input_map * step) * sums[STATES : 2 * STATES].T
    grad_step = jnp.sum(grad_mix * output_map * input_map + grad_speed * decay_rate, axis=1)
    return (
        result[None],
        grad_inputs[None],
        lines[0],
        lines[1],
        grad_query,
        grad_key,
        grad_value,
        grad_out,
        lines[2],
        lines[3],
        grad_up,
        grad_down,
        grad_speed * step,
        grad_mix * output_map * step,
        grad_mix * input_map * step,
        grad_step,
        grad_skip,
    )


def from_behind(x, axis, by):
    peers = lax.axis_size(axis)
    pairs = [(i, i + by) for i in range(peers) if 0 <= i + by < peers]
    return lax.ppermute(x, axis, pairs)


def smooth_gate(values):
    return jax.nn.gelu(values, approximate=True)


def ssm_kernel(decay_rate, input_map, output_map, step_size, length):
    offsets = jnp.arange(length).astype(jnp.float32)
    weight = output_map * input_map * step_size[:, None]
    decay_speed = step_size[:, None] * decay_rate
    total_sum = jnp.zeros((decay_rate.shape[0], length), jnp.float32)
    for state_index in range(decay_rate.shape[1]):
        total_sum = total_sum + weight[:, state_index : state_index + 1] * jnp.exp(
            -decay_speed[:, state_index : state_index + 1] * offsets[None, :]
        )
    return total_sum


def phase_table(row_count, col_count, period):
    first_ids = jnp.arange(row_count, dtype=jnp.int32)[:, None]
    second_ids = jnp.arange(col_count, dtype=jnp.int32)[None, :]
    angles = (first_ids * second_ids % period).astype(jnp.float32) * (2.0 * math.pi / period)
    return (jnp.cos(angles), jnp.sin(angles))


def exact_einsum(form, left_side, right_side):
    return jnp.einsum(form, left_side, right_side, precision=lax.Precision.HIGHEST)


def spectrum(signal, low_len, high_len):
    row_count = signal.shape[0]
    total_len = low_len * high_len
    grid_rows = signal.reshape(row_count, high_len, low_len)
    cos_high, sin_high = phase_table(high_len, high_len, high_len)
    real_part = exact_einsum("rmn,mk->rkn", grid_rows, cos_high)
    imag_part = -exact_einsum("rmn,mk->rkn", grid_rows, sin_high)
    cos_twist, sin_twist = phase_table(high_len, low_len, total_len)
    real_part, imag_part = (
        real_part * cos_twist + imag_part * sin_twist,
        imag_part * cos_twist - real_part * sin_twist,
    )
    cos_low, sin_low = phase_table(low_len, low_len, low_len)
    out_real = exact_einsum("rkn,nj->rkj", real_part, cos_low) + exact_einsum(
        "rkn,nj->rkj", imag_part, sin_low
    )
    out_imag = exact_einsum("rkn,nj->rkj", imag_part, cos_low) - exact_einsum(
        "rkn,nj->rkj", real_part, sin_low
    )
    return (out_real, out_imag)


def signal_of(real_part, imag_part, low_len, high_len, keep_len):
    row_count = real_part.shape[0]
    total_len = low_len * high_len
    cos_low, sin_low = phase_table(low_len, low_len, low_len)
    mid_real = exact_einsum("rkj,nj->rkn", real_part, cos_low) - exact_einsum(
        "rkj,nj->rkn", imag_part, sin_low
    )
    mid_imag = exact_einsum("rkj,nj->rkn", real_part, sin_low) + exact_einsum(
        "rkj,nj->rkn", imag_part, cos_low
    )
    cos_twist, sin_twist = phase_table(high_len, low_len, total_len)
    turn_real = mid_real * cos_twist - mid_imag * sin_twist
    turn_imag = mid_real * sin_twist + mid_imag * cos_twist
    cos_high, sin_high = phase_table(high_len, high_len, high_len)
    grid_rows = exact_einsum("rkn,km->rmn", turn_real, cos_high) - exact_einsum(
        "rkn,km->rmn", turn_imag, sin_high
    )
    return grid_rows.reshape(row_count, total_len)[:, :keep_len] / total_len


def padded(values):
    return jnp.concatenate([values, jnp.zeros_like(values)], axis=-1)


def norm_parts(values):
    center = values - jnp.mean(values, axis=-1, keepdims=True)
    inverse_dev = lax.rsqrt(jnp.mean(center * center, axis=-1, keepdims=True) + 1e-05)
    return (center * inverse_dev, inverse_dev)


def plain_norm_back(grad_values, scaled, inverse_dev, gain_vector):
    weighted = grad_values * gain_vector.astype(jnp.float32)
    return inverse_dev * (
        weighted
        - jnp.mean(weighted, axis=-1, keepdims=True)
        - scaled * jnp.mean(weighted * scaled, axis=-1, keepdims=True)
    )


def matmul(left_side, right_side):
    return jnp.einsum("...i,ij->...j", left_side, right_side, preferred_element_type=jnp.float32)


def matmul_t(left_side, right_side):
    return jnp.einsum("...j,ij->...i", left_side, right_side, preferred_element_type=jnp.float32)


def outer_sum(left_side, right_side):
    return jnp.einsum(
        "ri,rj->ij",
        left_side.reshape(-1, left_side.shape[-1]),
        right_side.reshape(-1, right_side.shape[-1]),
        preferred_element_type=jnp.float32,
    )


def take_rows(rows_table, row_ids):
    return jnp.take(rows_table, row_ids, axis=0)


def plain(
    activations,
    cotangent,
    block_sizes,
    context_back,
    first_gain,
    first_bias,
    w_query,
    w_key,
    w_value,
    w_out,
    second_gain,
    second_bias,
    w_up,
    w_down,
    decay_rate,
    input_map,
    output_map,
    step_size,
    skip_gain,
):
    seq_ways = lax.axis_size("seq")
    place = lax.axis_index("seq")
    seq_count, tokens, model_width = activations.shape
    channels = decay_rate.shape[0]
    length = tokens * seq_ways
    sub_len = min(BLK_A, tokens)
    sub_count = tokens // sub_len
    shift_count = max(BLK_B // tokens - 1, 0)
    head_dim = model_width // HEADS
    score_scale = head_dim ** (-0.5)
    per_dev = sub_count * CTX
    low_len = 2 * seq_ways
    (
        gain_one,
        bias_one,
        query_full,
        key_full,
        value_full,
        out_full,
        gain_two,
        bias_two,
        up_full,
        down_full,
    ) = (
        lax.all_gather(first_gain, "seq", axis=0, tiled=True),
        lax.all_gather(first_bias, "seq", axis=0, tiled=True),
        lax.all_gather(w_query, "seq", axis=0, tiled=True),
        lax.all_gather(w_key, "seq", axis=0, tiled=True),
        lax.all_gather(w_value, "seq", axis=0, tiled=True),
        lax.all_gather(w_out, "seq", axis=0, tiled=True),
        lax.all_gather(second_gain, "seq", axis=0, tiled=True),
        lax.all_gather(second_bias, "seq", axis=0, tiled=True),
        lax.all_gather(w_up, "seq", axis=0, tiled=True),
        lax.all_gather(w_down, "seq", axis=0, tiled=True),
    )
    scaled_one, inverse_one = norm_parts(activations)
    lowered = (scaled_one * gain_one.astype(jnp.float32) + bias_one.astype(jnp.float32)).astype(
        jnp.bfloat16
    )
    by_channel = lax.all_to_all(
        jnp.swapaxes(lowered, 1, 2), "seq", split_axis=1, concat_axis=2, tiled=True
    )
    channel_in = by_channel.astype(jnp.float32)
    kernel, kernel_pull = jax.vjp(
        lambda a, b, c, e: ssm_kernel(a, b, c, e, length),
        decay_rate,
        input_map,
        output_map,
        step_size,
    )
    input_real, input_imag = spectrum(padded(channel_in.reshape(-1, length)), low_len, tokens)
    input_real = input_real.reshape(seq_count, channels, tokens, low_len)
    input_imag = input_imag.reshape(seq_count, channels, tokens, low_len)
    kernel_real, kernel_imag = spectrum(padded(kernel), low_len, tokens)
    conv_real = input_real * kernel_real - input_imag * kernel_imag
    conv_imag = input_real * kernel_imag + input_imag * kernel_real
    convolved = signal_of(
        conv_real.reshape(-1, tokens, low_len),
        conv_imag.reshape(-1, tokens, low_len),
        low_len,
        tokens,
        length,
    )
    states = convolved.reshape(seq_count, channels, length) + skip_gain[None, :, None] * channel_in
    targets = (
        jnp.arange(seq_ways, dtype=jnp.int32)[:, None] * tokens
        + jnp.arange(sub_count, dtype=jnp.int32)[None, :] * sub_len
    )
    sizes_three = block_sizes[:, None, None]
    block_start = targets[None] // sizes_three * sizes_three
    positions = block_start[..., None] - context_back
    valid_all = positions >= 0
    picks = jnp.maximum(positions, 0).reshape(seq_count, -1)
    position_major = jnp.swapaxes(states, 1, 2)
    picked = jax.vmap(take_rows)(position_major, picks)
    picked = jnp.where(valid_all.reshape(seq_count, -1, 1), picked, 0.0).astype(jnp.bfloat16)
    picked = jnp.swapaxes(picked, 1, 2)
    arrived = lax.all_to_all(
        picked.reshape(seq_count, channels, seq_ways, per_dev),
        "seq",
        split_axis=2,
        concat_axis=1,
        tiled=True,
    )
    context = jnp.swapaxes(arrived.reshape(seq_count, model_width, per_dev), 1, 2)
    own_valid = lax.dynamic_index_in_dim(valid_all, place, axis=1, keepdims=False).reshape(
        seq_count, per_dev
    )
    queries = matmul(lowered, query_full).astype(jnp.bfloat16)
    keys_own = matmul(lowered, key_full).astype(jnp.bfloat16)
    values_own = matmul(lowered, value_full).astype(jnp.bfloat16)
    ctx_keys = matmul(context, key_full).astype(jnp.bfloat16)
    ctx_values = matmul(context, value_full).astype(jnp.bfloat16)
    key_parts = [ctx_keys]
    value_parts = [ctx_values]
    key_places = []
    token_ids = jnp.arange(tokens, dtype=jnp.int32)
    for distance in range(shift_count, 0, -1):
        far_keys, far_values = from_behind((keys_own, values_own), "seq", distance)
        key_parts.append(far_keys)
        value_parts.append(far_values)
        key_places.append((place - distance) * tokens + token_ids)
    key_parts.append(keys_own)
    value_parts.append(values_own)
    key_places.append(place * tokens + token_ids)
    all_keys = jnp.concatenate(key_parts, axis=1)
    all_values = jnp.concatenate(value_parts, axis=1)
    key_pos = jnp.concatenate(key_places)
    query_pos = place * tokens + token_ids
    same_block = key_pos[None, None, :] // sizes_three == query_pos[None, :, None] // sizes_three
    causal = key_pos[None, None, :] <= query_pos[None, :, None]
    ctx_allowed = (
        (token_ids // sub_len)[:, None] == (jnp.arange(per_dev, dtype=jnp.int32) // CTX)[None, :]
    )[None] & own_valid[:, None, :]
    allowed = jnp.concatenate([ctx_allowed, same_block & causal], axis=2)

    def split_heads(values):
        return values.reshape(values.shape[0], values.shape[1], HEADS, head_dim)

    def scores_of():
        raw_scores = (
            jnp.einsum(
                "sqhd,skhd->shqk",
                split_heads(queries),
                split_heads(all_keys),
                preferred_element_type=jnp.float32,
            )
            * score_scale
        )
        return jnp.where(allowed[:, None], raw_scores, -1e30)

    scores = scores_of()
    row_top = jnp.max(scores, axis=-1, keepdims=True)
    log_total = row_top + jnp.log(jnp.sum(jnp.exp(scores - row_top), axis=-1, keepdims=True))
    probs_low = jnp.exp(scores - log_total).astype(jnp.bfloat16)
    attended = jnp.einsum(
        "shqk,skhd->sqhd", probs_low, split_heads(all_values), preferred_element_type=jnp.float32
    )
    mixed_out = attended.reshape(seq_count, tokens, model_width).astype(jnp.bfloat16)
    first_sum = activations + matmul(mixed_out, out_full)
    scaled_two, inverse_two = norm_parts(first_sum)
    normal_two = (scaled_two * gain_two.astype(jnp.float32) + bias_two.astype(jnp.float32)).astype(
        jnp.bfloat16
    )
    pre_gate = matmul(normal_two, up_full)
    hidden, gate_pull = jax.vjp(smooth_gate, pre_gate)
    hidden_low = hidden.astype(jnp.bfloat16)
    result = first_sum + matmul(hidden_low, down_full)
    grad_down = outer_sum(hidden_low, cotangent)
    grad_hidden = matmul_t(cotangent, down_full)
    grad_pre = gate_pull(grad_hidden)[0].astype(jnp.bfloat16)
    grad_up = outer_sum(normal_two, grad_pre)
    grad_norm_two = matmul_t(grad_pre, up_full)
    grad_gain_two = jnp.sum(grad_norm_two * scaled_two, axis=(0, 1))
    grad_bias_two = jnp.sum(grad_norm_two, axis=(0, 1))
    grad_first = cotangent.astype(jnp.float32) + plain_norm_back(
        grad_norm_two, scaled_two, inverse_two, gain_two
    )
    grad_branch = grad_first.astype(jnp.bfloat16)
    grad_out = outer_sum(mixed_out, grad_branch)
    grad_mixed = split_heads(matmul_t(grad_branch, out_full).astype(jnp.bfloat16))
    scores = scores_of()
    probabilities = jnp.exp(scores - log_total)
    probs_low = probabilities.astype(jnp.bfloat16)
    grad_probs = jnp.einsum(
        "sqhd,skhd->shqk", grad_mixed, split_heads(all_values), preferred_element_type=jnp.float32
    )
    grad_all_values = jnp.einsum(
        "shqk,sqhd->skhd", probs_low, grad_mixed, preferred_element_type=jnp.float32
    )
    grad_scores = (
        probabilities * (grad_probs - jnp.sum(probabilities * grad_probs, axis=-1, keepdims=True))
    ).astype(jnp.bfloat16)
    grad_queries = (
        jnp.einsum(
            "shqk,skhd->sqhd",
            grad_scores,
            split_heads(all_keys),
            preferred_element_type=jnp.float32,
        )
        * score_scale
    )
    grad_queries = grad_queries.reshape(seq_count, tokens, model_width).astype(jnp.bfloat16)
    grad_all_keys = (
        jnp.einsum(
            "shqk,sqhd->skhd", grad_scores, split_heads(queries), preferred_element_type=jnp.float32
        )
        * score_scale
    )
    grad_all_keys = grad_all_keys.reshape(seq_count, -1, model_width)
    grad_all_values = grad_all_values.reshape(seq_count, -1, model_width)
    grad_ctx_keys = grad_all_keys[:, :per_dev]
    grad_ctx_values = grad_all_values[:, :per_dev]
    grad_keys = grad_all_keys[:, -tokens:]
    grad_values = grad_all_values[:, -tokens:]
    for distance in range(shift_count, 0, -1):
        begin = per_dev + (shift_count - distance) * tokens
        back_keys, back_values = (
            from_behind(
                grad_all_keys[:, begin : begin + tokens].astype(jnp.bfloat16), "seq", -distance
            ).astype(jnp.float32),
            from_behind(
                grad_all_values[:, begin : begin + tokens].astype(jnp.bfloat16), "seq", -distance
            ).astype(jnp.float32),
        )
        grad_keys = grad_keys + back_keys
        grad_values = grad_values + back_values
    grad_keys_low = grad_keys.astype(jnp.bfloat16)
    grad_values_low = grad_values.astype(jnp.bfloat16)
    context_wide = context.astype(jnp.float32)
    grad_query_w = outer_sum(lowered, grad_queries)
    grad_key_w = outer_sum(lowered, grad_keys_low) + outer_sum(context_wide, grad_ctx_keys)
    grad_value_w = outer_sum(lowered, grad_values_low) + outer_sum(context_wide, grad_ctx_values)
    grad_normal_one = (
        matmul_t(grad_queries, query_full)
        + matmul_t(grad_keys_low, key_full)
        + matmul_t(grad_values_low, value_full)
    )
    grad_context = matmul_t(grad_ctx_keys, key_full) + matmul_t(grad_ctx_values, value_full)
    sent_back = jnp.swapaxes(grad_context, 1, 2).reshape(seq_count, model_width, 1, per_dev)
    returned = lax.all_to_all(
        sent_back.astype(jnp.bfloat16), "seq", split_axis=1, concat_axis=2, tiled=True
    ).astype(sent_back.dtype)
    returned = jnp.where(
        valid_all.reshape(seq_count, 1, -1), returned.reshape(seq_count, channels, -1), 0.0
    )
    segment_ids = (jnp.arange(seq_count, dtype=jnp.int32)[:, None] * length + picks).reshape(-1)
    flat_rows = jnp.swapaxes(returned, 1, 2).reshape(-1, channels)
    grad_states = jax.ops.segment_sum(flat_rows, segment_ids, num_segments=seq_count * length)
    grad_states = jnp.swapaxes(grad_states.reshape(seq_count, length, channels), 1, 2)
    grad_real, grad_imag = spectrum(padded(grad_states.reshape(-1, length)), low_len, tokens)
    grad_real = grad_real.reshape(seq_count, channels, tokens, low_len)
    grad_imag = grad_imag.reshape(seq_count, channels, tokens, low_len)
    back_real = grad_real * kernel_real + grad_imag * kernel_imag
    back_imag = grad_imag * kernel_real - grad_real * kernel_imag
    grad_conv = signal_of(
        back_real.reshape(-1, tokens, low_len),
        back_imag.reshape(-1, tokens, low_len),
        low_len,
        tokens,
        length,
    )
    grad_conv = grad_conv.reshape(seq_count, channels, length)
    corr_real = jnp.sum(grad_real * input_real + grad_imag * input_imag, axis=0)
    corr_imag = jnp.sum(grad_imag * input_real - grad_real * input_imag, axis=0)
    grad_kernel = signal_of(corr_real, corr_imag, low_len, tokens, length)
    grad_rate, grad_in_map, grad_out_map, grad_step = kernel_pull(grad_kernel)
    grad_skip = jnp.sum(grad_states * channel_in, axis=(0, 2))
    grad_channel = grad_conv + skip_gain[None, :, None] * grad_states
    back_tokens = lax.all_to_all(
        grad_channel.astype(jnp.bfloat16), "seq", split_axis=2, concat_axis=1, tiled=True
    ).astype(grad_channel.dtype)
    grad_normal_one = grad_normal_one + jnp.swapaxes(back_tokens, 1, 2)
    grad_gain_one = jnp.sum(grad_normal_one * scaled_one, axis=(0, 1))
    grad_bias_one = jnp.sum(grad_normal_one, axis=(0, 1))
    grad_inputs = grad_first + plain_norm_back(grad_normal_one, scaled_one, inverse_one, gain_one)
    shares = (
        lax.psum_scatter(
            grad_gain_one.astype(jnp.bfloat16), "seq", scatter_dimension=0, tiled=True
        ).astype(jnp.float32),
        lax.psum_scatter(
            grad_bias_one.astype(jnp.bfloat16), "seq", scatter_dimension=0, tiled=True
        ).astype(jnp.float32),
        lax.psum_scatter(
            grad_query_w.astype(jnp.bfloat16), "seq", scatter_dimension=0, tiled=True
        ).astype(jnp.float32),
        lax.psum_scatter(
            grad_key_w.astype(jnp.bfloat16), "seq", scatter_dimension=0, tiled=True
        ).astype(jnp.float32),
        lax.psum_scatter(
            grad_value_w.astype(jnp.bfloat16), "seq", scatter_dimension=0, tiled=True
        ).astype(jnp.float32),
        lax.psum_scatter(
            grad_out.astype(jnp.bfloat16), "seq", scatter_dimension=0, tiled=True
        ).astype(jnp.float32),
        lax.psum_scatter(
            grad_gain_two.astype(jnp.bfloat16), "seq", scatter_dimension=0, tiled=True
        ).astype(jnp.float32),
        lax.psum_scatter(
            grad_bias_two.astype(jnp.bfloat16), "seq", scatter_dimension=0, tiled=True
        ).astype(jnp.float32),
        lax.psum_scatter(
            grad_up.astype(jnp.bfloat16), "seq", scatter_dimension=0, tiled=True
        ).astype(jnp.float32),
        lax.psum_scatter(
            grad_down.astype(jnp.bfloat16), "seq", scatter_dimension=0, tiled=True
        ).astype(jnp.float32),
    )
    summed = (
        lax.psum(shares[0].astype(jnp.bfloat16), "dp").astype(jnp.float32),
        lax.psum(shares[1].astype(jnp.bfloat16), "dp").astype(jnp.float32),
        lax.psum(shares[2].astype(jnp.bfloat16), "dp").astype(jnp.float32),
        lax.psum(shares[3].astype(jnp.bfloat16), "dp").astype(jnp.float32),
        lax.psum(shares[4].astype(jnp.bfloat16), "dp").astype(jnp.float32),
        lax.psum(shares[5].astype(jnp.bfloat16), "dp").astype(jnp.float32),
        lax.psum(shares[6].astype(jnp.bfloat16), "dp").astype(jnp.float32),
        lax.psum(shares[7].astype(jnp.bfloat16), "dp").astype(jnp.float32),
        lax.psum(shares[8].astype(jnp.bfloat16), "dp").astype(jnp.float32),
        lax.psum(shares[9].astype(jnp.bfloat16), "dp").astype(jnp.float32),
        lax.psum(grad_rate.astype(jnp.bfloat16), "dp").astype(jnp.float32),
        lax.psum(grad_in_map.astype(jnp.bfloat16), "dp").astype(jnp.float32),
        lax.psum(grad_out_map.astype(jnp.bfloat16), "dp").astype(jnp.float32),
        lax.psum(grad_step.astype(jnp.bfloat16), "dp").astype(jnp.float32),
        lax.psum(grad_skip.astype(jnp.bfloat16), "dp").astype(jnp.float32),
    )
    summed = tuple(summed)
    return (
        result,
        grad_inputs,
        summed[0],
        summed[1],
        summed[2],
        summed[3],
        summed[4],
        summed[5],
        summed[6],
        summed[7],
        summed[8],
        summed[9],
        summed[10],
        summed[11],
        summed[12],
        summed[13],
        summed[14],
    )


def solution(mesh):
    dp_ways, seq_ways = mesh.shape["dp"], mesh.shape["seq"]
    lone, data, flat, cut = P(), P("dp", "seq", None), P("seq"), P("seq", None)
    in_specs = (data, data, P("dp"), lone, flat, flat, cut, cut, cut, cut, flat, flat, cut, cut, cut, cut, cut, flat, flat)
    out_specs = (data, data, flat, flat, cut, cut, cut, cut, flat, flat, cut, cut, cut, cut, cut, flat, flat)

    def run(activations, *others):
        seqs, length, model = activations.shape
        tokens = length // seq_ways
        if (seqs, dp_ways, seq_ways, tokens, model) != (4, 4, 2 * TP, TOKENS, HEADS * LANES):
            return jax.shard_map(plain, mesh=mesh, in_specs=in_specs, out_specs=out_specs, check_vma=False)(activations, *others)
        fine = Mesh(mesh.devices.reshape(2, 2, 2, TP), ("y", "core", "span", "tp"))
        names = {"dp": ("y", "core"), "seq": ("span", "tp")}
        split = lambda specs: tuple(P(*(names.get(a) for a in spec)) for spec in specs)
        whole = jax.shard_map(by_spans, mesh=fine, in_specs=split(in_specs), out_specs=split(out_specs), check_vma=False)
        return whole(activations, *others)

    return run
```
